32 devices in a mesh: scene: 2 (over x), tile: 8 (over z, y), frame: 2 (over core).
Axes of the slice: x: 2, y: 2, z: 4, core: 2. Of those that a mesh axis runs over, the one named last changes fastest.
Arguments:
- observed: float32 [64, 256, 2048], P('frame', ('scene', 'tile')), parts along dimension 1, may hold values from -6 to 6
- frame_shift: int32 [4, 64], P('scene', 'frame'), parts along dimension 0, may hold values from 0 to 3
- kernel_ids: int32 [2, 64], P('scene', 'frame'), parts along dimension 0, may hold values from 0 to 7
- groups: int32 [2, 64], P('scene', 'frame'), parts along dimension 0, may hold values from 0 to 3
- kernels: float32 [8, 5, 5], replicated, may hold values from 0 to 0.08
- gains: float32 [4], replicated, may hold values from 0.5 to 2
Outputs:
- solution: float32 [1024, 8192], P(('scene', 'tile'), 'frame'), parts along dimension 0
- residual: float32 [1024, 8192], P(('scene', 'tile'), 'frame'), parts along dimension 0
The draws below stay inside these ranges and needn't reach their ends.
There are 2 independent parts, one for each index of `scene`. The reference program is written for one: setup_inputs(seed, part) draws one part's arguments, and reference() takes and returns one part's arrays. A program takes and returns all parts, laid end to end along the dimension named above; an argument that names none is the same for every part. Nothing has to cross between parts.
All inputs are finite; a program needn't handle non-finite values.
Results may differ from the reference program's by a relative error of at most 0.00026.
Values sent between devices are 32-bit elements; how exact they have to be, the bound alone decides.
No kernel may reach another device: no remote copies, remote signals or barrier semaphores. Data moves between devices by JAX's collectives and lax.ppermute only.
A program may use at most 128 MiB of HBM per device.

```python
import math
import jax
import jax.numpy as jnp
from jax import lax

W = 8192
KERNELS = 8
GROUPS = 4
ITERS = 2
FRAMES = 64
ROWS = 512


def set_ends(entries, rng, low, top_value):
    place = [jax.random.randint(jax.random.fold_in(rng, axis), (), 0, length) for axis, length in enumerate(entries.shape)]
    main_axis = entries.shape.index(max(entries.shape))
    beside = place[:main_axis] + [(place[main_axis] + 1) % entries.shape[main_axis]] + place[main_axis + 1:]
    return entries.at[tuple(place)].set(low).at[tuple(beside)].set(top_value)


def steps_of(rng, shape, cuts, least, largest):
    factor_of, own = 1.0, jax.random.fold_in(rng, 6)
    for axis_at, blocks in cuts:
        heights = jnp.exp(jax.random.uniform(jax.random.fold_in(own, axis_at), (blocks,), jnp.float32, least / len(cuts), largest / len(cuts)))
        factor_of = factor_of * jnp.repeat(heights, shape[axis_at] // blocks).reshape([-1 if axis == axis_at else 1 for axis in range(len(shape))])
    return factor_of


def centred(stream_key, extent, scale, reach, cuts=(), held_as=jnp.bfloat16):
    values = scale * jax.random.normal(stream_key, extent, jnp.float32)
    if cuts:
        values = values * steps_of(stream_key, extent, cuts, -0.22, 0.18)
    return jnp.clip(values, -reach, reach).astype(held_as)


def setup_inputs(seed: int = 0, part: int = 0) -> dict:
    streams_of = jax.random.split(jax.random.key(seed), 7)
    own_keys = jax.random.split(jax.random.fold_in(streams_of[6], part), 7)
    observed = centred(own_keys[0], (FRAMES, ROWS // 4, W // 4), 1.0, 6.0, ((0, 2), (1, 8)), jnp.float32)
    frame_shift = set_ends(jax.random.randint(own_keys[1], (2, FRAMES), 0, 4), jax.random.fold_in(own_keys[1], 1), 0, 3).astype(jnp.int32)
    kernel_ids = set_ends(jax.random.randint(own_keys[2], (1, FRAMES), 0, KERNELS), jax.random.fold_in(own_keys[2], 1), 0, KERNELS - 1).astype(jnp.int32)
    groups = set_ends(jax.random.randint(own_keys[3], (1, FRAMES), 0, GROUPS), jax.random.fold_in(own_keys[3], 1), 0, GROUPS - 1).astype(jnp.int32)
    kernels = jnp.clip(jax.random.uniform(streams_of[4], (KERNELS, 5, 5), jnp.float32, 0.0, 0.08), 0.0, 0.08)
    gains = jnp.clip(jnp.exp(jax.random.uniform(streams_of[5], (GROUPS,), jnp.float32, math.log(0.5), math.log(2.0))), 0.5, 2.0)
    return dict(observed=observed, frame_shift=frame_shift, kernel_ids=kernel_ids, groups=groups, kernels=kernels, gains=gains)


damping = 0.3
offsets = [(t, (t - 2) % 4, (t - 2) // 4) for t in range(8)]


def effective(frame_shift, kernel_ids, groups, kernels, gains):
    taps = jnp.arange(8, dtype=jnp.int32)
    span = jnp.arange(5, dtype=jnp.int32)
    rows = ((taps[None, :, None] - frame_shift[0][:, None, None]) == span[None, None, :]).astype(jnp.float32)
    cols = ((taps[None, :, None] - frame_shift[1][:, None, None]) == span[None, None, :]).astype(jnp.float32)
    count = kernels.shape[0]
    pick = (kernel_ids[0][:, None] == jnp.arange(count, dtype=jnp.int32)[None, :]).astype(jnp.float32)
    chosen = jnp.dot(pick, kernels.reshape(count, 25), precision=lax.Precision.HIGHEST).reshape(-1, 5, 5)
    member = (groups[0][:, None] == jnp.arange(gains.shape[0], dtype=jnp.int32)[None, :]).astype(jnp.float32)
    scale = jnp.dot(member, gains, precision=lax.Precision.HIGHEST)
    table = jnp.einsum("kra,kab,kcb->krc", rows, chosen, cols, precision=lax.Precision.HIGHEST)
    return (scale[:, None, None] * table).reshape(-1, 64)


def phases(field):
    height, width = field.shape
    return field.reshape(height // 4, 4, width // 4, 4).transpose(1, 3, 0, 2)


def unphase(field):
    return field.transpose(2, 0, 3, 1).reshape(4 * field.shape[2], 4 * field.shape[3])


def forward(extended, weights, count):
    quarter = extended.shape[3]
    padded = jnp.pad(extended, ((0, 0), (0, 0), (0, 0), (1, 1)))
    stack = jnp.stack([padded[pr, pc, 1 + qr:1 + qr + count, 1 + qc:1 + qc + quarter]
                       for (tr, pr, qr) in offsets for (tc, pc, qc) in offsets])
    return jnp.einsum("kt,tij->kij", weights, stack, precision=lax.Precision.HIGHEST)


def adjoint(images, weights, count):
    quarter = images.shape[2]
    padded = jnp.pad(images, ((0, 0), (0, 0), (1, 1)))
    mixed = jnp.einsum("kt,kij->tij", weights, padded, precision=lax.Precision.HIGHEST)
    pieces = []
    for phase_row in range(4):
        for phase_col in range(4):
            total = jnp.zeros((count, quarter), mixed.dtype)
            for (tr, pr, qr) in offsets:
                for (tc, pc, qc) in offsets:
                    if pr == phase_row and pc == phase_col:
                        total = total + mixed[tr * 8 + tc, 1 - qr:1 - qr + count, 1 - qc:1 - qc + quarter]
            pieces.append(total)
    return jnp.stack(pieces).reshape(4, 4, count, quarter)


def reference(observed, frame_shift, kernel_ids, groups, kernels, gains):
    weights = effective(frame_shift, kernel_ids, groups, kernels, gains)
    count = observed.shape[1]

    def operate(field):
        extended = jnp.pad(field, ((0, 0), (0, 0), (1, 1), (0, 0)))
        images = forward(extended, weights, count)
        images = jnp.pad(images, ((0, 0), (1, 1), (0, 0)))
        return adjoint(images, weights, count) + damping * field

    rhs = adjoint(jnp.pad(observed, ((0, 0), (1, 1), (0, 0))), weights, count)
    solution = jnp.zeros_like(rhs)
    residual, direction = rhs, rhs
    norm_now = jnp.sum(residual * residual)
    for step in range(ITERS):
        image = operate(direction)
        alpha = norm_now / jnp.sum(direction * image)
        solution = solution + alpha * direction
        residual = residual - alpha * image
        norm_next = jnp.sum(residual * residual)
        direction = residual + (norm_next / norm_now) * direction
        norm_now = norm_next
    return unphase(solution), unphase(residual)
```

```python
import functools

import jax
import jax.numpy as jnp
from jax import lax
from jax.experimental import pallas as pl
from jax.experimental.pallas import tpu as pltpu
from jax.sharding import PartitionSpec as P

DAMPING = 0.3
LANES = 128
HIGHEST = lax.Precision.HIGHEST
NT = (((1,), (1,)), ((), ()))
F32, BF16, I32 = jnp.float32, jnp.bfloat16, jnp.int32


def split(x):
    high = x.astype(BF16)
    return high, (x - high.astype(F32)).astype(BF16)


def paired(table):
    high, low = split(table)
    second = (lax.broadcasted_iota(I32, table.shape, 1) >> 5) & 1
    return jnp.concatenate([high, jnp.where(second == 0, low.astype(F32), 0.0).astype(BF16)], axis=0)


def row_phase(shape):
    return lax.broadcasted_iota(I32, shape, 0) & 3


def tap_table(shift, ids, members, kernels, gains):
    frames = shift.shape[1]
    copies = LANES // frames

    def tiled(x):
        return jnp.concatenate([x] * copies, axis=1)

    shape = (32, LANES)
    place = lax.broadcasted_iota(I32, shape, 0)
    lane = lax.broadcasted_iota(I32, shape, 1)
    group = place >> 3
    first = jnp.where(group == 0, 2, jnp.where(group == 1, 4, jnp.where(group == 2, 0, 6)))
    col = first + ((place >> 2) & 1)
    row = 2 + 4 * ((lane >> 5) - 1) + (place & 3)
    up = row - tiled(shift[0:1, :])
    along = col - tiled(shift[1:2, :])
    kind = tiled(ids[...])
    member = tiled(members[...])
    inside = (row >= 0) & (row < 8) & (up >= 0) & (up < 5) & (along >= 0) & (along < 5)
    count = kernels.shape[1]
    code = jnp.where(inside, kind * 25 + up * 5 + along, -1)
    total = jnp.zeros(shape, F32)
    for n in range(count):
        for a in range(5):
            for b in range(5):
                total = jnp.where(code == n * 25 + a * 5 + b, kernels[a, n, b], total)
    scale = jnp.zeros((1, LANES), F32)
    for g in range(gains.shape[0]):
        scale = jnp.where(member == g, gains[g], scale)
    return total * scale


def adjoint_kernel(shift, ids, members, kernels, gains, obs, own, send, landed, stack, mixed, sems):
    wide = obs.shape[1]
    frames = shift.shape[1]
    count = obs.shape[0] // frames
    half = wide // 2
    blocks = wide // LANES
    me = lax.axis_index("frame")

    def load(c):
        return pltpu.make_async_copy(
            obs.at[:, pl.ds(c * LANES, LANES)], landed.at[c], sems.at[c]
        )

    for c in range(blocks):
        load(c).start()
    table = tap_table(shift, ids, members, kernels, gains)
    for r in range(4):
        own[17 * 16 : 17 * 16 + 8, r * LANES : (r + 1) * LANES] = table[8 * r : 8 * r + 8]
        send[17 * 16 : 17 * 16 + 8, r * LANES : (r + 1) * LANES] = table[8 * r : 8 * r + 8]
    rest = own.shape[1] - 4 * LANES
    if rest > 0:
        own[17 * 16 : 17 * 16 + 8, 4 * LANES :] = jnp.zeros((8, rest), F32)
        send[17 * 16 : 17 * 16 + 8, 4 * LANES :] = jnp.zeros((8, rest), F32)
    source = lax.broadcasted_iota(I32, (LANES, 192), 0)
    target = lax.broadcasted_iota(I32, (LANES, 192), 1)
    pick = (source == (2 - (target >> 6)) * 32 + (target & 31)).astype(F32)
    left = paired(jnp.dot(table, pick, precision=HIGHEST, preferred_element_type=F32))

    nothing = jnp.zeros((128, wide), BF16)
    stack[0:128, :] = nothing
    stack[(count + 2) * 64 : (count + 4) * 64, :] = nothing
    for c in range(0, blocks, 2):
        load(c).wait()
        load(c + 1).wait()
        for r in range(count):
            for d in range(2):
                high, low = split(landed[c + d, pl.ds(r, frames, stride=count), :])
                cols = slice((c + d) * LANES, (c + d + 1) * LANES)
                stack[(r + 2) * 64 : (r + 2) * 64 + 32, cols] = high
                stack[(r + 2) * 64 + 32 : (r + 3) * 64, cols] = low
        cols = slice(c * LANES, (c + 2) * LANES)
        for r in range(count + 2):
            both = jnp.dot(left, stack[r * 64 : (r + 3) * 64, cols], preferred_element_type=F32)
            mixed[r * 32 : r * 32 + 32, cols] = both[:32] + both[32:]

    lane = lax.broadcasted_iota(I32, (8, wide), 1)
    near = lax.broadcasted_iota(I32, (8, LANES), 1) < 64

    def moved(r):
        t = mixed[r * 32 : r * 32 + 32, :]
        low = t[0:8] + jnp.where(lane == 0, 0.0, pltpu.roll(t[24:32], 1, 1))
        high = t[8:16] + jnp.where(lane == wide - 1, 0.0, pltpu.roll(t[16:24], wide - 1, 1))
        return low, high

    def put(at, value):
        first, second = value[:, :half], value[:, half:]
        own[at : at + 8, :half] = jnp.where(me == 0, first, second)
        send[at : at + 8, :half] = jnp.where(me == 0, second, first)
        first = jnp.where(near, value[:, half : half + LANES], 0.0)
        second = jnp.where(near, 0.0, value[:, half - LANES : half])
        own[at : at + 8, half:] = jnp.where(me == 0, first, second)
        send[at : at + 8, half:] = jnp.where(me == 0, second, first)

    for r in range(1, count + 1):
        low, high = moved(r)
        put((r - 1) * 16, low)
        put((r - 1) * 16 + 8, high)
    above, below = moved(0), moved(count + 1)
    put(count * 16, above[0] + below[0])
    put(count * 16 + 8, above[1] + below[1])


def border_kernel(own, other, first, second):
    count = (own.shape[0] - 24) // 16
    even = lax.rem(lax.axis_index("tile"), 2) == 0
    edge = own[count * 16 : count * 16 + 16] + other[count * 16 : count * 16 + 16]
    phase = row_phase((8, own.shape[1]))
    above = jnp.where(phase >= 2, edge[0:8], pltpu.roll(edge[8:16], 6, 0))
    below = jnp.where(phase < 2, edge[0:8], pltpu.roll(edge[8:16], 2, 0))
    top = own[0:32] + other[0:32]
    bottom = own[(count - 2) * 16 : count * 16] + other[(count - 2) * 16 : count * 16]
    first[0:32] = jnp.where(even, bottom, top)
    first[32:40] = jnp.where(even, below, above)
    second[0:32] = jnp.where(even, top, bottom)
    second[32:40] = jnp.where(even, above, below)


def operator_kernel(own, other, first, second, base, once, twice, sums, held, later, stack):
    ext = own.shape[1]
    half = ext - LANES
    count = (own.shape[0] - 24) // 16
    tile, tiles = lax.axis_index("tile"), lax.axis_size("tile")
    me = lax.axis_index("frame")
    even = lax.rem(tile, 2) == 0
    has_up = jnp.where(tile > 0, 1.0, 0.0).astype(F32)
    has_down = jnp.where(tile < tiles - 1, 1.0, 0.0).astype(F32)

    def both_tables(r):
        a = own[(count + 1) * 16 : (count + 1) * 16 + 8, r * LANES : (r + 1) * LANES]
        b = other[(count + 1) * 16 : (count + 1) * 16 + 8, r * LANES : (r + 1) * LANES]
        return a, b

    pieces = [both_tables(r) for r in range(4)]
    tables = [jnp.concatenate([p[d] for p in pieces], axis=0) for d in range(2)]
    earlier = [pltpu.roll(t, 32, 1) for t in tables]
    after = [pltpu.roll(t, LANES - 32, 1) for t in tables]
    block = lax.broadcasted_iota(I32, (32, LANES), 1) >> 5
    left = jnp.concatenate(
        [jnp.concatenate([t, jnp.where(block == 2, t, 0.0), jnp.where(block == 0, t, 0.0)], axis=0) for t in tables],
        axis=1,
    )
    right = jnp.concatenate(
        [jnp.concatenate([e, e, t, t, a, a], axis=0) for e, t, a in zip(earlier, tables, after)], axis=1
    )
    product = lax.dot_general(left, right, NT, precision=HIGHEST, preferred_element_type=F32)
    middle = (lax.broadcasted_iota(I32, (32, 192), 1) >> 6) == 1
    full = product[0:32]
    plain = paired(full)
    at_top = paired(full - (1.0 - has_up) * jnp.where(middle, product[32:64], 0.0))
    at_bottom = paired(full - (1.0 - has_down) * jnp.where(middle, product[64:96], 0.0))

    lane = lax.broadcasted_iota(I32, (8, LANES), 1)
    near = jnp.where(me == 0, jnp.where(lane < 64, 1.0, 0.0), jnp.where(lane < 64, 0.0, 1.0)).astype(F32)
    phase = row_phase((8, ext))

    def widen(value):
        return jnp.concatenate([value, value], axis=0)

    edge = own[count * 16 : count * 16 + 16] + other[count * 16 : count * 16 + 16]
    phase2 = row_phase((16, ext))
    up = jnp.where(even, second[...], first[...])
    down = jnp.where(even, first[...], second[...])
    held[0:16] = up[0:16]
    held[16:32] = up[16:32] + has_up * jnp.where(phase2 >= 2, edge, 0.0)
    for r in range(count):
        value = own[r * 16 : r * 16 + 16] + other[r * 16 : r * 16 + 16]
        if r == 0:
            e = up[32:40]
            value = value + jnp.where(phase2 < 2, jnp.concatenate([e, pltpu.roll(e, 6, 0)], axis=0), 0.0)
        if r == count - 1:
            e = down[32:40]
            value = value + jnp.where(phase2 >= 2, jnp.concatenate([e, pltpu.roll(e, 2, 0)], axis=0), 0.0)
        held[(r + 2) * 16 : (r + 3) * 16] = value
    held[(count + 2) * 16 : (count + 3) * 16] = down[0:16] + has_down * jnp.where(phase2 < 2, edge, 0.0)
    held[(count + 3) * 16 : (count + 4) * 16] = down[16:32]

    def expand(field, r):
        low, high = field[r * 16 : r * 16 + 8], field[r * 16 + 8 : r * 16 + 16]
        groups = jnp.concatenate([low, high, pltpu.roll(high, 1, 1), pltpu.roll(low, ext - 1, 1)], axis=0)
        a, b = split(groups)
        stack[r * 64 : r * 64 + 32] = a
        stack[r * 64 + 32 : r * 64 + 64] = b

    def masked(t):
        return jnp.concatenate([t[:, :half], t[:, half:] * near], axis=1)

    def apply(weights, field, r):
        both = jnp.dot(weights, stack[(r - 1) * 64 : (r + 2) * 64], preferred_element_type=F32)
        t = both[:32] + both[32:]
        low = t[0:8] + pltpu.roll(masked(t[24:32]), 1, 1)
        high = t[8:16] + pltpu.roll(masked(t[16:24]), ext - 1, 1)
        low = masked(low + DAMPING * field[r * 16 : r * 16 + 8])
        high = masked(high + DAMPING * field[r * 16 + 8 : r * 16 + 16])
        return jnp.concatenate([low, high], axis=0)

    def weights_of(r):
        return at_top if r == 0 else at_bottom if r == count - 1 else plain

    def folded(value):
        total = value[0:8, 0:LANES] + value[8:16, 0:LANES]
        for c in range(1, half // LANES):
            total = total + (value[0:8, c * LANES : (c + 1) * LANES] + value[8:16, c * LANES : (c + 1) * LANES])
        return total

    for r in range(count + 4):
        expand(held, r)
    totals = [jnp.zeros((8, LANES), F32) for _ in range(4)]
    for r in range(-1, count + 1):
        value = apply(weights_of(r), held, r + 2)
        if r == -1:
            value = value * has_up
        if r == count:
            value = value * has_down
        later[(r + 1) * 16 : (r + 2) * 16] = value
        if 0 <= r < count:
            once[r * 16 : r * 16 + 16] = value[:, :half]
            b = held[(r + 2) * 16 : (r + 3) * 16, :half]
            base[r * 16 : r * 16 + 16] = b
            totals[0] += folded(b * b)
            totals[1] += folded(b * value[:, :half])
            totals[2] += folded(value[:, :half] * value[:, :half])
    for r in range(count + 2):
        expand(later, r)
    for r in range(count):
        value = apply(weights_of(r), later, r + 1)[:, :half]
        twice[r * 16 : r * 16 + 16] = value
        totals[3] += folded(value * later[(r + 1) * 16 : (r + 2) * 16, :half])
    rows = jnp.concatenate([jnp.sum(t, axis=0, keepdims=True) for t in totals], axis=0)
    rows = jnp.concatenate([rows, jnp.zeros((4, LANES), F32)], axis=0)
    for p in range(sums.shape[0]):
        sums[p] = rows


def update_kernel(base, once, twice, sums, solution, residual, spread):
    @pl.when(pl.program_id(0) == 0)
    def _():
        source = lax.broadcasted_iota(I32, spread.shape, 0)
        target = lax.broadcasted_iota(I32, spread.shape, 1)
        hit = target == 4 * (source & (LANES - 1)) + (source >> 7)
        spread[...] = jnp.where(hit, 1.0, 0.0).astype(BF16)

    lanes = jnp.sum(sums[...], axis=0)

    def total(at):
        return jnp.sum(lanes[at : at + 1], axis=1, keepdims=True)

    bb, bm, mm, mmm = [total(at) for at in range(4)]
    alpha = bb / bm
    norm = alpha * alpha * mm - 2.0 * alpha * bm + bb
    beta = norm / bb
    grow = 1.0 + beta
    product = grow * grow * bm - 2.0 * grow * alpha * mm + alpha * alpha * mmm
    step = norm / product
    count = base.shape[0] // 16
    side = lax.broadcasted_iota(I32, (count // 2, 8, LANES), 1) < 4

    def arranged(x):
        x = x.reshape(count // 2, 4, 8, LANES)
        pieces = []
        for g in range(2):
            a, b = x[:, g], x[:, g + 2]
            pieces.append(jnp.where(side, a, pltpu.roll(b, 4, 1)).reshape(4 * count, LANES))
            pieces.append(jnp.where(side, pltpu.roll(a, 4, 1), b).reshape(4 * count, LANES))
        return split(jnp.concatenate(pieces, axis=1))

    for c in range(base.shape[1] // LANES):
        cols = slice(c * LANES, (c + 1) * LANES)
        b, m, mm_ = base[:, cols], once[:, cols], twice[:, cols]
        x = (alpha + step * grow) * b - (step * alpha) * m
        r = (b - alpha * m) - step * (grow * m - alpha * mm_)
        xh, xl = arranged(x)
        rh, rl = arranged(r)
        out = jnp.dot(jnp.concatenate([xh, xl, rh, rl], axis=0), spread[...], preferred_element_type=F32)
        n = 4 * count
        wide = slice(4 * c * LANES, 4 * (c + 1) * LANES)
        solution[:, wide] = out[0:n] + out[n : 2 * n]
        residual[:, wide] = out[2 * n : 3 * n] + out[3 * n : 4 * n]


def params():
    return pltpu.CompilerParams(vmem_limit_bytes=48 * 1024 * 1024)


def vmem(n):
    return [pl.BlockSpec(memory_space=pltpu.VMEM)] * n


def per_device(observed, frame_shift, kernel_ids, groups, kernels, gains):
    frames, count, wide = observed.shape
    half = wide // 2
    ext = half + LANES
    blocks = wide // LANES
    tiles, spread = lax.axis_size("tile"), lax.axis_size("frame")
    rows = (count + 1) * 16 + 8
    smem = pl.BlockSpec(memory_space=pltpu.SMEM)
    shape = jax.ShapeDtypeStruct

    own, send = pl.pallas_call(
        adjoint_kernel,
        out_shape=(shape((rows, ext), F32),) * 2,
        in_specs=vmem(3) + [smem, smem, pl.BlockSpec(memory_space=pl.ANY)],
        out_specs=tuple(vmem(2)),
        scratch_shapes=[
            pltpu.VMEM((blocks, frames * count, LANES), F32),
            pltpu.VMEM(((count + 4) * 64, wide), BF16),
            pltpu.VMEM(((count + 2) * 32, wide), F32),
            pltpu.SemaphoreType.DMA((blocks,)),
        ],
        compiler_params=params(),
        name="adjoint",
    )(frame_shift, kernel_ids, groups, kernels.transpose(1, 0, 2), gains, observed.reshape(frames * count, wide))
    other = lax.ppermute(send, "frame", [(0, 1), (1, 0)])

    first, second = pl.pallas_call(
        border_kernel,
        out_shape=(shape((40, ext), F32),) * 2,
        in_specs=vmem(2),
        out_specs=tuple(vmem(2)),
        compiler_params=params(),
        name="border",
    )(own, other)
    pairs = [(i, i ^ 1) for i in range(tiles) if i ^ 1 < tiles]
    odd_pairs = [p for i in range(1, tiles - 1, 2) for p in ((i, i + 1), (i + 1, i))]
    second = lax.ppermute(second, "tile", odd_pairs)
    first = lax.ppermute(first, "tile", pairs)

    peers = tiles * spread
    base, once, twice, sums = pl.pallas_call(
        operator_kernel,
        out_shape=(shape((count * 16, half), F32),) * 3 + (shape((peers, 8, LANES), F32),),
        in_specs=vmem(4),
        out_specs=tuple(vmem(4)),
        scratch_shapes=[
            pltpu.VMEM(((count + 4) * 16, ext), F32),
            pltpu.VMEM(((count + 2) * 16, ext), F32),
            pltpu.VMEM(((count + 4) * 64, ext), BF16),
        ],
        compiler_params=params(),
        name="operator",
    )(own, other, first, second)
    sums = lax.all_to_all(sums, ("tile", "frame"), 0, 0)

    steps = 4 if half % (4 * LANES) == 0 else 1
    part = half // steps
    solution, residual = pl.pallas_call(
        update_kernel,
        grid=(steps,),
        out_shape=(shape((count * 4, 4 * half), F32),) * 2,
        in_specs=[pl.BlockSpec((count * 16, part), lambda j: (0, j))] * 3
        + [pl.BlockSpec((peers, 8, LANES), lambda j: (0, 0, 0))],
        out_specs=(pl.BlockSpec((count * 4, 4 * part), lambda j: (0, j)),) * 2,
        scratch_shapes=[pltpu.VMEM((4 * LANES, 4 * LANES), BF16)],
        compiler_params=params(),
        name="update",
    )(base, once, twice, sums)
    return solution, residual


def solution(mesh):
    return jax.shard_map(
        per_device,
        mesh=mesh,
        in_specs=(
            P("frame", ("scene", "tile"), None),
            P("scene", "frame"),
            P("scene", "frame"),
            P("scene", "frame"),
            P(),
            P(),
        ),
        out_specs=(P(("scene", "tile"), "frame"), P(("scene", "tile"), "frame")),
        check_vma=False,
    )
```

```python
import functools

import jax
import jax.numpy as jnp
from jax import lax
from jax.experimental import pallas as pl
from jax.experimental.pallas import tpu as pltpu
from jax.sharding import PartitionSpec as P

DAMPING = 0.3
LANES = 128
HIGHEST = lax.Precision.HIGHEST
NT = (((1,), (1,)), ((), ()))
F32, BF16, I32 = jnp.float32, jnp.bfloat16, jnp.int32


def split(x):
    high = x.astype(BF16)
    return high, (x - high.astype(F32)).astype(BF16)


def paired(table):
    high, low = split(table)
    second = (lax.broadcasted_iota(I32, table.shape, 1) >> 5) & 1
    return jnp.concatenate([high, jnp.where(second == 0, low.astype(F32), 0.0).astype(BF16)], axis=0)


def row_phase(shape):
    return lax.broadcasted_iota(I32, shape, 0) & 3


def tap_table(shift, ids, members, kernels, gains):
    frames = shift.shape[1]
    copies = LANES // frames

    def tiled(x):
        return jnp.concatenate([x] * copies, axis=1)

    shape = (32, LANES)
    place = lax.broadcasted_iota(I32, shape, 0)
    lane = lax.broadcasted_iota(I32, shape, 1)
    group = place >> 3
    first = jnp.where(group == 0, 2, jnp.where(group == 1, 4, jnp.where(group == 2, 0, 6)))
    col = first + ((place >> 2) & 1)
    row = 2 + 4 * ((lane >> 5) - 1) + (place & 3)
    up = row - tiled(shift[0:1, :])
    along = col - tiled(shift[1:2, :])
    kind = tiled(ids[...])
    member = tiled(members[...])
    inside = (row >= 0) & (row < 8) & (up >= 0) & (up < 5) & (along >= 0) & (along < 5)
    count = kernels.shape[1]
    code = jnp.where(inside, kind * 25 + up * 5 + along, -1)
    total = jnp.zeros(shape, F32)
    for n in range(count):
        for a in range(5):
            for b in range(5):
                total = jnp.where(code == n * 25 + a * 5 + b, kernels[a, n, b], total)
    scale = jnp.zeros((1, LANES), F32)
    for g in range(gains.shape[0]):
        scale = jnp.where(member == g, gains[g], scale)
    return total * scale


def adjoint_kernel(
    far_shift, far_ids, far_members, far_kernels, far_gains, obs, own, send,
    landed, stack, mixed, sems, shift, ids, members, kernels, gains, small_sems,
):
    wide = obs.shape[1]
    frames = shift.shape[1]
    count = obs.shape[0] // frames
    half = wide // 2
    blocks = wide // LANES
    me = lax.axis_index("frame")

    def load(c):
        return pltpu.make_async_copy(
            obs.at[:, pl.ds(c * LANES, LANES)], landed.at[c], sems.at[c]
        )

    small = [
        pltpu.make_async_copy(far, near, small_sems.at[i])
        for i, (far, near) in enumerate(
            [(far_kernels, kernels), (far_gains, gains), (far_shift, shift), (far_ids, ids), (far_members, members)]
        )
    ]
    for copy in small:
        copy.start()
    for c in range(blocks):
        load(c).start()
    for copy in small:
        copy.wait()
    table = tap_table(shift, ids, members, kernels, gains)
    for r in range(4):
        own[17 * 16 : 17 * 16 + 8, r * LANES : (r + 1) * LANES] = table[8 * r : 8 * r + 8]
        send[17 * 16 : 17 * 16 + 8, r * LANES : (r + 1) * LANES] = table[8 * r : 8 * r + 8]
    rest = own.shape[1] - 4 * LANES
    if rest > 0:
        own[17 * 16 : 17 * 16 + 8, 4 * LANES :] = jnp.zeros((8, rest), F32)
        send[17 * 16 : 17 * 16 + 8, 4 * LANES :] = jnp.zeros((8, rest), F32)
    source = lax.broadcasted_iota(I32, (LANES, 192), 0)
    target = lax.broadcasted_iota(I32, (LANES, 192), 1)
    pick = (source == (2 - (target >> 6)) * 32 + (target & 31)).astype(F32)
    left = paired(jnp.dot(table, pick, precision=HIGHEST, preferred_element_type=F32))

    nothing = jnp.zeros((128, wide), BF16)
    stack[0:128, :] = nothing
    stack[(count + 2) * 64 : (count + 4) * 64, :] = nothing
    for c in range(0, blocks, 2):
        load(c).wait()
        load(c + 1).wait()
        for r in range(count):
            for d in range(2):
                high, low = split(landed[c + d, pl.ds(r, frames, stride=count), :])
                cols = slice((c + d) * LANES, (c + d + 1) * LANES)
                stack[(r + 2) * 64 : (r + 2) * 64 + 32, cols] = high
                stack[(r + 2) * 64 + 32 : (r + 3) * 64, cols] = low
        cols = slice(c * LANES, (c + 2) * LANES)
        for r in range(count + 2):
            both = jnp.dot(left, stack[r * 64 : (r + 3) * 64, cols], preferred_element_type=F32)
            mixed[r * 32 : r * 32 + 32, cols] = both[:32] + both[32:]

    lane = lax.broadcasted_iota(I32, (8, wide), 1)
    near = lax.broadcasted_iota(I32, (8, LANES), 1) < 64

    def moved(r):
        t = mixed[r * 32 : r * 32 + 32, :]
        low = t[0:8] + jnp.where(lane == 0, 0.0, pltpu.roll(t[24:32], 1, 1))
        high = t[8:16] + jnp.where(lane == wide - 1, 0.0, pltpu.roll(t[16:24], wide - 1, 1))
        return low, high

    def put(at, value):
        first, second = value[:, :half], value[:, half:]
        own[at : at + 8, :half] = jnp.where(me == 0, first, second)
        send[at : at + 8, :half] = jnp.where(me == 0, second, first)
        first = jnp.where(near, value[:, half : half + LANES], 0.0)
        second = jnp.where(near, 0.0, value[:, half - LANES : half])
        own[at : at + 8, half:] = jnp.where(me == 0, first, second)
        send[at : at + 8, half:] = jnp.where(me == 0, second, first)

    for r in range(1, count + 1):
        low, high = moved(r)
        put((r - 1) * 16, low)
        put((r - 1) * 16 + 8, high)
    above, below = moved(0), moved(count + 1)
    put(count * 16, above[0] + below[0])
    put(count * 16 + 8, above[1] + below[1])


def border_kernel(own, other, first, second):
    count = (own.shape[0] - 24) // 16
    even = lax.rem(lax.axis_index("tile"), 2) == 0
    edge = own[count * 16 : count * 16 + 16] + other[count * 16 : count * 16 + 16]
    phase = row_phase((8, own.shape[1]))
    above = jnp.where(phase >= 2, edge[0:8], pltpu.roll(edge[8:16], 6, 0))
    below = jnp.where(phase < 2, edge[0:8], pltpu.roll(edge[8:16], 2, 0))
    top = own[0:32] + other[0:32]
    bottom = own[(count - 2) * 16 : count * 16] + other[(count - 2) * 16 : count * 16]
    first[0:32] = jnp.where(even, bottom, top)
    first[32:40] = jnp.where(even, below, above)
    second[0:32] = jnp.where(even, top, bottom)
    second[32:40] = jnp.where(even, above, below)


def operator_kernel(own, other, first, second, base, once, twice, spread, sums, held, later, stack):
    ext = own.shape[1]
    half = ext - LANES
    count = (own.shape[0] - 24) // 16
    tile, tiles = lax.axis_index("tile"), lax.axis_size("tile")
    me = lax.axis_index("frame")
    even = lax.rem(tile, 2) == 0
    has_up = jnp.where(tile > 0, 1.0, 0.0).astype(F32)
    has_down = jnp.where(tile < tiles - 1, 1.0, 0.0).astype(F32)

    def both_tables(r):
        a = own[(count + 1) * 16 : (count + 1) * 16 + 8, r * LANES : (r + 1) * LANES]
        b = other[(count + 1) * 16 : (count + 1) * 16 + 8, r * LANES : (r + 1) * LANES]
        return a, b

    pieces = [both_tables(r) for r in range(4)]
    tables = [jnp.concatenate([p[d] for p in pieces], axis=0) for d in range(2)]
    earlier = [pltpu.roll(t, 32, 1) for t in tables]
    after = [pltpu.roll(t, LANES - 32, 1) for t in tables]
    block = lax.broadcasted_iota(I32, (32, LANES), 1) >> 5
    left = jnp.concatenate(
        [jnp.concatenate([t, jnp.where(block == 2, t, 0.0), jnp.where(block == 0, t, 0.0)], axis=0) for t in tables],
        axis=1,
    )
    right = jnp.concatenate(
        [jnp.concatenate([e, e, t, t, a, a], axis=0) for e, t, a in zip(earlier, tables, after)], axis=1
    )
    product = lax.dot_general(left, right, NT, precision=HIGHEST, preferred_element_type=F32)
    middle = (lax.broadcasted_iota(I32, (32, 192), 1) >> 6) == 1
    full = product[0:32]
    plain = paired(full)
    at_top = paired(full - (1.0 - has_up) * jnp.where(middle, product[32:64], 0.0))
    at_bottom = paired(full - (1.0 - has_down) * jnp.where(middle, product[64:96], 0.0))

    source = lax.broadcasted_iota(I32, spread.shape, 0)
    target = lax.broadcasted_iota(I32, spread.shape, 1)
    hit = target == 4 * (source & (LANES - 1)) + (source >> 7)
    spread[...] = jnp.where(hit, 1.0, 0.0).astype(BF16)
    lane = lax.broadcasted_iota(I32, (8, LANES), 1)
    near = jnp.where(me == 0, jnp.where(lane < 64, 1.0, 0.0), jnp.where(lane < 64, 0.0, 1.0)).astype(F32)
    phase = row_phase((8, ext))

    def widen(value):
        return jnp.concatenate([value, value], axis=0)

    edge = own[count * 16 : count * 16 + 16] + other[count * 16 : count * 16 + 16]
    phase2 = row_phase((16, ext))
    up = jnp.where(even, second[...], first[...])
    down = jnp.where(even, first[...], second[...])
    held[0:16] = up[0:16]
    held[16:32] = up[16:32] + has_up * jnp.where(phase2 >= 2, edge, 0.0)
    for r in range(count):
        value = own[r * 16 : r * 16 + 16] + other[r * 16 : r * 16 + 16]
        if r == 0:
            e = up[32:40]
            value = value + jnp.where(phase2 < 2, jnp.concatenate([e, pltpu.roll(e, 6, 0)], axis=0), 0.0)
        if r == count - 1:
            e = down[32:40]
            value = value + jnp.where(phase2 >= 2, jnp.concatenate([e, pltpu.roll(e, 2, 0)], axis=0), 0.0)
        held[(r + 2) * 16 : (r + 3) * 16] = value
    held[(count + 2) * 16 : (count + 3) * 16] = down[0:16] + has_down * jnp.where(phase2 < 2, edge, 0.0)
    held[(count + 3) * 16 : (count + 4) * 16] = down[16:32]

    def expand(field, r):
        low, high = field[r * 16 : r * 16 + 8], field[r * 16 + 8 : r * 16 + 16]
        groups = jnp.concatenate([low, high, pltpu.roll(high, 1, 1), pltpu.roll(low, ext - 1, 1)], axis=0)
        a, b = split(groups)
        stack[r * 64 : r * 64 + 32] = a
        stack[r * 64 + 32 : r * 64 + 64] = b

    def masked(t):
        return jnp.concatenate([t[:, :half], t[:, half:] * near], axis=1)

    def apply(weights, field, r):
        both = jnp.dot(weights, stack[(r - 1) * 64 : (r + 2) * 64], preferred_element_type=F32)
        t = both[:32] + both[32:]
        low = t[0:8] + pltpu.roll(masked(t[24:32]), 1, 1)
        high = t[8:16] + pltpu.roll(masked(t[16:24]), ext - 1, 1)
        low = masked(low + DAMPING * field[r * 16 : r * 16 + 8])
        high = masked(high + DAMPING * field[r * 16 + 8 : r * 16 + 16])
        return jnp.concatenate([low, high], axis=0)

    def weights_of(r):
        return at_top if r == 0 else at_bottom if r == count - 1 else plain

    def folded(value):
        total = value[0:8, 0:LANES] + value[8:16, 0:LANES]
        for c in range(1, half // LANES):
            total = total + (value[0:8, c * LANES : (c + 1) * LANES] + value[8:16, c * LANES : (c + 1) * LANES])
        return total

    for r in range(count + 4):
        expand(held, r)
    totals = [jnp.zeros((8, LANES), F32) for _ in range(4)]
    for r in range(-1, count + 1):
        value = apply(weights_of(r), held, r + 2)
        if r == -1:
            value = value * has_up
        if r == count:
            value = value * has_down
        later[(r + 1) * 16 : (r + 2) * 16] = value
        if 0 <= r < count:
            once[r * 16 : r * 16 + 16] = value[:, :half]
            b = held[(r + 2) * 16 : (r + 3) * 16, :half]
            base[r * 16 : r * 16 + 16] = b
            totals[0] += folded(b * b)
            totals[1] += folded(b * value[:, :half])
            totals[2] += folded(value[:, :half] * value[:, :half])
    for r in range(count + 2):
        expand(later, r)
    for r in range(count):
        value = apply(weights_of(r), later, r + 1)[:, :half]
        twice[r * 16 : r * 16 + 16] = value
        totals[3] += folded(value * later[(r + 1) * 16 : (r + 2) * 16, :half])
    rows = jnp.concatenate([jnp.sum(t, axis=0, keepdims=True) for t in totals], axis=0)
    rows = jnp.concatenate([rows, jnp.zeros((4, LANES), F32)], axis=0)
    for p in range(sums.shape[0]):
        sums[p] = rows


def update_kernel(base, once, twice, spread, sums, solution, residual, near_x, near_r, sems):
    lanes = jnp.sum(sums[...], axis=0)

    def total(at):
        return jnp.sum(lanes[at : at + 1], axis=1, keepdims=True)

    bb, bm, mm, mmm = [total(at) for at in range(4)]
    alpha = bb / bm
    norm = alpha * alpha * mm - 2.0 * alpha * bm + bb
    beta = norm / bb
    grow = 1.0 + beta
    product = grow * grow * bm - 2.0 * grow * alpha * mm + alpha * alpha * mmm
    step = norm / product
    count = base.shape[0] // 16
    side = lax.broadcasted_iota(I32, (count // 2, 8, LANES), 1) < 4

    def arranged(x):
        x = x.reshape(count // 2, 4, 8, LANES)
        pieces = []
        for g in range(2):
            a, b = x[:, g], x[:, g + 2]
            pieces.append(jnp.where(side, a, pltpu.roll(b, 4, 1)).reshape(4 * count, LANES))
            pieces.append(jnp.where(side, pltpu.roll(a, 4, 1), b).reshape(4 * count, LANES))
        return split(jnp.concatenate(pieces, axis=1))

    def stores(c):
        wide = pl.ds(4 * c * LANES, 4 * LANES)
        return [
            pltpu.make_async_copy(near.at[:, wide], far.at[:, wide], sems.at[i, c])
            for i, (near, far) in enumerate([(near_x, solution), (near_r, residual)])
        ]

    for c in range(base.shape[1] // LANES):
        cols = slice(c * LANES, (c + 1) * LANES)
        b, m, mm_ = base[:, cols], once[:, cols], twice[:, cols]
        x = (alpha + step * grow) * b - (step * alpha) * m
        r = (b - alpha * m) - step * (grow * m - alpha * mm_)
        xh, xl = arranged(x)
        rh, rl = arranged(r)
        out = jnp.dot(jnp.concatenate([xh, xl, rh, rl], axis=0), spread[...], preferred_element_type=F32)
        n = 4 * count
        wide = slice(4 * c * LANES, 4 * (c + 1) * LANES)
        near_x[:, wide] = out[0:n] + out[n : 2 * n]
        near_r[:, wide] = out[2 * n : 3 * n] + out[3 * n : 4 * n]
        for copy in stores(c):
            copy.start()
    for c in range(base.shape[1] // LANES):
        for copy in stores(c):
            copy.wait()


def params(mebibytes=24):
    return pltpu.CompilerParams(vmem_limit_bytes=mebibytes * 1024 * 1024)


def vmem(n):
    return [pl.BlockSpec(memory_space=pltpu.VMEM)] * n


def per_device(observed, frame_shift, kernel_ids, groups, kernels, gains):
    frames, count, wide = observed.shape
    half = wide // 2
    ext = half + LANES
    blocks = wide // LANES
    tiles, spread = lax.axis_size("tile"), lax.axis_size("frame")
    rows = (count + 1) * 16 + 8
    far = pl.BlockSpec(memory_space=pltpu.HBM)
    shape = jax.ShapeDtypeStruct

    own, send = pl.pallas_call(
        adjoint_kernel,
        out_shape=(shape((rows, ext), F32),) * 2,
        in_specs=[far] * 6,
        out_specs=tuple(vmem(2)),
        scratch_shapes=[
            pltpu.VMEM((blocks, frames * count, LANES), F32),
            pltpu.VMEM(((count + 4) * 64, wide), BF16),
            pltpu.VMEM(((count + 2) * 32, wide), F32),
            pltpu.SemaphoreType.DMA((blocks,)),
            pltpu.VMEM(frame_shift.shape, I32),
            pltpu.VMEM(kernel_ids.shape, I32),
            pltpu.VMEM(groups.shape, I32),
            pltpu.SMEM((5, kernels.shape[0], 5), F32),
            pltpu.SMEM(gains.shape, F32),
            pltpu.SemaphoreType.DMA((5,)),
        ],
        compiler_params=params(),
        name="adjoint",
    )(
        *(
            pltpu.with_memory_space_constraint(x, pltpu.HBM)
            for x in (frame_shift, kernel_ids, groups, kernels.transpose(1, 0, 2), gains, observed.reshape(-1, wide))
        )
    )
    other = lax.ppermute(send, "frame", [(0, 1), (1, 0)])

    first, second = pl.pallas_call(
        border_kernel,
        out_shape=(shape((40, ext), F32),) * 2,
        in_specs=vmem(2),
        out_specs=tuple(vmem(2)),
        compiler_params=params(),
        name="border",
    )(own, other)
    pairs = [(i, i ^ 1) for i in range(tiles) if i ^ 1 < tiles]
    odd_pairs = [p for i in range(1, tiles - 1, 2) for p in ((i, i + 1), (i + 1, i))]
    second = lax.ppermute(second, "tile", odd_pairs)
    first = lax.ppermute(first, "tile", pairs)

    peers = tiles * spread
    base, once, twice, spreading, sums = pl.pallas_call(
        operator_kernel,
        out_shape=(shape((count * 16, half), F32),) * 3
        + (shape((4 * LANES, 4 * LANES), BF16), shape((peers, 8, LANES), F32)),
        in_specs=vmem(4),
        out_specs=tuple(vmem(5)),
        scratch_shapes=[
            pltpu.VMEM(((count + 4) * 16, ext), F32),
            pltpu.VMEM(((count + 2) * 16, ext), F32),
            pltpu.VMEM(((count + 4) * 64, ext), BF16),
        ],
        compiler_params=params(),
        name="operator",
    )(own, other, first, second)
    sums = lax.all_to_all(sums, ("tile", "frame"), 0, 0)

    solution, residual = pl.pallas_call(
        update_kernel,
        out_shape=(shape((count * 4, 4 * half), F32),) * 2,
        in_specs=vmem(5),
        out_specs=(far,) * 2,
        scratch_shapes=[pltpu.VMEM((count * 4, 4 * half), F32)] * 2
        + [pltpu.SemaphoreType.DMA((2, half // LANES))],
        compiler_params=params(),
        name="update",
    )(base, once, twice, spreading, sums)
    return solution, residual


def solution(mesh):
    return jax.shard_map(
        per_device,
        mesh=mesh,
        in_specs=(
            P("frame", ("scene", "tile"), None),
            P("scene", "frame"),
            P("scene", "frame"),
            P("scene", "frame"),
            P(),
            P(),
        ),
        out_specs=(P(("scene", "tile"), "frame"), P(("scene", "tile"), "frame")),
        check_vma=False,
    )
```

```python
import functools

import jax
import jax.numpy as jnp
from jax import lax
from jax.experimental import pallas as pl
from jax.experimental.pallas import tpu as pltpu
from jax.sharding import PartitionSpec as P

DAMPING = 0.3
LANES = 128
HIGHEST = lax.Precision.HIGHEST
NT = (((1,), (1,)), ((), ()))
F32, BF16, I32 = jnp.float32, jnp.bfloat16, jnp.int32


def split(x):
    high = x.astype(BF16)
    return high, (x - high.astype(F32)).astype(BF16)


def paired(table):
    high, low = split(table)
    second = (lax.broadcasted_iota(I32, table.shape, 1) >> 5) & 1
    return jnp.concatenate([high, jnp.where(second == 0, low.astype(F32), 0.0).astype(BF16)], axis=0)


def row_phase(shape):
    return lax.broadcasted_iota(I32, shape, 0) & 3


def tap_table(shift, ids, members, kernels, gains):
    frames = shift.shape[1]
    copies = LANES // frames

    def tiled(x):
        return jnp.concatenate([x] * copies, axis=1)

    shape = (32, LANES)
    place = lax.broadcasted_iota(I32, shape, 0)
    lane = lax.broadcasted_iota(I32, shape, 1)
    group = place >> 3
    first = jnp.where(group == 0, 2, jnp.where(group == 1, 4, jnp.where(group == 2, 0, 6)))
    col = first + ((place >> 2) & 1)
    row = 2 + 4 * ((lane >> 5) - 1) + (place & 3)
    up = row - tiled(shift[0:1, :])
    along = col - tiled(shift[1:2, :])
    kind = tiled(ids[...])
    member = tiled(members[...])
    inside = (row >= 0) & (row < 8) & (up >= 0) & (up < 5) & (along >= 0) & (along < 5)
    count = kernels.shape[1]
    code = jnp.where(inside, kind * 25 + up * 5 + along, -1)
    total = jnp.zeros(shape, F32)
    for n in range(count):
        for a in range(5):
            for b in range(5):
                total = jnp.where(code == n * 25 + a * 5 + b, kernels[a, n, b], total)
    scale = jnp.zeros((1, LANES), F32)
    for g in range(gains.shape[0]):
        scale = jnp.where(member == g, gains[g], scale)
    return total * scale


def put_halves(own, send, at, value, me, near):
    half = value.shape[1] // 2
    first, second = value[:, :half], value[:, half:]
    own[at : at + 8, :half] = jnp.where(me == 0, first, second)
    send[at : at + 8, :half] = jnp.where(me == 0, second, first)
    first = jnp.where(near, value[:, half : half + LANES], 0.0)
    second = jnp.where(near, 0.0, value[:, half - LANES : half])
    own[at : at + 8, half:] = jnp.where(me == 0, first, second)
    send[at : at + 8, half:] = jnp.where(me == 0, second, first)


def moved_image(t, lane):
    wide = t.shape[1]
    low = t[0:8] + jnp.where(lane == 0, 0.0, pltpu.roll(t[24:32], 1, 1))
    high = t[8:16] + jnp.where(lane == wide - 1, 0.0, pltpu.roll(t[16:24], wide - 1, 1))
    return low, high


def two_rows(weights, columns):
    both = jnp.dot(weights, columns, preferred_element_type=F32)
    return both[0:32] + both[32:64], both[64:96] + both[96:128]


def one_row(weights, columns):
    both = jnp.dot(weights[0:64, 0:192], columns, preferred_element_type=F32)
    return both[0:32] + both[32:64]


def keep(stack, at, cols, high, low):
    stack[at * 64 : at * 64 + 32, cols] = high
    stack[at * 64 + 32 : at * 64 + 64, cols] = low


def outer_kernel(
    far_shift, far_ids, far_members, far_kernels, far_gains, obs, landed, own, send, weights,
    top, bottom, mixed, sems, shift, ids, members, kernels, gains, small_sems,
):
    wide = obs.shape[1]
    frames = shift.shape[1]
    count = obs.shape[0] // frames
    blocks = wide // LANES
    me = lax.axis_index("frame")

    def load(c):
        return pltpu.make_async_copy(obs.at[:, pl.ds(c * LANES, LANES)], landed.at[c], sems.at[c])

    small = [
        pltpu.make_async_copy(far, near, small_sems.at[i])
        for i, (far, near) in enumerate(
            [(far_kernels, kernels), (far_gains, gains), (far_shift, shift), (far_ids, ids), (far_members, members)]
        )
    ]
    for copy in small:
        copy.start()
    for c in range(blocks):
        load(c).start()
    nothing = jnp.zeros((128, wide), BF16)
    top[0:128, :] = nothing
    bottom[192:320, :] = nothing
    for copy in small:
        copy.wait()
    table = tap_table(shift, ids, members, kernels, gains)
    for r in range(4):
        own[80:88, r * LANES : (r + 1) * LANES] = table[8 * r : 8 * r + 8]
        send[80:88, r * LANES : (r + 1) * LANES] = table[8 * r : 8 * r + 8]
    rest = own.shape[1] - 4 * LANES
    if rest > 0:
        own[80:88, 4 * LANES :] = jnp.zeros((8, rest), F32)
        send[80:88, 4 * LANES :] = jnp.zeros((8, rest), F32)
    source = lax.broadcasted_iota(I32, (LANES, 512), 0)
    target = lax.broadcasted_iota(I32, (LANES, 512), 1)
    place = (target & 255) - 64 * (target >> 8)
    pick = (source == (2 - (place >> 6)) * 32 + (place & 31)) & (place >= 0) & (place < 192)
    both = jnp.dot(table, pick.astype(F32), precision=HIGHEST, preferred_element_type=F32)
    left = jnp.concatenate([paired(both[:, 0:256]), paired(both[:, 256:512])], axis=0)
    weights[...] = left

    for c in range(0, blocks, 2):
        load(c).wait()
        load(c + 1).wait()
        for d in range(2):
            cols = slice((c + d) * LANES, (c + d + 1) * LANES)
            for r in range(3):
                keep(top, 2 + r, cols, *split(landed[c + d, pl.ds(r, frames, stride=count), :]))
                keep(bottom, r, cols, *split(landed[c + d, pl.ds(count - 3 + r, frames, stride=count), :]))
        cols = slice(c * LANES, (c + 2) * LANES)
        a, b = two_rows(left, top[0:256, cols])
        mixed[0:32, cols] = a
        mixed[32:64, cols] = b
        mixed[64:96, cols] = one_row(left, top[128:320, cols])
        mixed[96:128, cols] = one_row(left, bottom[0:192, cols])
        a, b = two_rows(left, bottom[64:320, cols])
        mixed[128:160, cols] = a
        mixed[160:192, cols] = b

    lane = lax.broadcasted_iota(I32, (8, wide), 1)
    near = lax.broadcasted_iota(I32, (8, LANES), 1) < 64
    above, below = moved_image(mixed[0:32, :], lane), moved_image(mixed[160:192, :], lane)
    for g in range(2):
        put_halves(own, send, 8 * g, above[g] + below[g], me, near)
    for r in range(1, 5):
        image = moved_image(mixed[r * 32 : r * 32 + 32, :], lane)
        for g in range(2):
            put_halves(own, send, r * 16 + 8 * g, image[g], me, near)


def inner_rows(first, landed, weights, own, send, at, stack, mixed):
    blocks, wide = landed.shape[0], stack.shape[1]
    frames = 32
    count = landed.shape[1] // frames
    rows = mixed.shape[0] // 32
    left = weights[...]
    for c in range(0, blocks, 2):
        for d in range(2):
            cols = slice((c + d) * LANES, (c + d + 1) * LANES)
            for r in range(rows + 2):
                keep(stack, r, cols, *split(landed[c + d, pl.ds(first - 1 + r, frames, stride=count), :]))
        cols = slice(c * LANES, (c + 2) * LANES)
        for r in range(0, rows, 2):
            a, b = two_rows(left, stack[r * 64 : r * 64 + 256, cols])
            mixed[r * 32 : r * 32 + 32, cols] = a
            mixed[r * 32 + 32 : r * 32 + 64, cols] = b
    lane = lax.broadcasted_iota(I32, (8, wide), 1)
    near = lax.broadcasted_iota(I32, (8, LANES), 1) < 64
    me = lax.axis_index("frame")
    for r in range(rows):
        image = moved_image(mixed[r * 32 : r * 32 + 32, :], lane)
        for g in range(2):
            put_halves(own, send.at[at : at + rows * 16], r * 16 + 8 * g, image[g], me, near)


def early_kernel(first, landed, weights, own, send, stack, mixed):
    inner_rows(first, landed, weights, own, send, 0, stack, mixed)


def late_kernel(first, landed, weights, sent, after, own, send, stack, mixed):
    rows = sent.shape[0]
    send[0:rows] = sent[...]
    inner_rows(first, landed, weights, own, send, rows, stack, mixed)


def border_kernel(own, other, first, second):
    even = lax.rem(lax.axis_index("tile"), 2) == 0
    edge = own[0:16] + other[0:16]
    phase = row_phase((8, own.shape[1]))
    above = jnp.where(phase >= 2, edge[0:8], pltpu.roll(edge[8:16], 6, 0))
    below = jnp.where(phase < 2, edge[0:8], pltpu.roll(edge[8:16], 2, 0))
    top = own[16:48] + other[16:48]
    bottom = own[48:80] + other[48:80]
    first[0:32] = jnp.where(even, bottom, top)
    first[32:40] = jnp.where(even, below, above)
    second[0:32] = jnp.where(even, top, bottom)
    second[32:40] = jnp.where(even, above, below)


def halo_mask():
    lane = lax.broadcasted_iota(I32, (8, LANES), 1)
    here = lax.axis_index("frame") == 0
    return jnp.where(here, jnp.where(lane < 64, 1.0, 0.0), jnp.where(lane < 64, 0.0, 1.0)).astype(F32)


def expand(stack, at, value):
    ext = value.shape[1]
    low, high = value[0:8], value[8:16]
    groups = jnp.concatenate([low, high, pltpu.roll(high, 1, 1), pltpu.roll(low, ext - 1, 1)], axis=0)
    keep(stack, at, slice(None), *split(groups))


def finished(t, field, near):
    ext = t.shape[1]
    half = ext - LANES

    def masked(x):
        return jnp.concatenate([x[:, :half], x[:, half:] * near], axis=1)

    low = t[0:8] + pltpu.roll(masked(t[24:32]), 1, 1)
    high = t[8:16] + pltpu.roll(masked(t[16:24]), ext - 1, 1)
    return jnp.concatenate(
        [masked(low + DAMPING * field[0:8]), masked(high + DAMPING * field[8:16])], axis=0
    )


def folded(a, b):
    total = None
    for c in range(0, a.shape[1] - LANES + 1, LANES):
        for g in (0, 8):
            term = a[g : g + 8, c : c + LANES] * b[g : g + 8, c : c + LANES]
            total = term if total is None else total + term
    return total


def interior_kernel(
    own1, other1, own_early, own_late, other2, base, once, twice, stack1, stack2, tables, spread, sums
):
    ext = own1.shape[1]
    half = ext - LANES
    early = own_early.shape[0] // 16
    inner = other2.shape[0] // 16
    tile, tiles = lax.axis_index("tile"), lax.axis_size("tile")
    no_up = jnp.where(tile > 0, 0.0, 1.0).astype(F32)
    no_down = jnp.where(tile < tiles - 1, 0.0, 1.0).astype(F32)

    taps = [
        jnp.concatenate([ref[80:88, r * LANES : (r + 1) * LANES] for r in range(4)], axis=0) for ref in (own1, other1)
    ]
    block = lax.broadcasted_iota(I32, (32, LANES), 1) >> 5
    left = jnp.concatenate(
        [jnp.concatenate([t, jnp.where(block == 2, t, 0.0), jnp.where(block == 0, t, 0.0)], axis=0) for t in taps],
        axis=1,
    )
    empty = jnp.zeros((64, LANES), F32)
    right = []
    for t in taps:
        e, a = pltpu.roll(t, 32, 1), pltpu.roll(t, LANES - 32, 1)
        right.append(jnp.concatenate([e, e, t, t, a, a, empty, empty, e, e, t, t, a, a], axis=0))
    product = lax.dot_general(
        left, jnp.concatenate(right, axis=1), NT, precision=HIGHEST, preferred_element_type=F32
    )
    lane = lax.broadcasted_iota(I32, (32, 512), 1)
    middle = ((lane >> 6) == 1) | ((lane >> 6) == 6)
    full = product[0:32]
    at_top = full - no_up * jnp.where(middle, product[32:64], 0.0)
    at_bottom = full - no_down * jnp.where(middle, product[64:96], 0.0)
    plain_a, plain_b = paired(full[:, 0:256]), paired(full[:, 256:512])
    top_a, top_b = paired(at_top[:, 0:256]), paired(at_top[:, 256:512])
    bottom_a, bottom_b = paired(at_bottom[:, 0:256]), paired(at_bottom[:, 256:512])
    pairs = [(plain_a, plain_b), (plain_a, top_b), (top_a, plain_b), (plain_a, bottom_b), (bottom_a, plain_b)]
    for i, (a, b) in enumerate(pairs):
        tables[i * 128 : i * 128 + 64] = a
        tables[i * 128 + 64 : i * 128 + 128] = b
    plain = jnp.concatenate([plain_a, plain_b], axis=0)

    source = lax.broadcasted_iota(I32, spread.shape, 0)
    target = lax.broadcasted_iota(I32, spread.shape, 1)
    hit = target == 4 * (source & (LANES - 1)) + (source >> 7)
    spread[...] = jnp.where(hit, 1.0, 0.0).astype(BF16)
    near = halo_mask()
    totals = [jnp.zeros((8, LANES), F32) for _ in range(4)]

    for r in range(inner + 2):
        if r == 0:
            value = own1[32:48] + other1[32:48]
        elif r == inner + 1:
            value = own1[48:64] + other1[48:64]
        else:
            at = (r - 1) * 16
            mine = own_early if r - 1 < early else own_late
            off = at if r - 1 < early else at - early * 16
            value = mine[off : off + 16] + other2[at : at + 16]
        base[r * 16 : r * 16 + 16] = value
        totals[0] += folded(value[:, :half], value[:, :half])
        expand(stack1, r, value)
    for r in range(0, inner, 2):
        images = two_rows(plain, stack1[r * 64 : r * 64 + 256])
        for d in range(2):
            field = base[(r + d + 1) * 16 : (r + d + 2) * 16]
            value = finished(images[d], field, near)
            once[(r + d) * 16 : (r + d + 1) * 16] = value
            totals[1] += folded(field[:, :half], value[:, :half])
            totals[2] += folded(value[:, :half], value[:, :half])
            expand(stack2, r + d, value)
    for r in range(0, inner - 2, 2):
        images = two_rows(plain, stack2[r * 64 : r * 64 + 256])
        for d in range(2):
            field = once[(r + d + 1) * 16 : (r + d + 2) * 16]
            value = finished(images[d], field, near)[:, :half]
            twice[(r + d) * 16 : (r + d + 1) * 16] = value
            totals[3] += folded(field[:, :half], value)
    for i in range(4):
        sums[i * 8 : i * 8 + 8] = totals[i]


def rim_kernel(
    own, other, first, second, base, once, stack1, stack2, tables, partial,
    base_rim, once_rim, twice_rim, sums, above1, below1, above2, below2,
):
    ext = own.shape[1]
    half = ext - LANES
    inner = base.shape[0] // 16
    tile, tiles = lax.axis_index("tile"), lax.axis_size("tile")
    even = lax.rem(tile, 2) == 0
    has_up = jnp.where(tile > 0, 1.0, 0.0).astype(F32)
    has_down = jnp.where(tile < tiles - 1, 1.0, 0.0).astype(F32)
    near = halo_mask()
    phase = row_phase((16, ext))
    totals = [partial[i * 8 : i * 8 + 8] for i in range(4)]
    plain = tables[0:128]

    above1[192:320] = stack1[0:128]
    below1[0:128] = stack1[(inner - 2) * 64 : inner * 64]
    above2[192:320] = stack2[0:128]
    below2[0:128] = stack2[(inner - 4) * 64 : (inner - 2) * 64]

    edge = own[0:16] + other[0:16]
    up = jnp.where(even, second[...], first[...])
    down = jnp.where(even, first[...], second[...])
    rows = {-2: up[0:16]}
    rows[-1] = up[16:32] + has_up * jnp.where(phase >= 2, edge, 0.0)
    e = up[32:40]
    spare = jnp.where(phase < 2, jnp.concatenate([e, pltpu.roll(e, 6, 0)], axis=0), 0.0)
    rows[0] = own[16:32] + other[16:32] + spare
    rows[1] = base[0:16]
    e = down[32:40]
    spare = jnp.where(phase >= 2, jnp.concatenate([e, pltpu.roll(e, 2, 0)], axis=0), 0.0)
    low_rows = {0: base[(inner - 1) * 16 : inner * 16]}
    low_rows[1] = own[64:80] + other[64:80] + spare
    low_rows[2] = down[0:16] + has_down * jnp.where(phase < 2, edge, 0.0)
    low_rows[3] = down[16:32]
    for i in range(3):
        expand(above1, i, rows[i - 2])
        expand(below1, i + 2, low_rows[i + 1])
    base_rim[0:16] = rows[0][:, :half]
    base_rim[16:32] = low_rows[1][:, :half]
    totals[0] += folded(rows[0][:, :half], rows[0][:, :half])
    totals[0] += folded(low_rows[1][:, :half], low_rows[1][:, :half])

    a, b = two_rows(tables[128:256], above1[0:256])
    c = one_row(plain, above1[128:320])
    high = [finished(a, rows[-1], near) * has_up, finished(b, rows[0], near), finished(c, rows[1], near)]
    a = one_row(plain, below1[0:192])
    b, c = two_rows(tables[512:640], below1[64:320])
    deep = [
        finished(a, low_rows[0], near),
        finished(b, low_rows[1], near),
        finished(c, low_rows[2], near) * has_down,
    ]
    for i in range(3):
        expand(above2, i, high[i])
        expand(below2, i + 2, deep[i])
    pieces = [(rows[0], high[1]), (rows[1], high[2]), (low_rows[0], deep[0]), (low_rows[1], deep[1])]
    for i, (field, value) in enumerate(pieces):
        once_rim[i * 16 : i * 16 + 16] = value[:, :half]
        totals[1] += folded(field[:, :half], value[:, :half])
        totals[2] += folded(value[:, :half], value[:, :half])

    a, b = two_rows(tables[256:384], above2[0:256])
    c = one_row(plain, above2[128:320])
    d = one_row(plain, below2[0:192])
    e, f = two_rows(tables[384:512], below2[64:320])
    fields = [high[1], high[2], once[0:16], once[(inner - 3) * 16 : (inner - 2) * 16], deep[0], deep[1]]
    for i, (t, field) in enumerate(zip([a, b, c, d, e, f], fields)):
        value = finished(t, field, near)[:, :half]
        twice_rim[i * 16 : i * 16 + 16] = value
        totals[3] += folded(field[:, :half], value)
    lines = jnp.concatenate([jnp.sum(t, axis=0, keepdims=True) for t in totals], axis=0)
    lines = jnp.concatenate([lines, jnp.zeros((4, LANES), F32)], axis=0)
    for p in range(sums.shape[0]):
        sums[p] = lines


def update_kernel(base, once, twice, base_rim, once_rim, twice_rim, spread, sums, solution, residual, near_x, near_r, sems):
    lanes = jnp.sum(sums[...], axis=0)

    def total(at):
        return jnp.sum(lanes[at : at + 1], axis=1, keepdims=True)

    bb, bm, mm, mmm = [total(at) for at in range(4)]
    alpha = bb / bm
    norm = alpha * alpha * mm - 2.0 * alpha * bm + bb
    beta = norm / bb
    grow = 1.0 + beta
    product = grow * grow * bm - 2.0 * grow * alpha * mm + alpha * alpha * mmm
    step = norm / product
    count = base.shape[0] // 16 + 2
    half = base_rim.shape[1]
    side = lax.broadcasted_iota(I32, (count // 2, 8, LANES), 1) < 4

    def arranged(x):
        x = x.reshape(count // 2, 4, 8, LANES)
        pieces = []
        for g in range(2):
            a, b = x[:, g], x[:, g + 2]
            pieces.append(jnp.where(side, a, pltpu.roll(b, 4, 1)).reshape(4 * count, LANES))
            pieces.append(jnp.where(side, pltpu.roll(a, 4, 1), b).reshape(4 * count, LANES))
        return split(jnp.concatenate(pieces, axis=1))

    def stores(c):
        wide = pl.ds(4 * c * LANES, 4 * LANES)
        return [
            pltpu.make_async_copy(near.at[:, wide], far.at[:, wide], sems.at[i, c])
            for i, (near, far) in enumerate([(near_x, solution), (near_r, residual)])
        ]

    def rows_of(middle, rim, cols):
        n = rim.shape[0] // 2
        return jnp.concatenate([rim[0:n, cols], middle[:, cols], rim[n : 2 * n, cols]], axis=0)

    for c in range(half // LANES):
        cols = slice(c * LANES, (c + 1) * LANES)
        b, m, mm_ = rows_of(base, base_rim, cols), rows_of(once, once_rim, cols), rows_of(twice, twice_rim, cols)
        x = (alpha + step * grow) * b - (step * alpha) * m
        r = (b - alpha * m) - step * (grow * m - alpha * mm_)
        xh, xl = arranged(x)
        rh, rl = arranged(r)
        out = jnp.dot(jnp.concatenate([xh, xl, rh, rl], axis=0), spread[...], preferred_element_type=F32)
        n = 4 * count
        wide = slice(4 * c * LANES, 4 * (c + 1) * LANES)
        near_x[:, wide] = out[0:n] + out[n : 2 * n]
        near_r[:, wide] = out[2 * n : 3 * n] + out[3 * n : 4 * n]
        for copy in stores(c):
            copy.start()
    for c in range(half // LANES):
        for copy in stores(c):
            copy.wait()


def params(mebibytes=24):
    return pltpu.CompilerParams(vmem_limit_bytes=mebibytes * 1024 * 1024)


def cost(units):
    return pl.CostEstimate(flops=int(units * 10**9), bytes_accessed=int(units * 2**22), transcendentals=0)


def vmem(n):
    return [pl.BlockSpec(memory_space=pltpu.VMEM)] * n


def per_device(observed, frame_shift, kernel_ids, groups, kernels, gains):
    frames, count, wide = observed.shape
    half = wide // 2
    ext = half + LANES
    blocks = wide // LANES
    tiles, spread = lax.axis_size("tile"), lax.axis_size("frame")
    far = pl.BlockSpec(memory_space=pltpu.HBM)
    shape = jax.ShapeDtypeStruct
    inner = count - 4
    early = inner // 4 * 2
    late = inner - early

    landed, own, send, weights = pl.pallas_call(
        outer_kernel,
        out_shape=(
            shape((blocks, frames * count, LANES), F32),
            shape((88, ext), F32),
            shape((88, ext), F32),
            shape((128, 256), BF16),
        ),
        in_specs=[far] * 6,
        out_specs=tuple(vmem(4)),
        scratch_shapes=[
            pltpu.VMEM((320, wide), BF16),
            pltpu.VMEM((320, wide), BF16),
            pltpu.VMEM((192, wide), F32),
            pltpu.SemaphoreType.DMA((blocks,)),
            pltpu.VMEM(frame_shift.shape, I32),
            pltpu.VMEM(kernel_ids.shape, I32),
            pltpu.VMEM(groups.shape, I32),
            pltpu.SMEM((5, kernels.shape[0], 5), F32),
            pltpu.SMEM(gains.shape, F32),
            pltpu.SemaphoreType.DMA((5,)),
        ],
        compiler_params=params(),
        name="outer",
    )(
        *(
            pltpu.with_memory_space_constraint(x, pltpu.HBM)
            for x in (frame_shift, kernel_ids, groups, kernels.transpose(1, 0, 2), gains, observed.reshape(-1, wide))
        )
    )
    other = lax.ppermute(send, "frame", [(0, 1), (1, 0)])

    def inner_scratch(rows):
        return [pltpu.VMEM(((rows + 2) * 64, wide), BF16), pltpu.VMEM((rows * 32, wide), F32)]

    own_early, sent = pl.pallas_call(
        functools.partial(early_kernel, 2),
        out_shape=(shape((early * 16, ext), F32),) * 2,
        in_specs=vmem(2),
        out_specs=tuple(vmem(2)),
        scratch_shapes=inner_scratch(early),
        compiler_params=params(),
        cost_estimate=cost(1),
        name="early",
    )(landed, weights)
    first, second = pl.pallas_call(
        border_kernel,
        out_shape=(shape((40, ext), F32),) * 2,
        in_specs=vmem(2),
        out_specs=tuple(vmem(2)),
        compiler_params=params(),
        name="border",
    )(own, other)
    own_late, send2 = pl.pallas_call(
        functools.partial(late_kernel, 2 + early),
        out_shape=(shape((late * 16, ext), F32), shape((inner * 16, ext), F32)),
        in_specs=vmem(4),
        out_specs=tuple(vmem(2)),
        scratch_shapes=inner_scratch(late),
        compiler_params=params(),
        cost_estimate=cost(1),
        name="late",
    )(landed, weights, sent, first)
    pairs = [(i, i ^ 1) for i in range(tiles) if i ^ 1 < tiles]
    odd_pairs = [p for i in range(1, tiles - 1, 2) for p in ((i, i + 1), (i + 1, i))]
    second = lax.ppermute(second, "tile", odd_pairs)
    first = lax.ppermute(first, "tile", pairs)
    other2 = lax.ppermute(send2, "frame", [(0, 1), (1, 0)])

    base, once, twice, stack1, stack2, tables, spreading, partial = pl.pallas_call(
        interior_kernel,
        out_shape=(
            shape(((inner + 2) * 16, ext), F32),
            shape((inner * 16, ext), F32),
            shape(((inner - 2) * 16, half), F32),
            shape(((inner + 2) * 64, ext), BF16),
            shape((inner * 64, ext), BF16),
            shape((5 * 128, 256), BF16),
            shape((4 * LANES, 4 * LANES), BF16),
            shape((32, LANES), F32),
        ),
        in_specs=vmem(5),
        out_specs=tuple(vmem(8)),
        compiler_params=params(),
        cost_estimate=cost(2),
        name="interior",
    )(own, other, own_early, own_late, other2)
    peers = tiles * spread
    base_rim, once_rim, twice_rim, sums = pl.pallas_call(
        rim_kernel,
        out_shape=(
            shape((32, half), F32),
            shape((64, half), F32),
            shape((96, half), F32),
            shape((peers, 8, LANES), F32),
        ),
        in_specs=vmem(10),
        out_specs=tuple(vmem(4)),
        scratch_shapes=[pltpu.VMEM((320, ext), BF16)] * 4,
        compiler_params=params(),
        name="rim",
    )(own, other, first, second, base, once, stack1, stack2, tables, partial)
    sums = lax.all_to_all(sums, ("tile", "frame"), 0, 0)

    solution, residual = pl.pallas_call(
        update_kernel,
        out_shape=(shape((count * 4, 4 * half), F32),) * 2,
        in_specs=vmem(8),
        out_specs=(far,) * 2,
        scratch_shapes=[pltpu.VMEM((count * 4, 4 * half), F32)] * 2
        + [pltpu.SemaphoreType.DMA((2, half // LANES))],
        compiler_params=params(),
        name="update",
    )(base, once, twice, base_rim, once_rim, twice_rim, spreading, sums)
    return solution, residual


def solution(mesh):
    return jax.shard_map(
        per_device,
        mesh=mesh,
        in_specs=(
            P("frame", ("scene", "tile"), None),
            P("scene", "frame"),
            P("scene", "frame"),
            P("scene", "frame"),
            P(),
            P(),
        ),
        out_specs=(P(("scene", "tile"), "frame"), P(("scene", "tile"), "frame")),
        check_vma=False,
    )
```

```python
import functools

import jax
import jax.numpy as jnp
from jax import lax
from jax.experimental import pallas as pl
from jax.experimental.pallas import tpu as pltpu
from jax.sharding import PartitionSpec as P

DAMPING = 0.3
LANES = 128
HIGHEST = lax.Precision.HIGHEST
NT = (((1,), (1,)), ((), ()))
F32, BF16, I32 = jnp.float32, jnp.bfloat16, jnp.int32


def split(x):
    high = x.astype(BF16)
    return high, (x - high.astype(F32)).astype(BF16)


def paired(table):
    high, low = split(table)
    second = (lax.broadcasted_iota(I32, table.shape, 1) >> 5) & 1
    return jnp.concatenate([high, jnp.where(second == 0, low.astype(F32), 0.0).astype(BF16)], axis=0)


def row_phase(shape):
    return lax.broadcasted_iota(I32, shape, 0) & 3


def tap_table(shift, ids, members, kernels, gains):
    frames = shift.shape[1]
    copies = LANES // frames

    def tiled(x):
        return jnp.concatenate([x] * copies, axis=1)

    shape = (32, LANES)
    place = lax.broadcasted_iota(I32, shape, 0)
    lane = lax.broadcasted_iota(I32, shape, 1)
    group = place >> 3
    first = jnp.where(group == 0, 2, jnp.where(group == 1, 4, jnp.where(group == 2, 0, 6)))
    col = first + ((place >> 2) & 1)
    row = 2 + 4 * ((lane >> 5) - 1) + (place & 3)
    up = row - tiled(shift[0:1, :])
    along = col - tiled(shift[1:2, :])
    kind = tiled(ids[...])
    member = tiled(members[...])
    inside = (row >= 0) & (row < 8) & (up >= 0) & (up < 5) & (along >= 0) & (along < 5)
    count = kernels.shape[1]
    code = jnp.where(inside, kind * 25 + up * 5 + along, -1)
    total = jnp.zeros(shape, F32)
    for n in range(count):
        for a in range(5):
            for b in range(5):
                total = jnp.where(code == n * 25 + a * 5 + b, kernels[a, n, b], total)
    scale = jnp.zeros((1, LANES), F32)
    for g in range(gains.shape[0]):
        scale = jnp.where(member == g, gains[g], scale)
    return total * scale


def put_halves(own, send, at, value, me):
    half = value.shape[1] // 2
    near = lax.broadcasted_iota(I32, (8, LANES), 1) < 64
    own[at : at + 8, :half] = value[:, :half]
    send[at : at + 8, :half] = value[:, half:]
    after = jnp.where(near, value[:, half : half + LANES], 0.0)
    before = jnp.where(near, 0.0, value[:, 2 * half - LANES :])
    own[at : at + 8, half:] = jnp.where(me == 0, after, before)
    before = jnp.where(near, 0.0, value[:, half - LANES : half])
    after = jnp.where(near, value[:, 0:LANES], 0.0)
    send[at : at + 8, half:] = jnp.where(me == 0, before, after)


def moved_image(t, me):
    wide = t.shape[1]
    half = wide // 2
    lane = lax.broadcasted_iota(I32, (8, wide), 1)
    low = t[0:8] + jnp.where(lane == jnp.where(me == 0, 0, half), 0.0, pltpu.roll(t[24:32], 1, 1))
    last = jnp.where(me == 0, wide - 1, half - 1)
    high = t[8:16] + jnp.where(lane == last, 0.0, pltpu.roll(t[16:24], wide - 1, 1))
    return low, high


def two_rows(weights, columns):
    both = jnp.dot(weights, columns, preferred_element_type=F32)
    return both[0:32] + both[32:64], both[64:96] + both[96:128]


def one_row(weights, columns):
    both = jnp.dot(weights[0:64, 0:192], columns, preferred_element_type=F32)
    return both[0:32] + both[32:64]


def keep(stack, at, cols, high, low):
    stack[at * 64 : at * 64 + 32, cols] = high
    stack[at * 64 + 32 : at * 64 + 64, cols] = low


def adjoint_weights(table):
    source = lax.broadcasted_iota(I32, (LANES, 512), 0)
    target = lax.broadcasted_iota(I32, (LANES, 512), 1)
    place = (target & 255) - 64 * (target >> 8)
    pick = (source == (2 - (place >> 6)) * 32 + (place & 31)) & (place >= 0) & (place < 192)
    both = jnp.dot(table, pick.astype(F32), precision=HIGHEST, preferred_element_type=F32)
    return jnp.concatenate([paired(both[:, 0:256]), paired(both[:, 256:512])], axis=0)


def outer_kernel(
    far_shift, far_ids, far_members, far_kernels, far_gains, obs, mine, theirs, own, send, weights,
    top, bottom, mixed, sems, shift, ids, members, kernels, gains, small_sems,
):
    wide = obs.shape[1]
    frames = shift.shape[1]
    count = obs.shape[0] // frames
    blocks = wide // LANES
    me = lax.axis_index("frame")

    half = wide // 2

    def load(c):
        if c < blocks:
            start = jnp.where(me == 0, 0, half) if c < blocks // 2 else jnp.where(me == 0, half, 0)
            start = start + (c % (blocks // 2)) * LANES
            target = mine if c < blocks // 2 else theirs
            at = c % (blocks // 2)
        else:
            start = jnp.where(me == c - blocks, half, half - LANES)
            target = mine if c == blocks else theirs
            at = blocks // 2
        source = obs.at[:, pl.ds(pl.multiple_of(start, LANES), LANES)]
        return pltpu.make_async_copy(source, target.at[at], sems.at[c])

    small = [
        pltpu.make_async_copy(far, near, small_sems.at[i])
        for i, (far, near) in enumerate(
            [(far_kernels, kernels), (far_gains, gains), (far_shift, shift), (far_ids, ids), (far_members, members)]
        )
    ]
    for copy in small:
        copy.start()
    for c in range(blocks + 2):
        load(c).start()
    nothing = jnp.zeros((128, wide), BF16)
    top[0:128, :] = nothing
    bottom[192:320, :] = nothing
    for copy in small:
        copy.wait()
    table = tap_table(shift, ids, members, kernels, gains)
    for r in range(4):
        own[80:88, r * LANES : (r + 1) * LANES] = table[8 * r : 8 * r + 8]
        send[80:88, r * LANES : (r + 1) * LANES] = table[8 * r : 8 * r + 8]
    rest = own.shape[1] - 4 * LANES
    if rest > 0:
        own[80:88, 4 * LANES :] = jnp.zeros((8, rest), F32)
        send[80:88, 4 * LANES :] = jnp.zeros((8, rest), F32)
    left = adjoint_weights(table)
    weights[...] = left

    for c in range(0, blocks, 2):
        load(c).wait()
        load(c + 1).wait()
        for d in range(2):
            cols = slice((c + d) * LANES, (c + d + 1) * LANES)
            landed, at = (mine, c + d) if c < blocks // 2 else (theirs, c + d - blocks // 2)
            for r in range(3):
                keep(top, 2 + r, cols, *split(landed[at, pl.ds(r, frames, stride=count), :]))
                keep(bottom, r, cols, *split(landed[at, pl.ds(count - 3 + r, frames, stride=count), :]))
        cols = slice(c * LANES, (c + 2) * LANES)
        a, b = two_rows(left, top[0:256, cols])
        mixed[0:32, cols] = a
        mixed[32:64, cols] = b
        mixed[64:96, cols] = one_row(left, top[128:320, cols])
        mixed[96:128, cols] = one_row(left, bottom[0:192, cols])
        a, b = two_rows(left, bottom[64:320, cols])
        mixed[128:160, cols] = a
        mixed[160:192, cols] = b

    above, below = moved_image(mixed[0:32, :], me), moved_image(mixed[160:192, :], me)
    for g in range(2):
        put_halves(own, send, 8 * g, above[g] + below[g], me)
    for r in range(1, 5):
        image = moved_image(mixed[r * 32 : r * 32 + 32, :], me)
        for g in range(2):
            put_halves(own, send, r * 16 + 8 * g, image[g], me)
    load(blocks).wait()
    load(blocks + 1).wait()


def inner_sums(landed, left, stack, mixed):
    blocks = landed.shape[0]
    rows = mixed.shape[0] // 32
    count = rows + 4
    frames = landed.shape[1] // count
    for c in range(0, blocks, 2):
        pair = min(2, blocks - c)
        for d in range(pair):
            cols = slice((c + d) * LANES, (c + d + 1) * LANES)
            for r in range(rows + 2):
                keep(stack, r, cols, *split(landed[c + d, pl.ds(1 + r, frames, stride=count), :]))
        cols = slice(c * LANES, (c + pair) * LANES)
        for r in range(0, rows, 2):
            a, b = two_rows(left, stack[r * 64 : r * 64 + 256, cols])
            mixed[r * 32 : r * 32 + 32, cols] = a
            mixed[r * 32 + 32 : r * 32 + 64, cols] = b


def early_kernel(landed, weights, mixed, stack):
    inner_sums(landed, weights[...], stack, mixed)


def border_kernel(own, other, passed, first, second, onward):
    even = lax.rem(lax.axis_index("tile"), 2) == 0
    edge = own[0:16] + other[0:16]
    phase = row_phase((8, own.shape[1]))
    above = jnp.where(phase >= 2, edge[0:8], pltpu.roll(edge[8:16], 6, 0))
    below = jnp.where(phase < 2, edge[0:8], pltpu.roll(edge[8:16], 2, 0))
    top = own[16:48] + other[16:48]
    bottom = own[48:80] + other[48:80]
    first[0:32] = jnp.where(even, bottom, top)
    first[32:40] = jnp.where(even, below, above)
    second[0:32] = jnp.where(even, top, bottom)
    second[32:40] = jnp.where(even, above, below)


def halo_mask():
    lane = lax.broadcasted_iota(I32, (8, LANES), 1)
    here = lax.axis_index("frame") == 0
    return jnp.where(here, jnp.where(lane < 64, 1.0, 0.0), jnp.where(lane < 64, 0.0, 1.0)).astype(F32)


def expand(stack, at, value):
    ext = value.shape[1]
    low, high = value[0:8], value[8:16]
    groups = jnp.concatenate([low, high, pltpu.roll(high, 1, 1), pltpu.roll(low, ext - 1, 1)], axis=0)
    keep(stack, at, slice(None), *split(groups))


def assembled(t, near, field=None):
    ext = t.shape[1]
    half = ext - LANES

    def masked(x):
        return jnp.concatenate([x[:, :half], x[:, half:] * near], axis=1)

    low = t[0:8] + pltpu.roll(masked(t[24:32]), 1, 1)
    high = t[8:16] + pltpu.roll(masked(t[16:24]), ext - 1, 1)
    if field is not None:
        low, high = low + DAMPING * field[0:8], high + DAMPING * field[8:16]
    return jnp.concatenate([masked(low), masked(high)], axis=0)


def finished(t, field, near):
    return assembled(t, near, field)


def folded(a, b):
    total = None
    for c in range(0, a.shape[1] - LANES + 1, LANES):
        for g in (0, 8):
            term = a[g : g + 8, c : c + LANES] * b[g : g + 8, c : c + LANES]
            total = term if total is None else total + term
    return total


def interior_kernel(
    own1, other1, ours, landed, base, once, twice, stack1, stack2, tables, spread, sums, stack, mixed
):
    ext = own1.shape[1]
    half = ext - LANES
    inner = ours.shape[0] // 32
    tile, tiles = lax.axis_index("tile"), lax.axis_size("tile")
    no_up = jnp.where(tile > 0, 0.0, 1.0).astype(F32)
    no_down = jnp.where(tile < tiles - 1, 0.0, 1.0).astype(F32)

    taps = [
        jnp.concatenate([ref[80:88, r * LANES : (r + 1) * LANES] for r in range(4)], axis=0) for ref in (own1, other1)
    ]
    inner_sums(landed, adjoint_weights(taps[1]), stack, mixed)
    block = lax.broadcasted_iota(I32, (32, LANES), 1) >> 5
    left = jnp.concatenate(
        [jnp.concatenate([t, jnp.where(block == 2, t, 0.0), jnp.where(block == 0, t, 0.0)], axis=0) for t in taps],
        axis=1,
    )
    empty = jnp.zeros((64, LANES), F32)
    right = []
    for t in taps:
        e, a = pltpu.roll(t, 32, 1), pltpu.roll(t, LANES - 32, 1)
        right.append(jnp.concatenate([e, e, t, t, a, a, empty, empty, e, e, t, t, a, a], axis=0))
    product = lax.dot_general(
        left, jnp.concatenate(right, axis=1), NT, precision=HIGHEST, preferred_element_type=F32
    )
    lane = lax.broadcasted_iota(I32, (32, 512), 1)
    middle = ((lane >> 6) == 1) | ((lane >> 6) == 6)
    full = product[0:32]
    at_top = full - no_up * jnp.where(middle, product[32:64], 0.0)
    at_bottom = full - no_down * jnp.where(middle, product[64:96], 0.0)
    plain_a, plain_b = paired(full[:, 0:256]), paired(full[:, 256:512])
    top_a, top_b = paired(at_top[:, 0:256]), paired(at_top[:, 256:512])
    bottom_a, bottom_b = paired(at_bottom[:, 0:256]), paired(at_bottom[:, 256:512])
    pairs = [(plain_a, plain_b), (plain_a, top_b), (top_a, plain_b), (plain_a, bottom_b), (bottom_a, plain_b)]
    for i, (a, b) in enumerate(pairs):
        tables[i * 128 : i * 128 + 64] = a
        tables[i * 128 + 64 : i * 128 + 128] = b
    plain = jnp.concatenate([plain_a, plain_b], axis=0)

    source = lax.broadcasted_iota(I32, spread.shape, 0)
    target = lax.broadcasted_iota(I32, spread.shape, 1)
    hit = target == 4 * (source & (LANES - 1)) + (source >> 7)
    spread[...] = jnp.where(hit, 1.0, 0.0).astype(BF16)
    near = halo_mask()
    totals = [jnp.zeros((8, LANES), F32) for _ in range(4)]

    for r in range(inner + 2):
        if r == 0:
            value = own1[32:48] + other1[32:48]
        elif r == inner + 1:
            value = own1[48:64] + other1[48:64]
        else:
            at = (r - 1) * 32
            value = assembled(ours[at : at + 32] + mixed[at : at + 32], near)
        base[r * 16 : r * 16 + 16] = value
        totals[0] += folded(value[:, :half], value[:, :half])
        expand(stack1, r, value)
    for r in range(0, inner, 2):
        images = two_rows(plain, stack1[r * 64 : r * 64 + 256])
        for d in range(2):
            field = base[(r + d + 1) * 16 : (r + d + 2) * 16]
            value = finished(images[d], field, near)
            once[(r + d) * 16 : (r + d + 1) * 16] = value
            totals[1] += folded(field[:, :half], value[:, :half])
            totals[2] += folded(value[:, :half], value[:, :half])
            expand(stack2, r + d, value)
    for r in range(0, inner - 2, 2):
        images = two_rows(plain, stack2[r * 64 : r * 64 + 256])
        for d in range(2):
            field = once[(r + d + 1) * 16 : (r + d + 2) * 16]
            value = finished(images[d], field, near)[:, :half]
            twice[(r + d) * 16 : (r + d + 1) * 16] = value
            totals[3] += folded(field[:, :half], value)
    for i in range(4):
        sums[i * 8 : i * 8 + 8] = totals[i]


def rim_kernel(
    own, other, first, second, base, once, stack1, stack2, tables, partial,
    base_rim, once_rim, twice_rim, sums, above1, below1, above2, below2,
):
    ext = own.shape[1]
    half = ext - LANES
    inner = base.shape[0] // 16
    tile, tiles = lax.axis_index("tile"), lax.axis_size("tile")
    even = lax.rem(tile, 2) == 0
    has_up = jnp.where(tile > 0, 1.0, 0.0).astype(F32)
    has_down = jnp.where(tile < tiles - 1, 1.0, 0.0).astype(F32)
    near = halo_mask()
    phase = row_phase((16, ext))
    totals = [partial[i * 8 : i * 8 + 8] for i in range(4)]
    plain = tables[0:128]

    above1[192:320] = stack1[0:128]
    below1[0:128] = stack1[(inner - 2) * 64 : inner * 64]
    above2[192:320] = stack2[0:128]
    below2[0:128] = stack2[(inner - 4) * 64 : (inner - 2) * 64]

    edge = own[0:16] + other[0:16]
    up = jnp.where(even, second[...], first[...])
    down = jnp.where(even, first[...], second[...])
    rows = {-2: up[0:16]}
    rows[-1] = up[16:32] + has_up * jnp.where(phase >= 2, edge, 0.0)
    e = up[32:40]
    spare = jnp.where(phase < 2, jnp.concatenate([e, pltpu.roll(e, 6, 0)], axis=0), 0.0)
    rows[0] = own[16:32] + other[16:32] + spare
    rows[1] = base[0:16]
    e = down[32:40]
    spare = jnp.where(phase >= 2, jnp.concatenate([e, pltpu.roll(e, 2, 0)], axis=0), 0.0)
    low_rows = {0: base[(inner - 1) * 16 : inner * 16]}
    low_rows[1] = own[64:80] + other[64:80] + spare
    low_rows[2] = down[0:16] + has_down * jnp.where(phase < 2, edge, 0.0)
    low_rows[3] = down[16:32]
    for i in range(3):
        expand(above1, i, rows[i - 2])
        expand(below1, i + 2, low_rows[i + 1])
    base_rim[0:16] = rows[0][:, :half]
    base_rim[16:32] = low_rows[1][:, :half]
    totals[0] += folded(rows[0][:, :half], rows[0][:, :half])
    totals[0] += folded(low_rows[1][:, :half], low_rows[1][:, :half])

    a, b = two_rows(tables[128:256], above1[0:256])
    c = one_row(plain, above1[128:320])
    high = [finished(a, rows[-1], near) * has_up, finished(b, rows[0], near), finished(c, rows[1], near)]
    a = one_row(plain, below1[0:192])
    b, c = two_rows(tables[512:640], below1[64:320])
    deep = [
        finished(a, low_rows[0], near),
        finished(b, low_rows[1], near),
        finished(c, low_rows[2], near) * has_down,
    ]
    for i in range(3):
        expand(above2, i, high[i])
        expand(below2, i + 2, deep[i])
    pieces = [(rows[0], high[1]), (rows[1], high[2]), (low_rows[0], deep[0]), (low_rows[1], deep[1])]
    for i, (field, value) in enumerate(pieces):
        once_rim[i * 16 : i * 16 + 16] = value[:, :half]
        totals[1] += folded(field[:, :half], value[:, :half])
        totals[2] += folded(value[:, :half], value[:, :half])

    a, b = two_rows(tables[256:384], above2[0:256])
    c = one_row(plain, above2[128:320])
    d = one_row(plain, below2[0:192])
    e, f = two_rows(tables[384:512], below2[64:320])
    fields = [high[1], high[2], once[0:16], once[(inner - 3) * 16 : (inner - 2) * 16], deep[0], deep[1]]
    for i, (t, field) in enumerate(zip([a, b, c, d, e, f], fields)):
        value = finished(t, field, near)[:, :half]
        twice_rim[i * 16 : i * 16 + 16] = value
        totals[3] += folded(field[:, :half], value)
    lines = jnp.concatenate([jnp.sum(t, axis=0, keepdims=True) for t in totals], axis=0)
    lines = jnp.concatenate([lines, jnp.zeros((4, LANES), F32)], axis=0)
    for p in range(sums.shape[0]):
        sums[p] = lines


def update_kernel(base, once, twice, base_rim, once_rim, twice_rim, spread, sums, solution, residual, near_x, near_r, sems):
    lanes = jnp.sum(sums[...], axis=0)

    def total(at):
        return jnp.sum(lanes[at : at + 1], axis=1, keepdims=True)

    bb, bm, mm, mmm = [total(at) for at in range(4)]
    alpha = bb / bm
    norm = alpha * alpha * mm - 2.0 * alpha * bm + bb
    beta = norm / bb
    grow = 1.0 + beta
    product = grow * grow * bm - 2.0 * grow * alpha * mm + alpha * alpha * mmm
    step = norm / product
    count = base.shape[0] // 16 + 2
    half = base_rim.shape[1]
    side = lax.broadcasted_iota(I32, (count // 2, 8, LANES), 1) < 4

    def arranged(x):
        x = x.reshape(count // 2, 4, 8, LANES)
        pieces = []
        for g in range(2):
            a, b = x[:, g], x[:, g + 2]
            pieces.append(jnp.where(side, a, pltpu.roll(b, 4, 1)).reshape(4 * count, LANES))
            pieces.append(jnp.where(side, pltpu.roll(a, 4, 1), b).reshape(4 * count, LANES))
        return split(jnp.concatenate(pieces, axis=1))

    def stores(c):
        wide = pl.ds(4 * c * LANES, 4 * LANES)
        return [
            pltpu.make_async_copy(near.at[:, wide], far.at[:, wide], sems.at[i, c])
            for i, (near, far) in enumerate([(near_x, solution), (near_r, residual)])
        ]

    def rows_of(middle, rim, cols):
        n = rim.shape[0] // 2
        return jnp.concatenate([rim[0:n, cols], middle[:, cols], rim[n : 2 * n, cols]], axis=0)

    for c in range(half // LANES):
        cols = slice(c * LANES, (c + 1) * LANES)
        b, m, mm_ = rows_of(base, base_rim, cols), rows_of(once, once_rim, cols), rows_of(twice, twice_rim, cols)
        x = (alpha + step * grow) * b - (step * alpha) * m
        r = (b - alpha * m) - step * (grow * m - alpha * mm_)
        xh, xl = arranged(x)
        rh, rl = arranged(r)
        out = jnp.dot(jnp.concatenate([xh, xl, rh, rl], axis=0), spread[...], preferred_element_type=F32)
        n = 4 * count
        wide = slice(4 * c * LANES, 4 * (c + 1) * LANES)
        near_x[:, wide] = out[0:n] + out[n : 2 * n]
        near_r[:, wide] = out[2 * n : 3 * n] + out[3 * n : 4 * n]
        for copy in stores(c):
            copy.start()
    for c in range(half // LANES):
        for copy in stores(c):
            copy.wait()


def params(mebibytes=24):
    return pltpu.CompilerParams(vmem_limit_bytes=mebibytes * 1024 * 1024)


def cost(units):
    return pl.CostEstimate(flops=int(units * 10**9), bytes_accessed=int(units * 2**22), transcendentals=0)


def vmem(n):
    return [pl.BlockSpec(memory_space=pltpu.VMEM)] * n


def per_device(observed, frame_shift, kernel_ids, groups, kernels, gains):
    frames, count, wide = observed.shape
    half = wide // 2
    ext = half + LANES
    blocks = wide // LANES
    tiles, spread = lax.axis_size("tile"), lax.axis_size("frame")
    far = pl.BlockSpec(memory_space=pltpu.HBM)
    shape = jax.ShapeDtypeStruct
    inner = count - 4

    mine, theirs, own, send, weights = pl.pallas_call(
        outer_kernel,
        out_shape=(
            shape((blocks // 2 + 1, frames * count, LANES), F32),
            shape((blocks // 2 + 1, frames * count, LANES), F32),
            shape((88, ext), F32),
            shape((88, ext), F32),
            shape((128, 256), BF16),
        ),
        in_specs=[far] * 6,
        out_specs=tuple(vmem(5)),
        scratch_shapes=[
            pltpu.VMEM((320, wide), BF16),
            pltpu.VMEM((320, wide), BF16),
            pltpu.VMEM((192, wide), F32),
            pltpu.SemaphoreType.DMA((blocks + 2,)),
            pltpu.VMEM(frame_shift.shape, I32),
            pltpu.VMEM(kernel_ids.shape, I32),
            pltpu.VMEM(groups.shape, I32),
            pltpu.SMEM((5, kernels.shape[0], 5), F32),
            pltpu.SMEM(gains.shape, F32),
            pltpu.SemaphoreType.DMA((5,)),
        ],
        compiler_params=params(),
        name="outer",
    )(
        *(
            pltpu.with_memory_space_constraint(x, pltpu.HBM)
            for x in (frame_shift, kernel_ids, groups, kernels.transpose(1, 0, 2), gains, observed.reshape(-1, wide))
        )
    )
    other = lax.ppermute(send, "frame", [(0, 1), (1, 0)])

    ours = pl.pallas_call(
        early_kernel,
        out_shape=shape((inner * 32, ext), F32),
        in_specs=vmem(2),
        out_specs=vmem(1)[0],
        scratch_shapes=[pltpu.VMEM(((inner + 2) * 64, ext), BF16)],
        compiler_params=params(),
        cost_estimate=cost(1),
        name="early",
    )(mine, weights)
    first, second, theirs = pl.pallas_call(
        border_kernel,
        out_shape=(shape((40, ext), F32), shape((40, ext), F32), shape(theirs.shape, F32)),
        in_specs=vmem(3),
        out_specs=tuple(vmem(3)),
        input_output_aliases={2: 2},
        compiler_params=params(),
        name="border",
    )(own, other, theirs)
    theirs = lax.ppermute(theirs, "frame", [(0, 1), (1, 0)])
    pairs = [(i, i ^ 1) for i in range(tiles) if i ^ 1 < tiles]
    odd_pairs = [p for i in range(1, tiles - 1, 2) for p in ((i, i + 1), (i + 1, i))]
    second = lax.ppermute(second, "tile", odd_pairs)
    first = lax.ppermute(first, "tile", pairs)

    base, once, twice, stack1, stack2, tables, spreading, partial = pl.pallas_call(
        interior_kernel,
        out_shape=(
            shape(((inner + 2) * 16, ext), F32),
            shape((inner * 16, ext), F32),
            shape(((inner - 2) * 16, half), F32),
            shape(((inner + 2) * 64, ext), BF16),
            shape((inner * 64, ext), BF16),
            shape((5 * 128, 256), BF16),
            shape((4 * LANES, 4 * LANES), BF16),
            shape((32, LANES), F32),
        ),
        in_specs=vmem(4),
        out_specs=tuple(vmem(8)),
        scratch_shapes=[pltpu.VMEM(((inner + 2) * 64, ext), BF16), pltpu.VMEM((inner * 32, ext), F32)],
        compiler_params=params(),
        cost_estimate=cost(0.01),
        name="interior",
    )(own, other, ours, theirs)
    peers = tiles * spread
    base_rim, once_rim, twice_rim, sums = pl.pallas_call(
        rim_kernel,
        out_shape=(
            shape((32, half), F32),
            shape((64, half), F32),
            shape((96, half), F32),
            shape((peers, 8, LANES), F32),
        ),
        in_specs=vmem(10),
        out_specs=tuple(vmem(4)),
        scratch_shapes=[pltpu.VMEM((320, ext), BF16)] * 4,
        compiler_params=params(),
        name="rim",
    )(own, other, first, second, base, once, stack1, stack2, tables, partial)
    sums = lax.all_to_all(sums, ("tile", "frame"), 0, 0)

    solution, residual = pl.pallas_call(
        update_kernel,
        out_shape=(shape((count * 4, 4 * half), F32),) * 2,
        in_specs=vmem(8),
        out_specs=(far,) * 2,
        scratch_shapes=[pltpu.VMEM((count * 4, 4 * half), F32)] * 2
        + [pltpu.SemaphoreType.DMA((2, half // LANES))],
        compiler_params=params(),
        name="update",
    )(base, once, twice, base_rim, once_rim, twice_rim, spreading, sums)
    return solution, residual


def solution(mesh):
    return jax.shard_map(
        per_device,
        mesh=mesh,
        in_specs=(
            P("frame", ("scene", "tile"), None),
            P("scene", "frame"),
            P("scene", "frame"),
            P("scene", "frame"),
            P(),
            P(),
        ),
        out_specs=(P(("scene", "tile"), "frame"), P(("scene", "tile"), "frame")),
        check_vma=False,
    )
```

```python
import functools

import jax
import jax.numpy as jnp
from jax import lax
from jax.experimental import pallas as pl
from jax.experimental.pallas import tpu as pltpu
from jax.sharding import PartitionSpec as P

DAMPING = 0.3
LANES = 128
HIGHEST = lax.Precision.HIGHEST
NT = (((1,), (1,)), ((), ()))
F32, BF16, I32 = jnp.float32, jnp.bfloat16, jnp.int32


def split(x):
    high = x.astype(BF16)
    return high, (x - high.astype(F32)).astype(BF16)


def paired(table):
    high, low = split(table)
    second = (lax.broadcasted_iota(I32, table.shape, 1) >> 5) & 1
    return jnp.concatenate([high, jnp.where(second == 0, low.astype(F32), 0.0).astype(BF16)], axis=0)


def row_phase(shape):
    return lax.broadcasted_iota(I32, shape, 0) & 3


def tap_table(shift, ids, members, kernels, gains):
    frames = shift.shape[1]
    copies = LANES // frames

    def tiled(x):
        return jnp.concatenate([x] * copies, axis=1)

    shape = (32, LANES)
    place = lax.broadcasted_iota(I32, shape, 0)
    lane = lax.broadcasted_iota(I32, shape, 1)
    group = place >> 3
    first = jnp.where(group == 0, 2, jnp.where(group == 1, 4, jnp.where(group == 2, 0, 6)))
    col = first + ((place >> 2) & 1)
    row = 2 + 4 * ((lane >> 5) - 1) + (place & 3)
    up = row - tiled(shift[0:1, :])
    along = col - tiled(shift[1:2, :])
    kind = tiled(ids[...])
    member = tiled(members[...])
    inside = (row >= 0) & (row < 8) & (up >= 0) & (up < 5) & (along >= 0) & (along < 5)
    count = kernels.shape[1]
    code = jnp.where(inside, kind * 25 + up * 5 + along, -1)
    total = jnp.zeros(shape, F32)
    for n in range(count):
        for a in range(5):
            for b in range(5):
                total = jnp.where(code == n * 25 + a * 5 + b, kernels[a, n, b], total)
    scale = jnp.zeros((1, LANES), F32)
    for g in range(gains.shape[0]):
        scale = jnp.where(member == g, gains[g], scale)
    return total * scale


def put_halves(own, send, at, value, me):
    half = value.shape[1] // 2
    near = lax.broadcasted_iota(I32, (8, LANES), 1) < 64
    own[at : at + 8, :half] = value[:, :half]
    send[at : at + 8, :half] = value[:, half:]
    after = jnp.where(near, value[:, half : half + LANES], 0.0)
    before = jnp.where(near, 0.0, value[:, 2 * half - LANES :])
    own[at : at + 8, half:] = jnp.where(me == 0, after, before)
    before = jnp.where(near, 0.0, value[:, half - LANES : half])
    after = jnp.where(near, value[:, 0:LANES], 0.0)
    send[at : at + 8, half:] = jnp.where(me == 0, before, after)


def moved_image(t, me):
    wide = t.shape[1]
    half = wide // 2
    lane = lax.broadcasted_iota(I32, (8, wide), 1)
    low = t[0:8] + jnp.where(lane == jnp.where(me == 0, 0, half), 0.0, pltpu.roll(t[24:32], 1, 1))
    last = jnp.where(me == 0, wide - 1, half - 1)
    high = t[8:16] + jnp.where(lane == last, 0.0, pltpu.roll(t[16:24], wide - 1, 1))
    return low, high


def two_rows(weights, columns):
    both = jnp.dot(weights, columns, preferred_element_type=F32)
    return both[0:32] + both[32:64], both[64:96] + both[96:128]


def one_row(weights, columns):
    both = jnp.dot(weights[0:64, 0:192], columns, preferred_element_type=F32)
    return both[0:32] + both[32:64]


def keep(stack, at, cols, high, low):
    stack[at * 64 : at * 64 + 32, cols] = high
    stack[at * 64 + 32 : at * 64 + 64, cols] = low


def adjoint_weights(table):
    source = lax.broadcasted_iota(I32, (LANES, 512), 0)
    target = lax.broadcasted_iota(I32, (LANES, 512), 1)
    place = (target & 255) - 64 * (target >> 8)
    pick = (source == (2 - (place >> 6)) * 32 + (place & 31)) & (place >= 0) & (place < 192)
    both = jnp.dot(table, pick.astype(F32), precision=HIGHEST, preferred_element_type=F32)
    return jnp.concatenate([paired(both[:, 0:256]), paired(both[:, 256:512])], axis=0)


def outer_kernel(
    far_shift, far_ids, far_members, far_kernels, far_gains, obs, mine, theirs, own, send, weights,
    top, bottom, mixed, sems, shift, ids, members, kernels, gains, small_sems,
):
    wide = obs.shape[1]
    frames = shift.shape[1]
    count = obs.shape[0] // frames
    blocks = wide // LANES
    me = lax.axis_index("frame")

    half = wide // 2

    def load(c):
        start = jnp.where(me == 0, 0, half) if c < blocks // 2 else jnp.where(me == 0, half, 0)
        start = start + (c % (blocks // 2)) * LANES
        target = mine if c < blocks // 2 else theirs
        at = c % (blocks // 2)
        source = obs.at[:, pl.ds(pl.multiple_of(start, LANES), LANES)]
        return pltpu.make_async_copy(source, target.at[at], sems.at[c])

    def halo(from_theirs):
        last = blocks // 2 - 1
        source, target = (theirs, mine) if from_theirs else (mine, theirs)
        at = jnp.where(me == 0, 0, last) if from_theirs else jnp.where(me == 0, last, 0)
        return pltpu.make_async_copy(
            source.at[at], target.at[blocks // 2], sems.at[blocks + 1 if from_theirs else blocks]
        )

    ahead = min(8, blocks)
    small = [
        pltpu.make_async_copy(far, near, small_sems.at[i])
        for i, (far, near) in enumerate(
            [(far_kernels, kernels), (far_gains, gains), (far_shift, shift), (far_ids, ids), (far_members, members)]
        )
    ]
    for copy in small:
        copy.start()
    for c in range(ahead):
        load(c).start()
    nothing = jnp.zeros((128, wide), BF16)
    top[0:128, :] = nothing
    bottom[192:320, :] = nothing
    for copy in small:
        copy.wait()
    table = tap_table(shift, ids, members, kernels, gains)
    for r in range(4):
        own[80:88, r * LANES : (r + 1) * LANES] = table[8 * r : 8 * r + 8]
        send[80:88, r * LANES : (r + 1) * LANES] = table[8 * r : 8 * r + 8]
    rest = own.shape[1] - 4 * LANES
    if rest > 0:
        own[80:88, 4 * LANES :] = jnp.zeros((8, rest), F32)
        send[80:88, 4 * LANES :] = jnp.zeros((8, rest), F32)
    left = adjoint_weights(table)
    weights[...] = left

    cuts = [0, blocks // 2, blocks]
    for c, end in zip(cuts, cuts[1:]):
        step = end - c
        for d in range(step):
            load(c + d).wait()
            if c + d + ahead < blocks:
                load(c + d + ahead).start()
            cols = slice((c + d) * LANES, (c + d + 1) * LANES)
            landed, at = (mine, c + d) if c + d < blocks // 2 else (theirs, c + d - blocks // 2)
            for r in range(3):
                keep(top, 2 + r, cols, *split(landed[at, pl.ds(r, frames, stride=count), :]))
                keep(bottom, r, cols, *split(landed[at, pl.ds(count - 3 + r, frames, stride=count), :]))
        if end == blocks:
            halo(False).start()
            halo(True).start()
        cols = slice(c * LANES, (c + step) * LANES)
        a, b = two_rows(left, top[0:256, cols])
        mixed[0:32, cols] = a
        mixed[32:64, cols] = b
        mixed[64:96, cols] = one_row(left, top[128:320, cols])
        mixed[96:128, cols] = one_row(left, bottom[0:192, cols])
        a, b = two_rows(left, bottom[64:320, cols])
        mixed[128:160, cols] = a
        mixed[160:192, cols] = b

    above, below = moved_image(mixed[0:32, :], me), moved_image(mixed[160:192, :], me)
    for g in range(2):
        put_halves(own, send, 8 * g, above[g] + below[g], me)
    for r in range(1, 5):
        image = moved_image(mixed[r * 32 : r * 32 + 32, :], me)
        for g in range(2):
            put_halves(own, send, r * 16 + 8 * g, image[g], me)
    halo(False).wait()
    halo(True).wait()


def inner_sums(landed, left, stack, mixed):
    blocks = landed.shape[0]
    rows = mixed.shape[0] // 32
    count = rows + 4
    frames = landed.shape[1] // count
    for c in range(0, blocks, 2):
        pair = min(2, blocks - c)
        for d in range(pair):
            cols = slice((c + d) * LANES, (c + d + 1) * LANES)
            for r in range(rows + 2):
                keep(stack, r, cols, *split(landed[c + d, pl.ds(1 + r, frames, stride=count), :]))
        cols = slice(c * LANES, (c + pair) * LANES)
        for r in range(0, rows, 2):
            a, b = two_rows(left, stack[r * 64 : r * 64 + 256, cols])
            mixed[r * 32 : r * 32 + 32, cols] = a
            mixed[r * 32 + 32 : r * 32 + 64, cols] = b


def early_kernel(landed, weights, mixed, stack):
    inner_sums(landed, weights[...], stack, mixed)


def border_kernel(own, other, passed, made, first, second, onward):
    even = lax.rem(lax.axis_index("tile"), 2) == 0
    edge = own[0:16] + other[0:16]
    phase = row_phase((8, own.shape[1]))
    above = jnp.where(phase >= 2, edge[0:8], pltpu.roll(edge[8:16], 6, 0))
    below = jnp.where(phase < 2, edge[0:8], pltpu.roll(edge[8:16], 2, 0))
    top = own[16:48] + other[16:48]
    bottom = own[48:80] + other[48:80]
    first[0:32] = jnp.where(even, bottom, top)
    first[32:40] = jnp.where(even, below, above)
    second[0:32] = jnp.where(even, top, bottom)
    second[32:40] = jnp.where(even, above, below)


def halo_mask():
    lane = lax.broadcasted_iota(I32, (8, LANES), 1)
    here = lax.axis_index("frame") == 0
    return jnp.where(here, jnp.where(lane < 64, 1.0, 0.0), jnp.where(lane < 64, 0.0, 1.0)).astype(F32)


def expand(stack, at, value):
    ext = value.shape[1]
    low, high = value[0:8], value[8:16]
    groups = jnp.concatenate([low, high, pltpu.roll(high, 1, 1), pltpu.roll(low, ext - 1, 1)], axis=0)
    keep(stack, at, slice(None), *split(groups))


def assembled(t, near, field=None):
    ext = t.shape[1]
    half = ext - LANES

    def masked(x):
        return jnp.concatenate([x[:, :half], x[:, half:] * near], axis=1)

    low = t[0:8] + pltpu.roll(masked(t[24:32]), 1, 1)
    high = t[8:16] + pltpu.roll(masked(t[16:24]), ext - 1, 1)
    if field is not None:
        low, high = low + DAMPING * field[0:8], high + DAMPING * field[8:16]
    return jnp.concatenate([masked(low), masked(high)], axis=0)


def finished(t, field, near):
    return assembled(t, near, field)


def folded(a, b):
    total = None
    for c in range(0, a.shape[1] - LANES + 1, LANES):
        for g in (0, 8):
            term = a[g : g + 8, c : c + LANES] * b[g : g + 8, c : c + LANES]
            total = term if total is None else total + term
    return total


def interior_kernel(
    own1, other1, ours, landed, base, once, twice, stack1, stack2, tables, spread, sums, stack, mixed
):
    ext = own1.shape[1]
    half = ext - LANES
    inner = ours.shape[0] // 32
    tile, tiles = lax.axis_index("tile"), lax.axis_size("tile")
    no_up = jnp.where(tile > 0, 0.0, 1.0).astype(F32)
    no_down = jnp.where(tile < tiles - 1, 0.0, 1.0).astype(F32)

    taps = [
        jnp.concatenate([ref[80:88, r * LANES : (r + 1) * LANES] for r in range(4)], axis=0) for ref in (own1, other1)
    ]
    inner_sums(landed, adjoint_weights(taps[1]), stack, mixed)
    block = lax.broadcasted_iota(I32, (32, LANES), 1) >> 5
    left = jnp.concatenate(
        [jnp.concatenate([t, jnp.where(block == 2, t, 0.0), jnp.where(block == 0, t, 0.0)], axis=0) for t in taps],
        axis=1,
    )
    empty = jnp.zeros((64, LANES), F32)
    right = []
    for t in taps:
        e, a = pltpu.roll(t, 32, 1), pltpu.roll(t, LANES - 32, 1)
        right.append(jnp.concatenate([e, e, t, t, a, a, empty, empty, e, e, t, t, a, a], axis=0))
    product = lax.dot_general(
        left, jnp.concatenate(right, axis=1), NT, precision=HIGHEST, preferred_element_type=F32
    )
    lane = lax.broadcasted_iota(I32, (32, 512), 1)
    middle = ((lane >> 6) == 1) | ((lane >> 6) == 6)
    full = product[0:32]
    at_top = full - no_up * jnp.where(middle, product[32:64], 0.0)
    at_bottom = full - no_down * jnp.where(middle, product[64:96], 0.0)
    plain_a, plain_b = paired(full[:, 0:256]), paired(full[:, 256:512])
    top_a, top_b = paired(at_top[:, 0:256]), paired(at_top[:, 256:512])
    bottom_a, bottom_b = paired(at_bottom[:, 0:256]), paired(at_bottom[:, 256:512])
    pairs = [(plain_a, plain_b), (plain_a, top_b), (top_a, plain_b), (plain_a, bottom_b), (bottom_a, plain_b)]
    for i, (a, b) in enumerate(pairs):
        tables[i * 128 : i * 128 + 64] = a
        tables[i * 128 + 64 : i * 128 + 128] = b
    plain = jnp.concatenate([plain_a, plain_b], axis=0)

    source = lax.broadcasted_iota(I32, spread.shape, 0)
    target = lax.broadcasted_iota(I32, spread.shape, 1)
    hit = target == 4 * (source & (LANES - 1)) + (source >> 7)
    spread[...] = jnp.where(hit, 1.0, 0.0).astype(BF16)
    near = halo_mask()
    totals = [jnp.zeros((8, LANES), F32) for _ in range(4)]

    for r in range(inner + 2):
        if r == 0:
            value = own1[32:48] + other1[32:48]
        elif r == inner + 1:
            value = own1[48:64] + other1[48:64]
        else:
            at = (r - 1) * 32
            value = assembled(ours[at : at + 32] + mixed[at : at + 32], near)
        base[r * 16 : r * 16 + 16] = value
        totals[0] += folded(value[:, :half], value[:, :half])
        expand(stack1, r, value)
    for r in range(0, inner, 2):
        images = two_rows(plain, stack1[r * 64 : r * 64 + 256])
        for d in range(2):
            field = base[(r + d + 1) * 16 : (r + d + 2) * 16]
            value = finished(images[d], field, near)
            once[(r + d) * 16 : (r + d + 1) * 16] = value
            totals[1] += folded(field[:, :half], value[:, :half])
            totals[2] += folded(value[:, :half], value[:, :half])
            expand(stack2, r + d, value)
    for r in range(0, inner - 2, 2):
        images = two_rows(plain, stack2[r * 64 : r * 64 + 256])
        for d in range(2):
            field = once[(r + d + 1) * 16 : (r + d + 2) * 16]
            value = finished(images[d], field, near)[:, :half]
            twice[(r + d) * 16 : (r + d + 1) * 16] = value
            totals[3] += folded(field[:, :half], value)
    for i in range(4):
        sums[i * 8 : i * 8 + 8] = totals[i]


def rim_kernel(
    own, other, first, second, base, once, stack1, stack2, tables, partial,
    base_rim, once_rim, twice_rim, sums, above1, below1, above2, below2,
):
    ext = own.shape[1]
    half = ext - LANES
    inner = base.shape[0] // 16
    tile, tiles = lax.axis_index("tile"), lax.axis_size("tile")
    even = lax.rem(tile, 2) == 0
    has_up = jnp.where(tile > 0, 1.0, 0.0).astype(F32)
    has_down = jnp.where(tile < tiles - 1, 1.0, 0.0).astype(F32)
    near = halo_mask()
    phase = row_phase((16, ext))
    totals = [partial[i * 8 : i * 8 + 8] for i in range(4)]
    plain = tables[0:128]

    above1[192:320] = stack1[0:128]
    below1[0:128] = stack1[(inner - 2) * 64 : inner * 64]
    above2[192:320] = stack2[0:128]
    below2[0:128] = stack2[(inner - 4) * 64 : (inner - 2) * 64]

    edge = own[0:16] + other[0:16]
    up = jnp.where(even, second[...], first[...])
    down = jnp.where(even, first[...], second[...])
    rows = {-2: up[0:16]}
    rows[-1] = up[16:32] + has_up * jnp.where(phase >= 2, edge, 0.0)
    e = up[32:40]
    spare = jnp.where(phase < 2, jnp.concatenate([e, pltpu.roll(e, 6, 0)], axis=0), 0.0)
    rows[0] = own[16:32] + other[16:32] + spare
    rows[1] = base[0:16]
    e = down[32:40]
    spare = jnp.where(phase >= 2, jnp.concatenate([e, pltpu.roll(e, 2, 0)], axis=0), 0.0)
    low_rows = {0: base[(inner - 1) * 16 : inner * 16]}
    low_rows[1] = own[64:80] + other[64:80] + spare
    low_rows[2] = down[0:16] + has_down * jnp.where(phase < 2, edge, 0.0)
    low_rows[3] = down[16:32]
    for i in range(3):
        expand(above1, i, rows[i - 2])
        expand(below1, i + 2, low_rows[i + 1])
    base_rim[0:16] = rows[0][:, :half]
    base_rim[16:32] = low_rows[1][:, :half]
    totals[0] += folded(rows[0][:, :half], rows[0][:, :half])
    totals[0] += folded(low_rows[1][:, :half], low_rows[1][:, :half])

    a, b = two_rows(tables[128:256], above1[0:256])
    c = one_row(plain, above1[128:320])
    high = [finished(a, rows[-1], near) * has_up, finished(b, rows[0], near), finished(c, rows[1], near)]
    a = one_row(plain, below1[0:192])
    b, c = two_rows(tables[512:640], below1[64:320])
    deep = [
        finished(a, low_rows[0], near),
        finished(b, low_rows[1], near),
        finished(c, low_rows[2], near) * has_down,
    ]
    for i in range(3):
        expand(above2, i, high[i])
        expand(below2, i + 2, deep[i])
    pieces = [(rows[0], high[1]), (rows[1], high[2]), (low_rows[0], deep[0]), (low_rows[1], deep[1])]
    for i, (field, value) in enumerate(pieces):
        once_rim[i * 16 : i * 16 + 16] = value[:, :half]
        totals[1] += folded(field[:, :half], value[:, :half])
        totals[2] += folded(value[:, :half], value[:, :half])

    a, b = two_rows(tables[256:384], above2[0:256])
    c = one_row(plain, above2[128:320])
    d = one_row(plain, below2[0:192])
    e, f = two_rows(tables[384:512], below2[64:320])
    fields = [high[1], high[2], once[0:16], once[(inner - 3) * 16 : (inner - 2) * 16], deep[0], deep[1]]
    for i, (t, field) in enumerate(zip([a, b, c, d, e, f], fields)):
        value = finished(t, field, near)[:, :half]
        twice_rim[i * 16 : i * 16 + 16] = value
        totals[3] += folded(field[:, :half], value)
    lane = lax.broadcasted_iota(I32, (1, LANES), 1) >> 5
    line = jnp.zeros((1, LANES), F32)
    for i, t in enumerate(totals):
        part = jnp.sum(t, axis=0, keepdims=True)
        part = part + pltpu.roll(part, 64, 1)
        part = part + pltpu.roll(part, 32, 1)
        line = jnp.where(lane == i, part, line)
    sums[...] = jnp.broadcast_to(line, sums.shape)


def update_kernel(base, once, twice, base_rim, once_rim, twice_rim, spread, sums, solution, residual, near_x, near_r, sems):
    lanes = jnp.sum(sums[...], axis=0, keepdims=True)
    kind = lax.broadcasted_iota(I32, lanes.shape, 1) >> 5

    def total(at):
        return jnp.sum(jnp.where(kind == at, lanes, 0.0), axis=1, keepdims=True)

    bb, bm, mm, mmm = [total(at) for at in range(4)]
    alpha = bb / bm
    norm = alpha * alpha * mm - 2.0 * alpha * bm + bb
    beta = norm / bb
    grow = 1.0 + beta
    product = grow * grow * bm - 2.0 * grow * alpha * mm + alpha * alpha * mmm
    step = norm / product
    count = base.shape[0] // 16 + 2
    half = base_rim.shape[1]
    side = lax.broadcasted_iota(I32, (count // 2, 8, LANES), 1) < 4

    def arranged(x):
        x = x.reshape(count // 2, 4, 8, LANES)
        pieces = []
        for g in range(2):
            a, b = x[:, g], x[:, g + 2]
            pieces.append(jnp.where(side, a, pltpu.roll(b, 4, 1)).reshape(4 * count, LANES))
            pieces.append(jnp.where(side, pltpu.roll(a, 4, 1), b).reshape(4 * count, LANES))
        return split(jnp.concatenate(pieces, axis=1))

    def stores(c):
        wide = pl.ds(4 * c * LANES, 4 * LANES)
        return [
            pltpu.make_async_copy(near.at[:, wide], far.at[:, wide], sems.at[i, c])
            for i, (near, far) in enumerate([(near_x, solution), (near_r, residual)])
        ]

    def rows_of(middle, rim, cols):
        n = rim.shape[0] // 2
        return jnp.concatenate([rim[0:n, cols], middle[:, cols], rim[n : 2 * n, cols]], axis=0)

    for c in range(half // LANES):
        cols = slice(c * LANES, (c + 1) * LANES)
        b, m, mm_ = rows_of(base, base_rim, cols), rows_of(once, once_rim, cols), rows_of(twice, twice_rim, cols)
        x = (alpha + step * grow) * b - (step * alpha) * m
        r = (b - alpha * m) - step * (grow * m - alpha * mm_)
        xh, xl = arranged(x)
        rh, rl = arranged(r)
        out = jnp.dot(jnp.concatenate([xh, xl, rh, rl], axis=0), spread[...], preferred_element_type=F32)
        n = 4 * count
        wide = slice(4 * c * LANES, 4 * (c + 1) * LANES)
        near_x[:, wide] = out[0:n] + out[n : 2 * n]
        near_r[:, wide] = out[2 * n : 3 * n] + out[3 * n : 4 * n]
        for copy in stores(c):
            copy.start()
    for c in range(half // LANES):
        for copy in stores(c):
            copy.wait()


def params(mebibytes=24):
    return pltpu.CompilerParams(vmem_limit_bytes=mebibytes * 1024 * 1024)


def cost(units):
    return pl.CostEstimate(flops=int(units * 10**9), bytes_accessed=int(units * 2**22), transcendentals=0)


def vmem(n):
    return [pl.BlockSpec(memory_space=pltpu.VMEM)] * n


def per_device(observed, frame_shift, kernel_ids, groups, kernels, gains):
    frames, count, wide = observed.shape
    half = wide // 2
    ext = half + LANES
    blocks = wide // LANES
    tiles, spread = lax.axis_size("tile"), lax.axis_size("frame")
    far = pl.BlockSpec(memory_space=pltpu.HBM)
    shape = jax.ShapeDtypeStruct
    inner = count - 4

    mine, theirs, own, send, weights = pl.pallas_call(
        outer_kernel,
        out_shape=(
            shape((blocks // 2 + 1, frames * count, LANES), F32),
            shape((blocks // 2 + 1, frames * count, LANES), F32),
            shape((88, ext), F32),
            shape((88, ext), F32),
            shape((128, 256), BF16),
        ),
        in_specs=[far] * 6,
        out_specs=tuple(vmem(5)),
        scratch_shapes=[
            pltpu.VMEM((320, wide), BF16),
            pltpu.VMEM((320, wide), BF16),
            pltpu.VMEM((192, wide), F32),
            pltpu.SemaphoreType.DMA((blocks + 2,)),
            pltpu.VMEM(frame_shift.shape, I32),
            pltpu.VMEM(kernel_ids.shape, I32),
            pltpu.VMEM(groups.shape, I32),
            pltpu.SMEM((5, kernels.shape[0], 5), F32),
            pltpu.SMEM(gains.shape, F32),
            pltpu.SemaphoreType.DMA((5,)),
        ],
        compiler_params=params(),
        name="outer",
    )(
        *(
            pltpu.with_memory_space_constraint(x, pltpu.HBM)
            for x in (frame_shift, kernel_ids, groups, kernels.transpose(1, 0, 2), gains, observed.reshape(-1, wide))
        )
    )
    other = lax.ppermute(send, "frame", [(0, 1), (1, 0)])

    ours = pl.pallas_call(
        early_kernel,
        out_shape=shape((inner * 32, ext), F32),
        in_specs=vmem(2),
        out_specs=vmem(1)[0],
        scratch_shapes=[pltpu.VMEM(((inner + 2) * 64, ext), BF16)],
        compiler_params=params(),
        cost_estimate=cost(1),
        name="early",
    )(mine, weights)
    first, second, theirs = pl.pallas_call(
        border_kernel,
        out_shape=(shape((40, ext), F32), shape((40, ext), F32), shape(theirs.shape, F32)),
        in_specs=vmem(2) + [pl.BlockSpec(memory_space=pl.ANY)] * 2,
        out_specs=tuple(vmem(2)) + (pl.BlockSpec(memory_space=pl.ANY),),
        input_output_aliases={2: 2},
        compiler_params=params(),
        name="border",
    )(own, other, theirs, ours)
    theirs = lax.ppermute(theirs, "frame", [(0, 1), (1, 0)])
    pairs = [(i, i ^ 1) for i in range(tiles) if i ^ 1 < tiles]
    odd_pairs = [p for i in range(1, tiles - 1, 2) for p in ((i, i + 1), (i + 1, i))]
    second = lax.ppermute(second, "tile", odd_pairs)
    first = lax.ppermute(first, "tile", pairs)

    base, once, twice, stack1, stack2, tables, spreading, partial = pl.pallas_call(
        interior_kernel,
        out_shape=(
            shape(((inner + 2) * 16, ext), F32),
            shape((inner * 16, ext), F32),
            shape(((inner - 2) * 16, half), F32),
            shape(((inner + 2) * 64, ext), BF16),
            shape((inner * 64, ext), BF16),
            shape((5 * 128, 256), BF16),
            shape((4 * LANES, 4 * LANES), BF16),
            shape((32, LANES), F32),
        ),
        in_specs=vmem(4),
        out_specs=tuple(vmem(8)),
        scratch_shapes=[pltpu.VMEM(((inner + 2) * 64, ext), BF16), pltpu.VMEM((inner * 32, ext), F32)],
        compiler_params=params(),
        cost_estimate=cost(0.01),
        name="interior",
    )(own, other, ours, theirs)
    peers = tiles * spread
    base_rim, once_rim, twice_rim, sums = pl.pallas_call(
        rim_kernel,
        out_shape=(
            shape((32, half), F32),
            shape((64, half), F32),
            shape((96, half), F32),
            shape((peers, LANES), F32),
        ),
        in_specs=vmem(10),
        out_specs=tuple(vmem(4)),
        scratch_shapes=[pltpu.VMEM((320, ext), BF16)] * 4,
        compiler_params=params(),
        name="rim",
    )(own, other, first, second, base, once, stack1, stack2, tables, partial)
    sums = lax.all_to_all(sums, ("tile", "frame"), 0, 0)

    solution, residual = pl.pallas_call(
        update_kernel,
        out_shape=(shape((count * 4, 4 * half), F32),) * 2,
        in_specs=vmem(8),
        out_specs=(far,) * 2,
        scratch_shapes=[pltpu.VMEM((count * 4, 4 * half), F32)] * 2
        + [pltpu.SemaphoreType.DMA((2, half // LANES))],
        compiler_params=params(),
        name="update",
    )(base, once, twice, base_rim, once_rim, twice_rim, spreading, sums)
    return solution, residual


def solution(mesh):
    return jax.shard_map(
        per_device,
        mesh=mesh,
        in_specs=(
            P("frame", ("scene", "tile"), None),
            P("scene", "frame"),
            P("scene", "frame"),
            P("scene", "frame"),
            P(),
            P(),
        ),
        out_specs=(P(("scene", "tile"), "frame"), P(("scene", "tile"), "frame")),
        check_vma=False,
    )
```

```python
import functools

import jax
import jax.numpy as jnp
from jax import lax
from jax.experimental import pallas as pl
from jax.experimental.pallas import tpu as pltpu
from jax.sharding import PartitionSpec as P

DAMPING = 0.3
LANES = 128
HIGHEST = lax.Precision.HIGHEST
NT = (((1,), (1,)), ((), ()))
F32, BF16, I32 = jnp.float32, jnp.bfloat16, jnp.int32


def split(x):
    high = x.astype(BF16)
    return high, (x - high.astype(F32)).astype(BF16)


def paired(table):
    high, low = split(table)
    second = (lax.broadcasted_iota(I32, table.shape, 1) >> 5) & 1
    return jnp.concatenate([high, jnp.where(second == 0, low.astype(F32), 0.0).astype(BF16)], axis=0)


def row_phase(shape):
    return lax.broadcasted_iota(I32, shape, 0) & 3


def tap_table(shift, ids, members, kernels, gains):
    frames = shift.shape[1]
    copies = LANES // frames

    def tiled(x):
        return jnp.concatenate([x] * copies, axis=1)

    shape = (32, LANES)
    place = lax.broadcasted_iota(I32, shape, 0)
    lane = lax.broadcasted_iota(I32, shape, 1)
    group = place >> 3
    first = jnp.where(group == 0, 2, jnp.where(group == 1, 4, jnp.where(group == 2, 0, 6)))
    col = first + ((place >> 2) & 1)
    row = 2 + 4 * ((lane >> 5) - 1) + (place & 3)
    up = row - tiled(shift[0:1, :])
    along = col - tiled(shift[1:2, :])
    kind = tiled(ids[...])
    member = tiled(members[...])
    inside = (row >= 0) & (row < 8) & (up >= 0) & (up < 5) & (along >= 0) & (along < 5)
    count = kernels.shape[1]
    code = jnp.where(inside, kind * 25 + up * 5 + along, -1)
    total = jnp.zeros(shape, F32)
    for n in range(count):
        for a in range(5):
            for b in range(5):
                total = jnp.where(code == n * 25 + a * 5 + b, kernels[a, n, b], total)
    scale = jnp.zeros((1, LANES), F32)
    for g in range(gains.shape[0]):
        scale = jnp.where(member == g, gains[g], scale)
    return total * scale


def put_halves(own, send, at, value, me):
    half = value.shape[1] // 2
    near = lax.broadcasted_iota(I32, (8, LANES), 1) < 64
    own[at : at + 8, :half] = value[:, :half]
    send[at : at + 8, :half] = value[:, half:]
    after = jnp.where(near, value[:, half : half + LANES], 0.0)
    before = jnp.where(near, 0.0, value[:, 2 * half - LANES :])
    own[at : at + 8, half:] = jnp.where(me == 0, after, before)
    before = jnp.where(near, 0.0, value[:, half - LANES : half])
    after = jnp.where(near, value[:, 0:LANES], 0.0)
    send[at : at + 8, half:] = jnp.where(me == 0, before, after)


def moved_image(t, me):
    wide = t.shape[1]
    half = wide // 2
    lane = lax.broadcasted_iota(I32, (8, wide), 1)
    low = t[0:8] + jnp.where(lane == jnp.where(me == 0, 0, half), 0.0, pltpu.roll(t[24:32], 1, 1))
    last = jnp.where(me == 0, wide - 1, half - 1)
    high = t[8:16] + jnp.where(lane == last, 0.0, pltpu.roll(t[16:24], wide - 1, 1))
    return low, high


def two_rows(weights, columns):
    both = jnp.dot(weights, columns, preferred_element_type=F32)
    return both[0:32] + both[32:64], both[64:96] + both[96:128]


def one_row(weights, columns):
    both = jnp.dot(weights[0:64, 0:192], columns, preferred_element_type=F32)
    return both[0:32] + both[32:64]


def keep(stack, at, cols, high, low):
    stack[at * 64 : at * 64 + 32, cols] = high
    stack[at * 64 + 32 : at * 64 + 64, cols] = low


def adjoint_weights(table):
    source = lax.broadcasted_iota(I32, (LANES, 512), 0)
    target = lax.broadcasted_iota(I32, (LANES, 512), 1)
    place = (target & 255) - 64 * (target >> 8)
    pick = (source == (2 - (place >> 6)) * 32 + (place & 31)) & (place >= 0) & (place < 192)
    both = jnp.dot(table, pick.astype(F32), precision=HIGHEST, preferred_element_type=F32)
    return jnp.concatenate([paired(both[:, 0:256]), paired(both[:, 256:512])], axis=0)


def outer_kernel(
    far_shift, far_ids, far_members, far_kernels, far_gains, obs, mine, theirs, own, send, weights,
    top, bottom, mixed, sems, shift, ids, members, kernels, gains, small_sems,
):
    wide = obs.shape[1]
    frames = shift.shape[1]
    count = obs.shape[0] // frames
    blocks = wide // LANES
    me = lax.axis_index("frame")

    half = wide // 2

    def load(c):
        start = jnp.where(me == 0, 0, half) if c < blocks // 2 else jnp.where(me == 0, half, 0)
        start = start + (c % (blocks // 2)) * LANES
        target = mine if c < blocks // 2 else theirs
        at = c % (blocks // 2)
        source = obs.at[:, pl.ds(pl.multiple_of(start, LANES), LANES)]
        return pltpu.make_async_copy(source, target.at[at], sems.at[c])

    def halo(from_theirs):
        last = blocks // 2 - 1
        source, target = (theirs, mine) if from_theirs else (mine, theirs)
        at = jnp.where(me == 0, 0, last) if from_theirs else jnp.where(me == 0, last, 0)
        return pltpu.make_async_copy(
            source.at[at], target.at[blocks // 2], sems.at[blocks + 1 if from_theirs else blocks]
        )

    ahead = min(8, blocks)
    small = [
        pltpu.make_async_copy(far, near, small_sems.at[i])
        for i, (far, near) in enumerate(
            [(far_kernels, kernels), (far_gains, gains), (far_shift, shift), (far_ids, ids), (far_members, members)]
        )
    ]
    for copy in small:
        copy.start()
    for c in range(ahead):
        load(c).start()
    nothing = jnp.zeros((128, wide), BF16)
    top[0:128, :] = nothing
    bottom[192:320, :] = nothing
    for copy in small:
        copy.wait()
    table = tap_table(shift, ids, members, kernels, gains)
    for r in range(4):
        own[80:88, r * LANES : (r + 1) * LANES] = table[8 * r : 8 * r + 8]
        send[80:88, r * LANES : (r + 1) * LANES] = table[8 * r : 8 * r + 8]
    rest = own.shape[1] - 4 * LANES
    if rest > 0:
        own[80:88, 4 * LANES :] = jnp.zeros((8, rest), F32)
        send[80:88, 4 * LANES :] = jnp.zeros((8, rest), F32)
    left = adjoint_weights(table)
    weights[...] = left

    cuts = [0, blocks // 2, blocks]
    for c, end in zip(cuts, cuts[1:]):
        step = end - c
        for d in range(step):
            load(c + d).wait()
            if c + d + ahead < blocks:
                load(c + d + ahead).start()
            cols = slice((c + d) * LANES, (c + d + 1) * LANES)
            landed, at = (mine, c + d) if c + d < blocks // 2 else (theirs, c + d - blocks // 2)
            for r in range(3):
                keep(top, 2 + r, cols, *split(landed[at, pl.ds(r, frames, stride=count), :]))
                keep(bottom, r, cols, *split(landed[at, pl.ds(count - 3 + r, frames, stride=count), :]))
        if end == blocks:
            halo(False).start()
            halo(True).start()
        cols = slice(c * LANES, (c + step) * LANES)
        a, b = two_rows(left, top[0:256, cols])
        mixed[0:32, cols] = a
        mixed[32:64, cols] = b
        mixed[64:96, cols] = one_row(left, top[128:320, cols])
        mixed[96:128, cols] = one_row(left, bottom[0:192, cols])
        a, b = two_rows(left, bottom[64:320, cols])
        mixed[128:160, cols] = a
        mixed[160:192, cols] = b

    above, below = moved_image(mixed[0:32, :], me), moved_image(mixed[160:192, :], me)
    for g in range(2):
        put_halves(own, send, 8 * g, above[g] + below[g], me)
    for r in range(1, 5):
        image = moved_image(mixed[r * 32 : r * 32 + 32, :], me)
        for g in range(2):
            put_halves(own, send, r * 16 + 8 * g, image[g], me)
    halo(False).wait()
    halo(True).wait()


def inner_sums(landed, left, stack, mixed):
    blocks = landed.shape[0]
    rows = mixed.shape[0] // 32
    count = rows + 4
    frames = landed.shape[1] // count
    for c in range(0, blocks, 2):
        pair = min(2, blocks - c)
        for d in range(pair):
            cols = slice((c + d) * LANES, (c + d + 1) * LANES)
            for r in range(rows + 2):
                keep(stack, r, cols, *split(landed[c + d, pl.ds(1 + r, frames, stride=count), :]))
        cols = slice(c * LANES, (c + pair) * LANES)
        for r in range(0, rows, 2):
            a, b = two_rows(left, stack[r * 64 : r * 64 + 256, cols])
            mixed[r * 32 : r * 32 + 32, cols] = a
            mixed[r * 32 + 32 : r * 32 + 64, cols] = b


def early_kernel(landed, weights, mixed, stack):
    inner_sums(landed, weights[...], stack, mixed)


def border_kernel(own, other, passed, made, first, second, onward):
    even = lax.rem(lax.axis_index("tile"), 2) == 0
    edge = own[0:16] + other[0:16]
    phase = row_phase((8, own.shape[1]))
    above = jnp.where(phase >= 2, edge[0:8], pltpu.roll(edge[8:16], 6, 0))
    below = jnp.where(phase < 2, edge[0:8], pltpu.roll(edge[8:16], 2, 0))
    top = own[16:48] + other[16:48]
    bottom = own[48:80] + other[48:80]
    here = lax.axis_index("frame")
    half = own.shape[1] - LANES
    kind = lax.broadcasted_iota(I32, (8, LANES), 1) >> 3

    def pack(ref, rows, last):
        tail = jnp.zeros((8, LANES), F32)
        for g in range(5):
            value = last if g == 4 else rows[8 * g : 8 * g + 8]
            for c in range(half // LANES):
                ref[g * (half // LANES) + c] = value[:, c * LANES : (c + 1) * LANES]
            spare = value[:, half:] if g == 0 else pltpu.roll(value[:, half:], 8 * g, 1)
            tail = jnp.where(kind == jnp.where(here == 0, g, (15 + g) % 16), spare, tail)
        ref[5 * (half // LANES)] = tail

    pack(first, jnp.where(even, bottom, top), jnp.where(even, below, above))
    pack(second, jnp.where(even, top, bottom), jnp.where(even, above, below))


def unpacked(tiles):
    per = tiles.shape[0] // 5
    kind = lax.broadcasted_iota(I32, (8, LANES), 1) >> 3
    mine = kind == jnp.where(lax.axis_index("frame") == 0, 0, 15)
    groups = []
    for g in range(5):
        tail = tiles[5 * per] if g == 0 else pltpu.roll(tiles[5 * per], LANES - 8 * g, 1)
        groups.append(
            jnp.concatenate([tiles[g * per + c] for c in range(per)] + [jnp.where(mine, tail, 0.0)], axis=1)
        )
    return jnp.concatenate(groups, axis=0)


def halo_mask():
    lane = lax.broadcasted_iota(I32, (8, LANES), 1)
    here = lax.axis_index("frame") == 0
    return jnp.where(here, jnp.where(lane < 64, 1.0, 0.0), jnp.where(lane < 64, 0.0, 1.0)).astype(F32)


def expand(stack, at, value):
    ext = value.shape[1]
    low, high = value[0:8], value[8:16]
    groups = jnp.concatenate([low, high, pltpu.roll(high, 1, 1), pltpu.roll(low, ext - 1, 1)], axis=0)
    keep(stack, at, slice(None), *split(groups))


def assembled(t, near, field=None):
    ext = t.shape[1]
    half = ext - LANES

    def masked(x):
        return jnp.concatenate([x[:, :half], x[:, half:] * near], axis=1)

    low = t[0:8] + pltpu.roll(masked(t[24:32]), 1, 1)
    high = t[8:16] + pltpu.roll(masked(t[16:24]), ext - 1, 1)
    if field is not None:
        low, high = low + DAMPING * field[0:8], high + DAMPING * field[8:16]
    return jnp.concatenate([masked(low), masked(high)], axis=0)


def finished(t, field, near):
    return assembled(t, near, field)


def folded(a, b):
    total = None
    for c in range(0, a.shape[1] - LANES + 1, LANES):
        for g in (0, 8):
            term = a[g : g + 8, c : c + LANES] * b[g : g + 8, c : c + LANES]
            total = term if total is None else total + term
    return total


def interior_kernel(
    own1, other1, ours, landed, base, once, twice, stack1, stack2, tables, spread, sums, stack, mixed
):
    ext = own1.shape[1]
    half = ext - LANES
    inner = ours.shape[0] // 32
    tile, tiles = lax.axis_index("tile"), lax.axis_size("tile")
    no_up = jnp.where(tile > 0, 0.0, 1.0).astype(F32)
    no_down = jnp.where(tile < tiles - 1, 0.0, 1.0).astype(F32)

    taps = [
        jnp.concatenate([ref[80:88, r * LANES : (r + 1) * LANES] for r in range(4)], axis=0) for ref in (own1, other1)
    ]
    inner_sums(landed, adjoint_weights(taps[1]), stack, mixed)
    block = lax.broadcasted_iota(I32, (32, LANES), 1) >> 5
    left = jnp.concatenate(
        [jnp.concatenate([t, jnp.where(block == 2, t, 0.0), jnp.where(block == 0, t, 0.0)], axis=0) for t in taps],
        axis=1,
    )
    empty = jnp.zeros((64, LANES), F32)
    right = []
    for t in taps:
        e, a = pltpu.roll(t, 32, 1), pltpu.roll(t, LANES - 32, 1)
        right.append(jnp.concatenate([e, e, t, t, a, a, empty, empty, e, e, t, t, a, a], axis=0))
    product = lax.dot_general(
        left, jnp.concatenate(right, axis=1), NT, precision=HIGHEST, preferred_element_type=F32
    )
    lane = lax.broadcasted_iota(I32, (32, 512), 1)
    middle = ((lane >> 6) == 1) | ((lane >> 6) == 6)
    full = product[0:32]
    at_top = full - no_up * jnp.where(middle, product[32:64], 0.0)
    at_bottom = full - no_down * jnp.where(middle, product[64:96], 0.0)
    plain_a, plain_b = paired(full[:, 0:256]), paired(full[:, 256:512])
    top_a, top_b = paired(at_top[:, 0:256]), paired(at_top[:, 256:512])
    bottom_a, bottom_b = paired(at_bottom[:, 0:256]), paired(at_bottom[:, 256:512])
    pairs = [(plain_a, plain_b), (plain_a, top_b), (top_a, plain_b), (plain_a, bottom_b), (bottom_a, plain_b)]
    for i, (a, b) in enumerate(pairs):
        tables[i * 128 : i * 128 + 64] = a
        tables[i * 128 + 64 : i * 128 + 128] = b
    plain = jnp.concatenate([plain_a, plain_b], axis=0)

    source = lax.broadcasted_iota(I32, spread.shape, 0)
    target = lax.broadcasted_iota(I32, spread.shape, 1)
    hit = target == 4 * (source & (LANES - 1)) + (source >> 7)
    spread[...] = jnp.where(hit, 1.0, 0.0).astype(BF16)
    near = halo_mask()
    totals = [jnp.zeros((8, LANES), F32) for _ in range(4)]

    for r in range(inner + 2):
        if r == 0:
            value = own1[32:48] + other1[32:48]
        elif r == inner + 1:
            value = own1[48:64] + other1[48:64]
        else:
            at = (r - 1) * 32
            value = assembled(ours[at : at + 32] + mixed[at : at + 32], near)
        base[r * 16 : r * 16 + 16] = value
        totals[0] += folded(value[:, :half], value[:, :half])
        expand(stack1, r, value)
    for r in range(0, inner, 2):
        images = two_rows(plain, stack1[r * 64 : r * 64 + 256])
        for d in range(2):
            field = base[(r + d + 1) * 16 : (r + d + 2) * 16]
            value = finished(images[d], field, near)
            once[(r + d) * 16 : (r + d + 1) * 16] = value
            totals[1] += folded(field[:, :half], value[:, :half])
            totals[2] += folded(value[:, :half], value[:, :half])
            expand(stack2, r + d, value)
    for r in range(0, inner - 2, 2):
        images = two_rows(plain, stack2[r * 64 : r * 64 + 256])
        for d in range(2):
            field = once[(r + d + 1) * 16 : (r + d + 2) * 16]
            value = finished(images[d], field, near)[:, :half]
            twice[(r + d) * 16 : (r + d + 1) * 16] = value
            totals[3] += folded(field[:, :half], value)
    for i in range(4):
        sums[i * 8 : i * 8 + 8] = totals[i]


def rim_kernel(
    own, other, first, second, base, once, stack1, stack2, tables, partial,
    base_rim, once_rim, twice_rim, sums, above1, below1, above2, below2,
):
    ext = own.shape[1]
    half = ext - LANES
    inner = base.shape[0] // 16
    tile, tiles = lax.axis_index("tile"), lax.axis_size("tile")
    even = lax.rem(tile, 2) == 0
    has_up = jnp.where(tile > 0, 1.0, 0.0).astype(F32)
    has_down = jnp.where(tile < tiles - 1, 1.0, 0.0).astype(F32)
    near = halo_mask()
    phase = row_phase((16, ext))
    totals = [partial[i * 8 : i * 8 + 8] for i in range(4)]
    plain = tables[0:128]

    above1[192:320] = stack1[0:128]
    below1[0:128] = stack1[(inner - 2) * 64 : inner * 64]
    above2[192:320] = stack2[0:128]
    below2[0:128] = stack2[(inner - 4) * 64 : (inner - 2) * 64]

    edge = own[0:16] + other[0:16]
    up = unpacked(jnp.where(even, second[...], first[...]))
    down = unpacked(jnp.where(even, first[...], second[...]))
    rows = {-2: up[0:16]}
    rows[-1] = up[16:32] + has_up * jnp.where(phase >= 2, edge, 0.0)
    e = up[32:40]
    spare = jnp.where(phase < 2, jnp.concatenate([e, pltpu.roll(e, 6, 0)], axis=0), 0.0)
    rows[0] = own[16:32] + other[16:32] + spare
    rows[1] = base[0:16]
    e = down[32:40]
    spare = jnp.where(phase >= 2, jnp.concatenate([e, pltpu.roll(e, 2, 0)], axis=0), 0.0)
    low_rows = {0: base[(inner - 1) * 16 : inner * 16]}
    low_rows[1] = own[64:80] + other[64:80] + spare
    low_rows[2] = down[0:16] + has_down * jnp.where(phase < 2, edge, 0.0)
    low_rows[3] = down[16:32]
    for i in range(3):
        expand(above1, i, rows[i - 2])
        expand(below1, i + 2, low_rows[i + 1])
    base_rim[0:16] = rows[0][:, :half]
    base_rim[16:32] = low_rows[1][:, :half]
    totals[0] += folded(rows[0][:, :half], rows[0][:, :half])
    totals[0] += folded(low_rows[1][:, :half], low_rows[1][:, :half])

    a, b = two_rows(tables[128:256], above1[0:256])
    c = one_row(plain, above1[128:320])
    high = [finished(a, rows[-1], near) * has_up, finished(b, rows[0], near), finished(c, rows[1], near)]
    a = one_row(plain, below1[0:192])
    b, c = two_rows(tables[512:640], below1[64:320])
    deep = [
        finished(a, low_rows[0], near),
        finished(b, low_rows[1], near),
        finished(c, low_rows[2], near) * has_down,
    ]
    for i in range(3):
        expand(above2, i, high[i])
        expand(below2, i + 2, deep[i])
    pieces = [(rows[0], high[1]), (rows[1], high[2]), (low_rows[0], deep[0]), (low_rows[1], deep[1])]
    for i, (field, value) in enumerate(pieces):
        once_rim[i * 16 : i * 16 + 16] = value[:, :half]
        totals[1] += folded(field[:, :half], value[:, :half])
        totals[2] += folded(value[:, :half], value[:, :half])

    a, b = two_rows(tables[256:384], above2[0:256])
    c = one_row(plain, above2[128:320])
    d = one_row(plain, below2[0:192])
    e, f = two_rows(tables[384:512], below2[64:320])
    fields = [high[1], high[2], once[0:16], once[(inner - 3) * 16 : (inner - 2) * 16], deep[0], deep[1]]
    for i, (t, field) in enumerate(zip([a, b, c, d, e, f], fields)):
        value = finished(t, field, near)[:, :half]
        twice_rim[i * 16 : i * 16 + 16] = value
        totals[3] += folded(field[:, :half], value)
    lane = lax.broadcasted_iota(I32, (1, LANES), 1) >> 5
    line = jnp.zeros((1, LANES), F32)
    for i, t in enumerate(totals):
        part = jnp.sum(t, axis=0, keepdims=True)
        part = part + pltpu.roll(part, 64, 1)
        part = part + pltpu.roll(part, 32, 1)
        line = jnp.where(lane == i, part, line)
    sums[...] = jnp.broadcast_to(line, sums.shape)


def update_kernel(base, once, twice, base_rim, once_rim, twice_rim, spread, sums, solution, residual, near_x, near_r, sems):
    lanes = jnp.sum(sums[...], axis=0, keepdims=True)
    kind = lax.broadcasted_iota(I32, lanes.shape, 1) >> 5

    def total(at):
        return jnp.sum(jnp.where(kind == at, lanes, 0.0), axis=1, keepdims=True)

    bb, bm, mm, mmm = [total(at) for at in range(4)]
    alpha = bb / bm
    norm = alpha * alpha * mm - 2.0 * alpha * bm + bb
    beta = norm / bb
    grow = 1.0 + beta
    product = grow * grow * bm - 2.0 * grow * alpha * mm + alpha * alpha * mmm
    step = norm / product
    count = base.shape[0] // 16 + 2
    half = base_rim.shape[1]
    side = lax.broadcasted_iota(I32, (count // 2, 8, LANES), 1) < 4

    def arranged(x):
        x = x.reshape(count // 2, 4, 8, LANES)
        pieces = []
        for g in range(2):
            a, b = x[:, g], x[:, g + 2]
            pieces.append(jnp.where(side, a, pltpu.roll(b, 4, 1)).reshape(4 * count, LANES))
            pieces.append(jnp.where(side, pltpu.roll(a, 4, 1), b).reshape(4 * count, LANES))
        return split(jnp.concatenate(pieces, axis=1))

    def stores(c):
        wide = pl.ds(4 * c * LANES, 4 * LANES)
        return [
            pltpu.make_async_copy(near.at[:, wide], far.at[:, wide], sems.at[i, c])
            for i, (near, far) in enumerate([(near_x, solution), (near_r, residual)])
        ]

    def rows_of(middle, rim, cols):
        n = rim.shape[0] // 2
        return jnp.concatenate([rim[0:n, cols], middle[:, cols], rim[n : 2 * n, cols]], axis=0)

    for c in range(half // LANES):
        cols = slice(c * LANES, (c + 1) * LANES)
        b, m, mm_ = rows_of(base, base_rim, cols), rows_of(once, once_rim, cols), rows_of(twice, twice_rim, cols)
        x = (alpha + step * grow) * b - (step * alpha) * m
        r = (b - alpha * m) - step * (grow * m - alpha * mm_)
        xh, xl = arranged(x)
        rh, rl = arranged(r)
        out = jnp.dot(jnp.concatenate([xh, xl, rh, rl], axis=0), spread[...], preferred_element_type=F32)
        n = 4 * count
        wide = slice(4 * c * LANES, 4 * (c + 1) * LANES)
        near_x[:, wide] = out[0:n] + out[n : 2 * n]
        near_r[:, wide] = out[2 * n : 3 * n] + out[3 * n : 4 * n]
        for copy in stores(c):
            copy.start()
    for c in range(half // LANES):
        for copy in stores(c):
            copy.wait()


def params(mebibytes=24):
    return pltpu.CompilerParams(vmem_limit_bytes=mebibytes * 1024 * 1024)


def cost(units):
    return pl.CostEstimate(flops=int(units * 10**9), bytes_accessed=int(units * 2**22), transcendentals=0)


def vmem(n):
    return [pl.BlockSpec(memory_space=pltpu.VMEM)] * n


def per_device(observed, frame_shift, kernel_ids, groups, kernels, gains):
    frames, count, wide = observed.shape
    half = wide // 2
    ext = half + LANES
    blocks = wide // LANES
    tiles, spread = lax.axis_size("tile"), lax.axis_size("frame")
    far = pl.BlockSpec(memory_space=pltpu.HBM)
    shape = jax.ShapeDtypeStruct
    inner = count - 4

    mine, theirs, own, send, weights = pl.pallas_call(
        outer_kernel,
        out_shape=(
            shape((blocks // 2 + 1, frames * count, LANES), F32),
            shape((blocks // 2 + 1, frames * count, LANES), F32),
            shape((88, ext), F32),
            shape((88, ext), F32),
            shape((128, 256), BF16),
        ),
        in_specs=[far] * 6,
        out_specs=tuple(vmem(5)),
        scratch_shapes=[
            pltpu.VMEM((320, wide), BF16),
            pltpu.VMEM((320, wide), BF16),
            pltpu.VMEM((192, wide), F32),
            pltpu.SemaphoreType.DMA((blocks + 2,)),
            pltpu.VMEM(frame_shift.shape, I32),
            pltpu.VMEM(kernel_ids.shape, I32),
            pltpu.VMEM(groups.shape, I32),
            pltpu.SMEM((5, kernels.shape[0], 5), F32),
            pltpu.SMEM(gains.shape, F32),
            pltpu.SemaphoreType.DMA((5,)),
        ],
        compiler_params=params(),
        name="outer",
    )(
        *(
            pltpu.with_memory_space_constraint(x, pltpu.HBM)
            for x in (frame_shift, kernel_ids, groups, kernels.transpose(1, 0, 2), gains, observed.reshape(-1, wide))
        )
    )
    other = lax.ppermute(send, "frame", [(0, 1), (1, 0)])

    ours = pl.pallas_call(
        early_kernel,
        out_shape=shape((inner * 32, ext), F32),
        in_specs=vmem(2),
        out_specs=vmem(1)[0],
        scratch_shapes=[pltpu.VMEM(((inner + 2) * 64, ext), BF16)],
        compiler_params=params(),
        cost_estimate=cost(1),
        name="early",
    )(mine, weights)
    halo = (5 * half // LANES + 1, 8, LANES)
    first, second, theirs = pl.pallas_call(
        border_kernel,
        out_shape=(shape(halo, F32), shape(halo, F32), shape(theirs.shape, F32)),
        in_specs=vmem(2) + [pl.BlockSpec(memory_space=pl.ANY)] * 2,
        out_specs=tuple(vmem(2)) + (pl.BlockSpec(memory_space=pl.ANY),),
        input_output_aliases={2: 2},
        compiler_params=params(),
        name="border",
    )(own, other, theirs, ours)
    theirs = lax.ppermute(theirs, "frame", [(0, 1), (1, 0)])
    pairs = [(i, i ^ 1) for i in range(tiles) if i ^ 1 < tiles]
    odd_pairs = [p for i in range(1, tiles - 1, 2) for p in ((i, i + 1), (i + 1, i))]
    second = lax.ppermute(second, "tile", odd_pairs)
    first = lax.ppermute(first, "tile", pairs)

    base, once, twice, stack1, stack2, tables, spreading, partial = pl.pallas_call(
        interior_kernel,
        out_shape=(
            shape(((inner + 2) * 16, ext), F32),
            shape((inner * 16, ext), F32),
            shape(((inner - 2) * 16, half), F32),
            shape(((inner + 2) * 64, ext), BF16),
            shape((inner * 64, ext), BF16),
            shape((5 * 128, 256), BF16),
            shape((4 * LANES, 4 * LANES), BF16),
            shape((32, LANES), F32),
        ),
        in_specs=vmem(4),
        out_specs=tuple(vmem(8)),
        scratch_shapes=[pltpu.VMEM(((inner + 2) * 64, ext), BF16), pltpu.VMEM((inner * 32, ext), F32)],
        compiler_params=params(),
        cost_estimate=cost(0.01),
        name="interior",
    )(own, other, ours, theirs)
    peers = tiles * spread
    base_rim, once_rim, twice_rim, sums = pl.pallas_call(
        rim_kernel,
        out_shape=(
            shape((32, half), F32),
            shape((64, half), F32),
            shape((96, half), F32),
            shape((peers, LANES), F32),
        ),
        in_specs=vmem(10),
        out_specs=tuple(vmem(4)),
        scratch_shapes=[pltpu.VMEM((320, ext), BF16)] * 4,
        compiler_params=params(),
        name="rim",
    )(own, other, first, second, base, once, stack1, stack2, tables, partial)
    sums = lax.all_to_all(sums, ("tile", "frame"), 0, 0)

    solution, residual = pl.pallas_call(
        update_kernel,
        out_shape=(shape((count * 4, 4 * half), F32),) * 2,
        in_specs=vmem(8),
        out_specs=(far,) * 2,
        scratch_shapes=[pltpu.VMEM((count * 4, 4 * half), F32)] * 2
        + [pltpu.SemaphoreType.DMA((2, half // LANES))],
        compiler_params=params(),
        name="update",
    )(base, once, twice, base_rim, once_rim, twice_rim, spreading, sums)
    return solution, residual


def solution(mesh):
    return jax.shard_map(
        per_device,
        mesh=mesh,
        in_specs=(
            P("frame", ("scene", "tile"), None),
            P("scene", "frame"),
            P("scene", "frame"),
            P("scene", "frame"),
            P(),
            P(),
        ),
        out_specs=(P(("scene", "tile"), "frame"), P(("scene", "tile"), "frame")),
        check_vma=False,
    )
```

```python
import functools

import jax
import jax.numpy as jnp
from jax import lax
from jax.experimental import pallas as pl
from jax.experimental.pallas import tpu as pltpu
from jax.sharding import PartitionSpec as P

DAMPING = 0.3
LANES = 128
HIGHEST = lax.Precision.HIGHEST
NT = (((1,), (1,)), ((), ()))
F32, BF16, I32 = jnp.float32, jnp.bfloat16, jnp.int32


def split(x):
    high = x.astype(BF16)
    return high, (x - high.astype(F32)).astype(BF16)


def paired(table):
    high, low = split(table)
    second = (lax.broadcasted_iota(I32, table.shape, 1) >> 5) & 1
    return jnp.concatenate([high, jnp.where(second == 0, low.astype(F32), 0.0).astype(BF16)], axis=0)


def row_phase(shape):
    return lax.broadcasted_iota(I32, shape, 0) & 3


def tap_table(shift, ids, members, kernels, gains):
    frames = shift.shape[1]
    copies = LANES // frames

    def tiled(x):
        return jnp.concatenate([x] * copies, axis=1)

    shape = (32, LANES)
    place = lax.broadcasted_iota(I32, shape, 0)
    lane = lax.broadcasted_iota(I32, shape, 1)
    group = place >> 3
    first = jnp.where(group == 0, 2, jnp.where(group == 1, 4, jnp.where(group == 2, 0, 6)))
    col = first + ((place >> 2) & 1)
    row = 2 + 4 * ((lane >> 5) - 1) + (place & 3)
    up = row - tiled(shift[0:1, :])
    along = col - tiled(shift[1:2, :])
    kind = tiled(ids[...])
    member = tiled(members[...])
    inside = (row >= 0) & (row < 8) & (up >= 0) & (up < 5) & (along >= 0) & (along < 5)
    count = kernels.shape[1]
    code = jnp.where(inside, kind * 25 + up * 5 + along, -1)
    total = jnp.zeros(shape, F32)
    for n in range(count):
        for a in range(5):
            for b in range(5):
                total = jnp.where(code == n * 25 + a * 5 + b, kernels[a, n, b], total)
    scale = jnp.zeros((1, LANES), F32)
    for g in range(gains.shape[0]):
        scale = jnp.where(member == g, gains[g], scale)
    return total * scale


def put_halves(own, send, at, value, me):
    half = value.shape[1] // 2
    near = lax.broadcasted_iota(I32, (8, LANES), 1) < 64
    own[at : at + 8, :half] = value[:, :half]
    send[at : at + 8, :half] = value[:, half:]
    after = jnp.where(near, value[:, half : half + LANES], 0.0)
    before = jnp.where(near, 0.0, value[:, 2 * half - LANES :])
    own[at : at + 8, half:] = jnp.where(me == 0, after, before)
    before = jnp.where(near, 0.0, value[:, half - LANES : half])
    after = jnp.where(near, value[:, 0:LANES], 0.0)
    send[at : at + 8, half:] = jnp.where(me == 0, before, after)


def moved_image(t, me):
    wide = t.shape[1]
    half = wide // 2
    lane = lax.broadcasted_iota(I32, (8, wide), 1)
    low = t[0:8] + jnp.where(lane == jnp.where(me == 0, 0, half), 0.0, pltpu.roll(t[24:32], 1, 1))
    last = jnp.where(me == 0, wide - 1, half - 1)
    high = t[8:16] + jnp.where(lane == last, 0.0, pltpu.roll(t[16:24], wide - 1, 1))
    return low, high


def two_rows(weights, columns):
    both = jnp.dot(weights, columns, preferred_element_type=F32)
    return both[0:32] + both[32:64], both[64:96] + both[96:128]


def one_row(weights, columns):
    both = jnp.dot(weights[0:64, 0:192], columns, preferred_element_type=F32)
    return both[0:32] + both[32:64]


def keep(stack, at, cols, high, low):
    stack[at * 64 : at * 64 + 32, cols] = high
    stack[at * 64 + 32 : at * 64 + 64, cols] = low


def adjoint_weights(table):
    source = lax.broadcasted_iota(I32, (LANES, 512), 0)
    target = lax.broadcasted_iota(I32, (LANES, 512), 1)
    place = (target & 255) - 64 * (target >> 8)
    pick = (source == (2 - (place >> 6)) * 32 + (place & 31)) & (place >= 0) & (place < 192)
    both = jnp.dot(table, pick.astype(F32), precision=HIGHEST, preferred_element_type=F32)
    return jnp.concatenate([paired(both[:, 0:256]), paired(both[:, 256:512])], axis=0)


def outer_kernel(
    far_shift, far_ids, far_members, far_kernels, far_gains, obs, mine, theirs, own, send, weights,
    top, bottom, mixed, sems, shift, ids, members, kernels, gains, small_sems,
):
    wide = obs.shape[1]
    frames = shift.shape[1]
    count = obs.shape[0] // frames
    blocks = wide // LANES
    me = lax.axis_index("frame")

    half = wide // 2

    def load(c):
        start = jnp.where(me == 0, 0, half) if c < blocks // 2 else jnp.where(me == 0, half, 0)
        start = start + (c % (blocks // 2)) * LANES
        target = mine if c < blocks // 2 else theirs
        at = c % (blocks // 2)
        source = obs.at[:, pl.ds(pl.multiple_of(start, LANES), LANES)]
        return pltpu.make_async_copy(source, target.at[at], sems.at[c])

    def halo(from_theirs):
        last = blocks // 2 - 1
        source, target = (theirs, mine) if from_theirs else (mine, theirs)
        at = jnp.where(me == 0, 0, last) if from_theirs else jnp.where(me == 0, last, 0)
        return pltpu.make_async_copy(
            source.at[at], target.at[blocks // 2], sems.at[blocks + 1 if from_theirs else blocks]
        )

    ahead = min(10, blocks)
    small = [
        pltpu.make_async_copy(far, near, small_sems.at[i])
        for i, (far, near) in enumerate(
            [(far_kernels, kernels), (far_gains, gains), (far_shift, shift), (far_ids, ids), (far_members, members)]
        )
    ]
    for copy in small:
        copy.start()
    for c in range(ahead):
        load(c).start()
    for copy in small:
        copy.wait()
    table = tap_table(shift, ids, members, kernels, gains)
    for r in range(4):
        own[80:88, r * LANES : (r + 1) * LANES] = table[8 * r : 8 * r + 8]
        send[80:88, r * LANES : (r + 1) * LANES] = table[8 * r : 8 * r + 8]
    rest = own.shape[1] - 4 * LANES
    if rest > 0:
        own[80:88, 4 * LANES :] = jnp.zeros((8, rest), F32)
        send[80:88, 4 * LANES :] = jnp.zeros((8, rest), F32)
    left = adjoint_weights(table)
    weights[...] = left

    cuts = [0, blocks // 2, 3 * blocks // 4, blocks]
    for c, end in zip(cuts, cuts[1:]):
        step = end - c
        for d in range(step):
            load(c + d).wait()
            if c + d + ahead < blocks:
                load(c + d + ahead).start()
            cols = slice((c + d) * LANES, (c + d + 1) * LANES)
            landed, at = (mine, c + d) if c + d < blocks // 2 else (theirs, c + d - blocks // 2)
            for r in range(3):
                keep(top, r, cols, *split(landed[at, pl.ds(r, frames, stride=count), :]))
                keep(bottom, r, cols, *split(landed[at, pl.ds(count - 3 + r, frames, stride=count), :]))
        if end == blocks:
            halo(False).start()
            halo(True).start()
        cols = slice(c * LANES, (c + step) * LANES)
        a, b = two_rows(left[:, 128:256], top[0:128, cols])
        mixed[0:32, cols] = a
        mixed[32:64, cols] = b
        mixed[64:96, cols] = one_row(left, top[:, cols])
        mixed[96:128, cols] = one_row(left, bottom[:, cols])
        a, b = two_rows(left[:, 0:128], bottom[64:192, cols])
        mixed[128:160, cols] = a
        mixed[160:192, cols] = b

    above, below = moved_image(mixed[0:32, :], me), moved_image(mixed[160:192, :], me)
    for g in range(2):
        put_halves(own, send, 8 * g, above[g] + below[g], me)
    for r in range(1, 5):
        image = moved_image(mixed[r * 32 : r * 32 + 32, :], me)
        for g in range(2):
            put_halves(own, send, r * 16 + 8 * g, image[g], me)
    halo(False).wait()
    halo(True).wait()


def inner_sums(landed, left, stack, mixed):
    blocks = landed.shape[0]
    rows = mixed.shape[0] // 32
    count = rows + 4
    frames = landed.shape[1] // count
    for c in range(0, blocks, 2):
        pair = min(2, blocks - c)
        for d in range(pair):
            cols = slice((c + d) * LANES, (c + d + 1) * LANES)
            for r in range(rows + 2):
                keep(stack, r, cols, *split(landed[c + d, pl.ds(1 + r, frames, stride=count), :]))
        cols = slice(c * LANES, (c + pair) * LANES)
        for r in range(0, rows, 2):
            a, b = two_rows(left, stack[r * 64 : r * 64 + 256, cols])
            mixed[r * 32 : r * 32 + 32, cols] = a
            mixed[r * 32 + 32 : r * 32 + 64, cols] = b


def early_kernel(landed, weights, mixed, stack):
    inner_sums(landed, weights[...], stack, mixed)


def border_kernel(own, other, passed, made, first, second, onward):
    even = lax.rem(lax.axis_index("tile"), 2) == 0
    edge = own[0:16] + other[0:16]
    phase = row_phase((8, own.shape[1]))
    above = jnp.where(phase >= 2, edge[0:8], pltpu.roll(edge[8:16], 6, 0))
    below = jnp.where(phase < 2, edge[0:8], pltpu.roll(edge[8:16], 2, 0))
    top = own[16:48] + other[16:48]
    bottom = own[48:80] + other[48:80]
    here = lax.axis_index("frame")
    half = own.shape[1] - LANES
    kind = lax.broadcasted_iota(I32, (8, LANES), 1) >> 3

    def pack(ref, rows, last):
        tail = jnp.zeros((8, LANES), F32)
        for g in range(5):
            value = last if g == 4 else rows[8 * g : 8 * g + 8]
            for c in range(half // LANES):
                ref[g * (half // LANES) + c] = value[:, c * LANES : (c + 1) * LANES]
            spare = value[:, half:] if g == 0 else pltpu.roll(value[:, half:], 8 * g, 1)
            tail = jnp.where(kind == jnp.where(here == 0, g, (15 + g) % 16), spare, tail)
        ref[5 * (half // LANES)] = tail

    pack(first, jnp.where(even, bottom, top), jnp.where(even, below, above))
    pack(second, jnp.where(even, top, bottom), jnp.where(even, above, below))


def unpacked(tiles):
    per = tiles.shape[0] // 5
    kind = lax.broadcasted_iota(I32, (8, LANES), 1) >> 3
    mine = kind == jnp.where(lax.axis_index("frame") == 0, 0, 15)
    groups = []
    for g in range(5):
        tail = tiles[5 * per] if g == 0 else pltpu.roll(tiles[5 * per], LANES - 8 * g, 1)
        groups.append(
            jnp.concatenate([tiles[g * per + c] for c in range(per)] + [jnp.where(mine, tail, 0.0)], axis=1)
        )
    return jnp.concatenate(groups, axis=0)


def halo_mask():
    lane = lax.broadcasted_iota(I32, (8, LANES), 1)
    here = lax.axis_index("frame") == 0
    return jnp.where(here, jnp.where(lane < 64, 1.0, 0.0), jnp.where(lane < 64, 0.0, 1.0)).astype(F32)


def expand(stack, at, value):
    ext = value.shape[1]
    low, high = value[0:8], value[8:16]
    groups = jnp.concatenate([low, high, pltpu.roll(high, 1, 1), pltpu.roll(low, ext - 1, 1)], axis=0)
    keep(stack, at, slice(None), *split(groups))


def assembled(t, near, field=None):
    ext = t.shape[1]
    half = ext - LANES

    def masked(x):
        return jnp.concatenate([x[:, :half], x[:, half:] * near], axis=1)

    low = t[0:8] + pltpu.roll(masked(t[24:32]), 1, 1)
    high = t[8:16] + pltpu.roll(masked(t[16:24]), ext - 1, 1)
    if field is not None:
        low, high = low + DAMPING * field[0:8], high + DAMPING * field[8:16]
    return jnp.concatenate([masked(low), masked(high)], axis=0)


def finished(t, field, near):
    return assembled(t, near, field)


def folded(a, b):
    total = None
    for c in range(0, a.shape[1] - LANES + 1, LANES):
        for g in (0, 8):
            term = a[g : g + 8, c : c + LANES] * b[g : g + 8, c : c + LANES]
            total = term if total is None else total + term
    return total


def interior_kernel(
    own1, other1, ours, landed, base, once, twice, stack1, stack2, tables, spread, sums, stack, mixed
):
    ext = own1.shape[1]
    half = ext - LANES
    inner = ours.shape[0] // 32
    tile, tiles = lax.axis_index("tile"), lax.axis_size("tile")
    no_up = jnp.where(tile > 0, 0.0, 1.0).astype(F32)
    no_down = jnp.where(tile < tiles - 1, 0.0, 1.0).astype(F32)

    taps = [
        jnp.concatenate([ref[80:88, r * LANES : (r + 1) * LANES] for r in range(4)], axis=0) for ref in (own1, other1)
    ]
    inner_sums(landed, adjoint_weights(taps[1]), stack, mixed)
    block = lax.broadcasted_iota(I32, (32, LANES), 1) >> 5
    left = jnp.concatenate(
        [jnp.concatenate([t, jnp.where(block == 2, t, 0.0), jnp.where(block == 0, t, 0.0)], axis=0) for t in taps],
        axis=1,
    )
    empty = jnp.zeros((64, LANES), F32)
    right = []
    for t in taps:
        e, a = pltpu.roll(t, 32, 1), pltpu.roll(t, LANES - 32, 1)
        right.append(jnp.concatenate([e, e, t, t, a, a, empty, empty, e, e, t, t, a, a], axis=0))
    product = lax.dot_general(
        left, jnp.concatenate(right, axis=1), NT, precision=HIGHEST, preferred_element_type=F32
    )
    lane = lax.broadcasted_iota(I32, (32, 512), 1)
    middle = ((lane >> 6) == 1) | ((lane >> 6) == 6)
    full = product[0:32]
    at_top = full - no_up * jnp.where(middle, product[32:64], 0.0)
    at_bottom = full - no_down * jnp.where(middle, product[64:96], 0.0)
    plain_a, plain_b = paired(full[:, 0:256]), paired(full[:, 256:512])
    top_a, top_b = paired(at_top[:, 0:256]), paired(at_top[:, 256:512])
    bottom_a, bottom_b = paired(at_bottom[:, 0:256]), paired(at_bottom[:, 256:512])
    pairs = [(plain_a, plain_b), (plain_a, top_b), (top_a, plain_b), (plain_a, bottom_b), (bottom_a, plain_b)]
    for i, (a, b) in enumerate(pairs):
        tables[i * 128 : i * 128 + 64] = a
        tables[i * 128 + 64 : i * 128 + 128] = b
    plain = jnp.concatenate([plain_a, plain_b], axis=0)

    source = lax.broadcasted_iota(I32, spread.shape, 0)
    target = lax.broadcasted_iota(I32, spread.shape, 1)
    hit = target == 4 * (source & (LANES - 1)) + (source >> 7)
    spread[...] = jnp.where(hit, 1.0, 0.0).astype(BF16)
    near = halo_mask()
    totals = [jnp.zeros((8, LANES), F32) for _ in range(4)]

    for r in range(inner + 2):
        if r == 0:
            value = own1[32:48] + other1[32:48]
        elif r == inner + 1:
            value = own1[48:64] + other1[48:64]
        else:
            at = (r - 1) * 32
            value = assembled(ours[at : at + 32] + mixed[at : at + 32], near)
        base[r * 16 : r * 16 + 16] = value
        totals[0] += folded(value[:, :half], value[:, :half])
        expand(stack1, r, value)
    for r in range(0, inner, 2):
        images = two_rows(plain, stack1[r * 64 : r * 64 + 256])
        for d in range(2):
            field = base[(r + d + 1) * 16 : (r + d + 2) * 16]
            value = finished(images[d], field, near)
            once[(r + d) * 16 : (r + d + 1) * 16] = value
            totals[1] += folded(field[:, :half], value[:, :half])
            totals[2] += folded(value[:, :half], value[:, :half])
            expand(stack2, r + d, value)
    for r in range(0, inner - 2, 2):
        images = two_rows(plain, stack2[r * 64 : r * 64 + 256])
        for d in range(2):
            field = once[(r + d + 1) * 16 : (r + d + 2) * 16]
            value = finished(images[d], field, near)[:, :half]
            twice[(r + d) * 16 : (r + d + 1) * 16] = value
            totals[3] += folded(field[:, :half], value)
    for i in range(4):
        sums[i * 8 : i * 8 + 8] = totals[i]


def rim_kernel(
    own, other, first, second, base, once, stack1, stack2, tables, partial,
    base_rim, once_rim, twice_rim, sums, above1, below1, above2, below2,
):
    ext = own.shape[1]
    half = ext - LANES
    inner = base.shape[0] // 16
    tile, tiles = lax.axis_index("tile"), lax.axis_size("tile")
    even = lax.rem(tile, 2) == 0
    has_up = jnp.where(tile > 0, 1.0, 0.0).astype(F32)
    has_down = jnp.where(tile < tiles - 1, 1.0, 0.0).astype(F32)
    near = halo_mask()
    phase = row_phase((16, ext))
    totals = [partial[i * 8 : i * 8 + 8] for i in range(4)]
    plain = tables[0:128]

    above1[192:320] = stack1[0:128]
    below1[0:128] = stack1[(inner - 2) * 64 : inner * 64]
    above2[192:320] = stack2[0:128]
    below2[0:128] = stack2[(inner - 4) * 64 : (inner - 2) * 64]

    edge = own[0:16] + other[0:16]
    up = unpacked(jnp.where(even, second[...], first[...]))
    down = unpacked(jnp.where(even, first[...], second[...]))
    rows = {-2: up[0:16]}
    rows[-1] = up[16:32] + has_up * jnp.where(phase >= 2, edge, 0.0)
    e = up[32:40]
    spare = jnp.where(phase < 2, jnp.concatenate([e, pltpu.roll(e, 6, 0)], axis=0), 0.0)
    rows[0] = own[16:32] + other[16:32] + spare
    rows[1] = base[0:16]
    e = down[32:40]
    spare = jnp.where(phase >= 2, jnp.concatenate([e, pltpu.roll(e, 2, 0)], axis=0), 0.0)
    low_rows = {0: base[(inner - 1) * 16 : inner * 16]}
    low_rows[1] = own[64:80] + other[64:80] + spare
    low_rows[2] = down[0:16] + has_down * jnp.where(phase < 2, edge, 0.0)
    low_rows[3] = down[16:32]
    for i in range(3):
        expand(above1, i, rows[i - 2])
        expand(below1, i + 2, low_rows[i + 1])
    base_rim[0:16] = rows[0][:, :half]
    base_rim[16:32] = low_rows[1][:, :half]
    totals[0] += folded(rows[0][:, :half], rows[0][:, :half])
    totals[0] += folded(low_rows[1][:, :half], low_rows[1][:, :half])

    a, b = two_rows(tables[128:256], above1[0:256])
    c = one_row(plain, above1[128:320])
    high = [finished(a, rows[-1], near) * has_up, finished(b, rows[0], near), finished(c, rows[1], near)]
    a = one_row(plain, below1[0:192])
    b, c = two_rows(tables[512:640], below1[64:320])
    deep = [
        finished(a, low_rows[0], near),
        finished(b, low_rows[1], near),
        finished(c, low_rows[2], near) * has_down,
    ]
    for i in range(3):
        expand(above2, i, high[i])
        expand(below2, i + 2, deep[i])
    pieces = [(rows[0], high[1]), (rows[1], high[2]), (low_rows[0], deep[0]), (low_rows[1], deep[1])]
    for i, (field, value) in enumerate(pieces):
        once_rim[i * 16 : i * 16 + 16] = value[:, :half]
        totals[1] += folded(field[:, :half], value[:, :half])
        totals[2] += folded(value[:, :half], value[:, :half])

    a, b = two_rows(tables[256:384], above2[0:256])
    c = one_row(plain, above2[128:320])
    d = one_row(plain, below2[0:192])
    e, f = two_rows(tables[384:512], below2[64:320])
    fields = [high[1], high[2], once[0:16], once[(inner - 3) * 16 : (inner - 2) * 16], deep[0], deep[1]]
    for i, (t, field) in enumerate(zip([a, b, c, d, e, f], fields)):
        value = finished(t, field, near)[:, :half]
        twice_rim[i * 16 : i * 16 + 16] = value
        totals[3] += folded(field[:, :half], value)
    lane = lax.broadcasted_iota(I32, (1, LANES), 1) >> 5
    line = jnp.zeros((1, LANES), F32)
    for i, t in enumerate(totals):
        part = jnp.sum(t, axis=0, keepdims=True)
        part = part + pltpu.roll(part, 64, 1)
        part = part + pltpu.roll(part, 32, 1)
        line = jnp.where(lane == i, part, line)
    sums[...] = jnp.broadcast_to(line, sums.shape)


def update_kernel(base, once, twice, base_rim, once_rim, twice_rim, spread, sums, solution, residual, near_x, near_r, sems):
    lanes = jnp.sum(sums[...], axis=0, keepdims=True)
    kind = lax.broadcasted_iota(I32, lanes.shape, 1) >> 5

    def total(at):
        return jnp.sum(jnp.where(kind == at, lanes, 0.0), axis=1, keepdims=True)

    bb, bm, mm, mmm = [total(at) for at in range(4)]
    alpha = bb / bm
    norm = alpha * alpha * mm - 2.0 * alpha * bm + bb
    beta = norm / bb
    grow = 1.0 + beta
    product = grow * grow * bm - 2.0 * grow * alpha * mm + alpha * alpha * mmm
    step = norm / product
    count = base.shape[0] // 16 + 2
    half = base_rim.shape[1]
    side = lax.broadcasted_iota(I32, (count // 2, 8, LANES), 1) < 4

    def arranged(x):
        x = x.reshape(count // 2, 4, 8, LANES)
        pieces = []
        for g in range(2):
            a, b = x[:, g], x[:, g + 2]
            pieces.append(jnp.where(side, a, pltpu.roll(b, 4, 1)).reshape(4 * count, LANES))
            pieces.append(jnp.where(side, pltpu.roll(a, 4, 1), b).reshape(4 * count, LANES))
        return split(jnp.concatenate(pieces, axis=1))

    def stores(c):
        wide = pl.ds(4 * c * LANES, 4 * LANES)
        return [
            pltpu.make_async_copy(near.at[:, wide], far.at[:, wide], sems.at[i, c])
            for i, (near, far) in enumerate([(near_x, solution), (near_r, residual)])
        ]

    def rows_of(middle, rim, cols):
        n = rim.shape[0] // 2
        return jnp.concatenate([rim[0:n, cols], middle[:, cols], rim[n : 2 * n, cols]], axis=0)

    for c in range(half // LANES):
        cols = slice(c * LANES, (c + 1) * LANES)
        b, m, mm_ = rows_of(base, base_rim, cols), rows_of(once, once_rim, cols), rows_of(twice, twice_rim, cols)
        x = (alpha + step * grow) * b - (step * alpha) * m
        r = (b - alpha * m) - step * (grow * m - alpha * mm_)
        xh, xl = arranged(x)
        rh, rl = arranged(r)
        out = jnp.dot(jnp.concatenate([xh, xl, rh, rl], axis=0), spread[...], preferred_element_type=F32)
        n = 4 * count
        wide = slice(4 * c * LANES, 4 * (c + 1) * LANES)
        near_x[:, wide] = out[0:n] + out[n : 2 * n]
        near_r[:, wide] = out[2 * n : 3 * n] + out[3 * n : 4 * n]
        for copy in stores(c):
            copy.start()
    for c in range(half // LANES):
        for copy in stores(c):
            copy.wait()


def params(mebibytes=24):
    return pltpu.CompilerParams(vmem_limit_bytes=mebibytes * 1024 * 1024)


def cost(units):
    return pl.CostEstimate(flops=int(units * 10**9), bytes_accessed=int(units * 2**22), transcendentals=0)


def vmem(n):
    return [pl.BlockSpec(memory_space=pltpu.VMEM)] * n


def per_device(observed, frame_shift, kernel_ids, groups, kernels, gains):
    frames, count, wide = observed.shape
    half = wide // 2
    ext = half + LANES
    blocks = wide // LANES
    tiles, spread = lax.axis_size("tile"), lax.axis_size("frame")
    far = pl.BlockSpec(memory_space=pltpu.HBM)
    shape = jax.ShapeDtypeStruct
    inner = count - 4

    mine, theirs, own, send, weights = pl.pallas_call(
        outer_kernel,
        out_shape=(
            shape((blocks // 2 + 1, frames * count, LANES), F32),
            shape((blocks // 2 + 1, frames * count, LANES), F32),
            shape((88, ext), F32),
            shape((88, ext), F32),
            shape((128, 256), BF16),
        ),
        in_specs=[far] * 6,
        out_specs=tuple(vmem(5)),
        scratch_shapes=[
            pltpu.VMEM((192, wide), BF16),
            pltpu.VMEM((192, wide), BF16),
            pltpu.VMEM((192, wide), F32),
            pltpu.SemaphoreType.DMA((blocks + 2,)),
            pltpu.VMEM(frame_shift.shape, I32),
            pltpu.VMEM(kernel_ids.shape, I32),
            pltpu.VMEM(groups.shape, I32),
            pltpu.SMEM((5, kernels.shape[0], 5), F32),
            pltpu.SMEM(gains.shape, F32),
            pltpu.SemaphoreType.DMA((5,)),
        ],
        compiler_params=params(),
        name="outer",
    )(
        *(
            pltpu.with_memory_space_constraint(x, pltpu.HBM)
            for x in (frame_shift, kernel_ids, groups, kernels.transpose(1, 0, 2), gains, observed.reshape(-1, wide))
        )
    )
    other = lax.ppermute(send, "frame", [(0, 1), (1, 0)])

    ours = pl.pallas_call(
        early_kernel,
        out_shape=shape((inner * 32, ext), F32),
        in_specs=vmem(2),
        out_specs=vmem(1)[0],
        scratch_shapes=[pltpu.VMEM(((inner + 2) * 64, ext), BF16)],
        compiler_params=params(),
        cost_estimate=cost(1),
        name="early",
    )(mine, weights)
    halo = (5 * half // LANES + 1, 8, LANES)
    first, second, theirs = pl.pallas_call(
        border_kernel,
        out_shape=(shape(halo, F32), shape(halo, F32), shape(theirs.shape, F32)),
        in_specs=vmem(2) + [pl.BlockSpec(memory_space=pl.ANY)] * 2,
        out_specs=tuple(vmem(2)) + (pl.BlockSpec(memory_space=pl.ANY),),
        input_output_aliases={2: 2},
        compiler_params=params(),
        name="border",
    )(own, other, theirs, ours)
    theirs = lax.ppermute(theirs, "frame", [(0, 1), (1, 0)])
    pairs = [(i, i ^ 1) for i in range(tiles) if i ^ 1 < tiles]
    odd_pairs = [p for i in range(1, tiles - 1, 2) for p in ((i, i + 1), (i + 1, i))]
    second = lax.ppermute(second, "tile", odd_pairs)
    first = lax.ppermute(first, "tile", pairs)

    base, once, twice, stack1, stack2, tables, spreading, partial = pl.pallas_call(
        interior_kernel,
        out_shape=(
            shape(((inner + 2) * 16, ext), F32),
            shape((inner * 16, ext), F32),
            shape(((inner - 2) * 16, half), F32),
            shape(((inner + 2) * 64, ext), BF16),
            shape((inner * 64, ext), BF16),
            shape((5 * 128, 256), BF16),
            shape((4 * LANES, 4 * LANES), BF16),
            shape((32, LANES), F32),
        ),
        in_specs=vmem(4),
        out_specs=tuple(vmem(8)),
        scratch_shapes=[pltpu.VMEM(((inner + 2) * 64, ext), BF16), pltpu.VMEM((inner * 32, ext), F32)],
        compiler_params=params(),
        cost_estimate=cost(0.01),
        name="interior",
    )(own, other, ours, theirs)
    peers = tiles * spread
    base_rim, once_rim, twice_rim, sums = pl.pallas_call(
        rim_kernel,
        out_shape=(
            shape((32, half), F32),
            shape((64, half), F32),
            shape((96, half), F32),
            shape((peers, LANES), F32),
        ),
        in_specs=vmem(10),
        out_specs=tuple(vmem(4)),
        scratch_shapes=[pltpu.VMEM((320, ext), BF16)] * 4,
        compiler_params=params(),
        name="rim",
    )(own, other, first, second, base, once, stack1, stack2, tables, partial)
    sums = lax.all_to_all(sums, ("tile", "frame"), 0, 0)

    solution, residual = pl.pallas_call(
        update_kernel,
        out_shape=(shape((count * 4, 4 * half), F32),) * 2,
        in_specs=vmem(8),
        out_specs=(far,) * 2,
        scratch_shapes=[pltpu.VMEM((count * 4, 4 * half), F32)] * 2
        + [pltpu.SemaphoreType.DMA((2, half // LANES))],
        compiler_params=params(),
        name="update",
    )(base, once, twice, base_rim, once_rim, twice_rim, spreading, sums)
    return solution, residual


def solution(mesh):
    return jax.shard_map(
        per_device,
        mesh=mesh,
        in_specs=(
            P("frame", ("scene", "tile"), None),
            P("scene", "frame"),
            P("scene", "frame"),
            P("scene", "frame"),
            P(),
            P(),
        ),
        out_specs=(P(("scene", "tile"), "frame"), P(("scene", "tile"), "frame")),
        check_vma=False,
    )
```

```python
import functools

import jax
import jax.numpy as jnp
from jax import lax
from jax.experimental import pallas as pl
from jax.experimental.pallas import tpu as pltpu
from jax.sharding import PartitionSpec as P

DAMPING = 0.3
LANES = 128
HIGHEST = lax.Precision.HIGHEST
NT = (((1,), (1,)), ((), ()))
F32, BF16, I32 = jnp.float32, jnp.bfloat16, jnp.int32


def split(x):
    high = x.astype(BF16)
    return high, (x - high.astype(F32)).astype(BF16)


def paired(table):
    return jnp.concatenate(split(table), axis=0)


def row_phase(shape):
    return lax.broadcasted_iota(I32, shape, 0) & 3


def tap_table(shift, ids, members, kernels, gains):
    frames = shift.shape[1]
    copies = LANES // frames

    def tiled(x):
        return jnp.concatenate([x] * copies, axis=1)

    shape = (32, LANES)
    place = lax.broadcasted_iota(I32, shape, 0)
    lane = lax.broadcasted_iota(I32, shape, 1)
    group = place >> 3
    first = jnp.where(group == 0, 2, jnp.where(group == 1, 4, jnp.where(group == 2, 0, 6)))
    col = first + ((place >> 2) & 1)
    row = 2 + 4 * ((lane >> 5) - 1) + (place & 3)
    up = row - tiled(shift[0:1, :])
    along = col - tiled(shift[1:2, :])
    kind = tiled(ids[...])
    member = tiled(members[...])
    inside = (row >= 0) & (row < 8) & (up >= 0) & (up < 5) & (along >= 0) & (along < 5)
    count = kernels.shape[1]
    code = jnp.where(inside, kind * 25 + up * 5 + along, -1)
    total = jnp.zeros(shape, F32)
    for n in range(count):
        for a in range(5):
            for b in range(5):
                total = jnp.where(code == n * 25 + a * 5 + b, kernels[a, n, b], total)
    scale = jnp.zeros((1, LANES), F32)
    for g in range(gains.shape[0]):
        scale = jnp.where(member == g, gains[g], scale)
    return total * scale


def put_halves(own, send, at, value, me):
    half = value.shape[1] // 2
    near = lax.broadcasted_iota(I32, (8, LANES), 1) < 64
    own[at : at + 8, :half] = value[:, :half]
    send[at : at + 8, :half] = value[:, half:]
    after = jnp.where(near, value[:, half : half + LANES], 0.0)
    before = jnp.where(near, 0.0, value[:, 2 * half - LANES :])
    own[at : at + 8, half:] = jnp.where(me == 0, after, before)
    before = jnp.where(near, 0.0, value[:, half - LANES : half])
    after = jnp.where(near, value[:, 0:LANES], 0.0)
    send[at : at + 8, half:] = jnp.where(me == 0, before, after)


def moved_image(t, me):
    wide = t.shape[1]
    half = wide // 2
    lane = lax.broadcasted_iota(I32, (8, wide), 1)
    low = t[0:8] + jnp.where(lane == jnp.where(me == 0, 0, half), 0.0, pltpu.roll(t[24:32], 1, 1))
    last = jnp.where(me == 0, wide - 1, half - 1)
    high = t[8:16] + jnp.where(lane == last, 0.0, pltpu.roll(t[16:24], wide - 1, 1))
    return low, high


def two_rows(weights, columns):
    both = jnp.dot(weights, columns, preferred_element_type=F32)
    return both[0:32] + both[32:64], both[64:96] + both[96:128]


def one_row(weights, columns):
    both = jnp.dot(weights[0:64, 0:192], columns, preferred_element_type=F32)
    return both[0:32] + both[32:64]


def keep(stack, at, cols, high, low):
    stack[at * 64 : at * 64 + 32, cols] = high
    stack[at * 64 + 32 : at * 64 + 64, cols] = low


def adjoint_weights(table):
    source = lax.broadcasted_iota(I32, (LANES, 512), 0)
    target = lax.broadcasted_iota(I32, (LANES, 512), 1)
    place = (target & 255) - 64 * (target >> 8)
    pick = (source == (2 - (place >> 6)) * 32 + (place & 31)) & (place >= 0) & (place < 192)
    both = jnp.dot(table, pick.astype(F32), precision=HIGHEST, preferred_element_type=F32)
    return jnp.concatenate([paired(both[:, 0:256]), paired(both[:, 256:512])], axis=0)


def outer_kernel(
    far_shift, far_ids, far_members, far_kernels, far_gains, obs, mine, theirs, own, send, weights,
    top, bottom, mixed, sems, shift, ids, members, kernels, gains, small_sems,
):
    wide = obs.shape[1]
    frames = shift.shape[1]
    count = obs.shape[0] // frames
    blocks = wide // LANES
    me = lax.axis_index("frame")

    half = wide // 2

    def load(c):
        start = jnp.where(me == 0, 0, half) if c < blocks // 2 else jnp.where(me == 0, half, 0)
        start = start + (c % (blocks // 2)) * LANES
        target = mine if c < blocks // 2 else theirs
        at = c % (blocks // 2)
        source = obs.at[:, pl.ds(pl.multiple_of(start, LANES), LANES)]
        return pltpu.make_async_copy(source, target.at[at], sems.at[c])

    def halo(from_theirs):
        last = blocks // 2 - 1
        source, target = (theirs, mine) if from_theirs else (mine, theirs)
        at = jnp.where(me == 0, 0, last) if from_theirs else jnp.where(me == 0, last, 0)
        return pltpu.make_async_copy(
            source.at[at], target.at[blocks // 2], sems.at[blocks + 1 if from_theirs else blocks]
        )

    ahead = min(10, blocks)
    small = [
        pltpu.make_async_copy(far, near, small_sems.at[i])
        for i, (far, near) in enumerate(
            [(far_kernels, kernels), (far_gains, gains), (far_shift, shift), (far_ids, ids), (far_members, members)]
        )
    ]
    for copy in small:
        copy.start()
    for c in range(ahead):
        load(c).start()
    for copy in small:
        copy.wait()
    table = tap_table(shift, ids, members, kernels, gains)
    for r in range(4):
        own[80:88, r * LANES : (r + 1) * LANES] = table[8 * r : 8 * r + 8]
        send[80:88, r * LANES : (r + 1) * LANES] = table[8 * r : 8 * r + 8]
    rest = own.shape[1] - 4 * LANES
    if rest > 0:
        own[80:88, 4 * LANES :] = jnp.zeros((8, rest), F32)
        send[80:88, 4 * LANES :] = jnp.zeros((8, rest), F32)
    left = adjoint_weights(table)
    weights[...] = left

    cuts = [0, blocks // 2, 3 * blocks // 4, blocks]
    for c, end in zip(cuts, cuts[1:]):
        step = end - c
        for d in range(step):
            load(c + d).wait()
            if c + d + ahead < blocks:
                load(c + d + ahead).start()
            cols = slice((c + d) * LANES, (c + d + 1) * LANES)
            landed, at = (mine, c + d) if c + d < blocks // 2 else (theirs, c + d - blocks // 2)
            for r in range(3):
                keep(top, r, cols, *split(landed[at, pl.ds(r, frames, stride=count), :]))
                keep(bottom, r, cols, *split(landed[at, pl.ds(count - 3 + r, frames, stride=count), :]))
        if end == blocks:
            halo(False).start()
            halo(True).start()
        cols = slice(c * LANES, (c + step) * LANES)
        a, b = two_rows(left[:, 128:256], top[0:128, cols])
        mixed[0:32, cols] = a
        mixed[32:64, cols] = b
        mixed[64:96, cols] = one_row(left, top[:, cols])
        mixed[96:128, cols] = one_row(left, bottom[:, cols])
        a, b = two_rows(left[:, 0:128], bottom[64:192, cols])
        mixed[128:160, cols] = a
        mixed[160:192, cols] = b

    above, below = moved_image(mixed[0:32, :], me), moved_image(mixed[160:192, :], me)
    for g in range(2):
        put_halves(own, send, 8 * g, above[g] + below[g], me)
    for r in range(1, 5):
        image = moved_image(mixed[r * 32 : r * 32 + 32, :], me)
        for g in range(2):
            put_halves(own, send, r * 16 + 8 * g, image[g], me)
    halo(False).wait()
    halo(True).wait()


def inner_sums(landed, left, stack, mixed):
    blocks = landed.shape[0]
    rows = mixed.shape[0] // 32
    count = rows + 4
    frames = landed.shape[1] // count
    for c in range(0, blocks, 2):
        pair = min(2, blocks - c)
        for d in range(pair):
            cols = slice((c + d) * LANES, (c + d + 1) * LANES)
            for r in range(rows + 2):
                keep(stack, r, cols, *split(landed[c + d, pl.ds(1 + r, frames, stride=count), :]))
        cols = slice(c * LANES, (c + pair) * LANES)
        for r in range(0, rows, 2):
            a, b = two_rows(left, stack[r * 64 : r * 64 + 256, cols])
            mixed[r * 32 : r * 32 + 32, cols] = a
            mixed[r * 32 + 32 : r * 32 + 64, cols] = b


def early_kernel(landed, weights, mixed, stack):
    inner_sums(landed, weights[...], stack, mixed)


def border_kernel(own, other, passed, made, first, second, onward):
    even = lax.rem(lax.axis_index("tile"), 2) == 0
    edge = own[0:16] + other[0:16]
    phase = row_phase((8, own.shape[1]))
    above = jnp.where(phase >= 2, edge[0:8], pltpu.roll(edge[8:16], 6, 0))
    below = jnp.where(phase < 2, edge[0:8], pltpu.roll(edge[8:16], 2, 0))
    top = own[16:48] + other[16:48]
    bottom = own[48:80] + other[48:80]
    here = lax.axis_index("frame")
    half = own.shape[1] - LANES
    kind = lax.broadcasted_iota(I32, (8, LANES), 1) >> 3

    def pack(ref, rows, last):
        tail = jnp.zeros((8, LANES), F32)
        for g in range(5):
            value = last if g == 4 else rows[8 * g : 8 * g + 8]
            for c in range(half // LANES):
                ref[g * (half // LANES) + c] = value[:, c * LANES : (c + 1) * LANES]
            spare = value[:, half:] if g == 0 else pltpu.roll(value[:, half:], 8 * g, 1)
            tail = jnp.where(kind == jnp.where(here == 0, g, (15 + g) % 16), spare, tail)
        ref[5 * (half // LANES)] = tail

    pack(first, jnp.where(even, bottom, top), jnp.where(even, below, above))
    pack(second, jnp.where(even, top, bottom), jnp.where(even, above, below))


def unpacked(tiles):
    per = tiles.shape[0] // 5
    kind = lax.broadcasted_iota(I32, (8, LANES), 1) >> 3
    mine = kind == jnp.where(lax.axis_index("frame") == 0, 0, 15)
    groups = []
    for g in range(5):
        tail = tiles[5 * per] if g == 0 else pltpu.roll(tiles[5 * per], LANES - 8 * g, 1)
        groups.append(
            jnp.concatenate([tiles[g * per + c] for c in range(per)] + [jnp.where(mine, tail, 0.0)], axis=1)
        )
    return jnp.concatenate(groups, axis=0)


def halo_mask():
    lane = lax.broadcasted_iota(I32, (8, LANES), 1)
    here = lax.axis_index("frame") == 0
    return jnp.where(here, jnp.where(lane < 64, 1.0, 0.0), jnp.where(lane < 64, 0.0, 1.0)).astype(F32)


def expand(stack, at, value):
    ext = value.shape[1]
    low, high = value[0:8], value[8:16]
    groups = jnp.concatenate([low, high, pltpu.roll(high, 1, 1), pltpu.roll(low, ext - 1, 1)], axis=0)
    keep(stack, at, slice(None), *split(groups))


def assembled(t, near, field=None):
    ext = t.shape[1]
    half = ext - LANES

    def masked(x):
        return jnp.concatenate([x[:, :half], x[:, half:] * near], axis=1)

    low = t[0:8] + pltpu.roll(masked(t[24:32]), 1, 1)
    high = t[8:16] + pltpu.roll(masked(t[16:24]), ext - 1, 1)
    if field is not None:
        low, high = low + DAMPING * field[0:8], high + DAMPING * field[8:16]
    return jnp.concatenate([masked(low), masked(high)], axis=0)


def finished(t, field, near):
    return assembled(t, near, field)


def folded(a, b):
    total = None
    for c in range(0, a.shape[1] - LANES + 1, LANES):
        for g in (0, 8):
            term = a[g : g + 8, c : c + LANES] * b[g : g + 8, c : c + LANES]
            total = term if total is None else total + term
    return total


def interior_kernel(
    own1, other1, ours, landed, base, once, twice, stack1, stack2, tables, spread, sums, stack, mixed
):
    ext = own1.shape[1]
    half = ext - LANES
    inner = ours.shape[0] // 32
    tile, tiles = lax.axis_index("tile"), lax.axis_size("tile")
    no_up = jnp.where(tile > 0, 0.0, 1.0).astype(F32)
    no_down = jnp.where(tile < tiles - 1, 0.0, 1.0).astype(F32)

    taps = [
        jnp.concatenate([ref[80:88, r * LANES : (r + 1) * LANES] for r in range(4)], axis=0) for ref in (own1, other1)
    ]
    inner_sums(landed, adjoint_weights(taps[1]), stack, mixed)
    block = lax.broadcasted_iota(I32, (32, LANES), 1) >> 5
    left = jnp.concatenate(
        [jnp.concatenate([t, jnp.where(block == 2, t, 0.0), jnp.where(block == 0, t, 0.0)], axis=0) for t in taps],
        axis=1,
    )
    empty = jnp.zeros((64, LANES), F32)
    right = []
    for t in taps:
        e, a = pltpu.roll(t, 32, 1), pltpu.roll(t, LANES - 32, 1)
        right.append(jnp.concatenate([e, e, t, t, a, a, empty, empty, e, e, t, t, a, a], axis=0))
    product = lax.dot_general(
        left, jnp.concatenate(right, axis=1), NT, precision=HIGHEST, preferred_element_type=F32
    )
    lane = lax.broadcasted_iota(I32, (32, 512), 1)
    middle = ((lane >> 6) == 1) | ((lane >> 6) == 6)
    full = product[0:32]
    at_top = full - no_up * jnp.where(middle, product[32:64], 0.0)
    at_bottom = full - no_down * jnp.where(middle, product[64:96], 0.0)
    plain_a, plain_b = paired(full[:, 0:256]), paired(full[:, 256:512])
    top_a, top_b = paired(at_top[:, 0:256]), paired(at_top[:, 256:512])
    bottom_a, bottom_b = paired(at_bottom[:, 0:256]), paired(at_bottom[:, 256:512])
    pairs = [(plain_a, plain_b), (plain_a, top_b), (top_a, plain_b), (plain_a, bottom_b), (bottom_a, plain_b)]
    for i, (a, b) in enumerate(pairs):
        tables[i * 128 : i * 128 + 64] = a
        tables[i * 128 + 64 : i * 128 + 128] = b
    plain = jnp.concatenate([plain_a, plain_b], axis=0)

    source = lax.broadcasted_iota(I32, spread.shape, 0)
    target = lax.broadcasted_iota(I32, spread.shape, 1)
    hit = target == 4 * (source & (LANES - 1)) + (source >> 7)
    spread[...] = jnp.where(hit, 1.0, 0.0).astype(BF16)
    near = halo_mask()
    totals = [jnp.zeros((8, LANES), F32) for _ in range(4)]

    for r in range(inner + 2):
        if r == 0:
            value = own1[32:48] + other1[32:48]
        elif r == inner + 1:
            value = own1[48:64] + other1[48:64]
        else:
            at = (r - 1) * 32
            value = assembled(ours[at : at + 32] + mixed[at : at + 32], near)
        base[r * 16 : r * 16 + 16] = value
        totals[0] += folded(value[:, :half], value[:, :half])
        expand(stack1, r, value)
    for r in range(0, inner, 2):
        images = two_rows(plain, stack1[r * 64 : r * 64 + 256])
        for d in range(2):
            field = base[(r + d + 1) * 16 : (r + d + 2) * 16]
            value = finished(images[d], field, near)
            once[(r + d) * 16 : (r + d + 1) * 16] = value
            totals[1] += folded(field[:, :half], value[:, :half])
            totals[2] += folded(value[:, :half], value[:, :half])
            expand(stack2, r + d, value)
    for r in range(0, inner - 2, 2):
        images = two_rows(plain, stack2[r * 64 : r * 64 + 256])
        for d in range(2):
            field = once[(r + d + 1) * 16 : (r + d + 2) * 16]
            value = finished(images[d], field, near)[:, :half]
            twice[(r + d) * 16 : (r + d + 1) * 16] = value
            totals[3] += folded(field[:, :half], value)
    for i in range(4):
        sums[i * 8 : i * 8 + 8] = totals[i]


def rim_kernel(
    own, other, first, second, base, once, stack1, stack2, tables, partial,
    base_rim, once_rim, twice_rim, sums, above1, below1, above2, below2,
):
    ext = own.shape[1]
    half = ext - LANES
    inner = base.shape[0] // 16
    tile, tiles = lax.axis_index("tile"), lax.axis_size("tile")
    even = lax.rem(tile, 2) == 0
    has_up = jnp.where(tile > 0, 1.0, 0.0).astype(F32)
    has_down = jnp.where(tile < tiles - 1, 1.0, 0.0).astype(F32)
    near = halo_mask()
    phase = row_phase((16, ext))
    totals = [partial[i * 8 : i * 8 + 8] for i in range(4)]
    plain = tables[0:128]

    above1[192:320] = stack1[0:128]
    below1[0:128] = stack1[(inner - 2) * 64 : inner * 64]
    above2[192:320] = stack2[0:128]
    below2[0:128] = stack2[(inner - 4) * 64 : (inner - 2) * 64]

    edge = own[0:16] + other[0:16]
    up = unpacked(jnp.where(even, second[...], first[...]))
    down = unpacked(jnp.where(even, first[...], second[...]))
    rows = {-2: up[0:16]}
    rows[-1] = up[16:32] + has_up * jnp.where(phase >= 2, edge, 0.0)
    e = up[32:40]
    spare = jnp.where(phase < 2, jnp.concatenate([e, pltpu.roll(e, 6, 0)], axis=0), 0.0)
    rows[0] = own[16:32] + other[16:32] + spare
    rows[1] = base[0:16]
    e = down[32:40]
    spare = jnp.where(phase >= 2, jnp.concatenate([e, pltpu.roll(e, 2, 0)], axis=0), 0.0)
    low_rows = {0: base[(inner - 1) * 16 : inner * 16]}
    low_rows[1] = own[64:80] + other[64:80] + spare
    low_rows[2] = down[0:16] + has_down * jnp.where(phase < 2, edge, 0.0)
    low_rows[3] = down[16:32]
    for i in range(3):
        expand(above1, i, rows[i - 2])
        expand(below1, i + 2, low_rows[i + 1])
    base_rim[0:16] = rows[0][:, :half]
    base_rim[16:32] = low_rows[1][:, :half]
    totals[0] += folded(rows[0][:, :half], rows[0][:, :half])
    totals[0] += folded(low_rows[1][:, :half], low_rows[1][:, :half])

    a, b = two_rows(tables[128:256], above1[0:256])
    c = one_row(plain, above1[128:320])
    high = [finished(a, rows[-1], near) * has_up, finished(b, rows[0], near), finished(c, rows[1], near)]
    a = one_row(plain, below1[0:192])
    b, c = two_rows(tables[512:640], below1[64:320])
    deep = [
        finished(a, low_rows[0], near),
        finished(b, low_rows[1], near),
        finished(c, low_rows[2], near) * has_down,
    ]
    for i in range(3):
        expand(above2, i, high[i])
        expand(below2, i + 2, deep[i])
    pieces = [(rows[0], high[1]), (rows[1], high[2]), (low_rows[0], deep[0]), (low_rows[1], deep[1])]
    for i, (field, value) in enumerate(pieces):
        once_rim[i * 16 : i * 16 + 16] = value[:, :half]
        totals[1] += folded(field[:, :half], value[:, :half])
        totals[2] += folded(value[:, :half], value[:, :half])

    a, b = two_rows(tables[256:384], above2[0:256])
    c = one_row(plain, above2[128:320])
    d = one_row(plain, below2[0:192])
    e, f = two_rows(tables[384:512], below2[64:320])
    fields = [high[1], high[2], once[0:16], once[(inner - 3) * 16 : (inner - 2) * 16], deep[0], deep[1]]
    for i, (t, field) in enumerate(zip([a, b, c, d, e, f], fields)):
        value = finished(t, field, near)[:, :half]
        twice_rim[i * 16 : i * 16 + 16] = value
        totals[3] += folded(field[:, :half], value)
    lane = lax.broadcasted_iota(I32, (1, LANES), 1) >> 5
    line = jnp.zeros((1, LANES), F32)
    for i, t in enumerate(totals):
        part = jnp.sum(t, axis=0, keepdims=True)
        part = part + pltpu.roll(part, 64, 1)
        part = part + pltpu.roll(part, 32, 1)
        line = jnp.where(lane == i, part, line)
    sums[...] = jnp.broadcast_to(line, sums.shape)


def update_kernel(base, once, twice, base_rim, once_rim, twice_rim, spread, sums, solution, residual, near_x, near_r, sems):
    lanes = jnp.sum(sums[...], axis=0, keepdims=True)
    kind = lax.broadcasted_iota(I32, lanes.shape, 1) >> 5

    def total(at):
        return jnp.sum(jnp.where(kind == at, lanes, 0.0), axis=1, keepdims=True)

    bb, bm, mm, mmm = [total(at) for at in range(4)]
    alpha = bb / bm
    norm = alpha * alpha * mm - 2.0 * alpha * bm + bb
    beta = norm / bb
    grow = 1.0 + beta
    product = grow * grow * bm - 2.0 * grow * alpha * mm + alpha * alpha * mmm
    step = norm / product
    count = base.shape[0] // 16 + 2
    half = base_rim.shape[1]
    side = lax.broadcasted_iota(I32, (count // 2, 8, LANES), 1) < 4

    def arranged(x):
        x = x.reshape(count // 2, 4, 8, LANES)
        pieces = []
        for g in range(2):
            a, b = x[:, g], x[:, g + 2]
            pieces.append(jnp.where(side, a, pltpu.roll(b, 4, 1)).reshape(4 * count, LANES))
            pieces.append(jnp.where(side, pltpu.roll(a, 4, 1), b).reshape(4 * count, LANES))
        return split(jnp.concatenate(pieces, axis=1))

    def stores(c):
        wide = pl.ds(4 * c * LANES, 4 * LANES)
        return [
            pltpu.make_async_copy(near.at[:, wide], far.at[:, wide], sems.at[i, c])
            for i, (near, far) in enumerate([(near_x, solution), (near_r, residual)])
        ]

    def rows_of(middle, rim, cols):
        n = rim.shape[0] // 2
        return jnp.concatenate([rim[0:n, cols], middle[:, cols], rim[n : 2 * n, cols]], axis=0)

    for c in range(half // LANES):
        cols = slice(c * LANES, (c + 1) * LANES)
        b, m, mm_ = rows_of(base, base_rim, cols), rows_of(once, once_rim, cols), rows_of(twice, twice_rim, cols)
        x = (alpha + step * grow) * b - (step * alpha) * m
        r = (b - alpha * m) - step * (grow * m - alpha * mm_)
        xh, xl = arranged(x)
        rh, rl = arranged(r)
        out = jnp.dot(jnp.concatenate([xh, xl, rh, rl], axis=0), spread[...], preferred_element_type=F32)
        n = 4 * count
        wide = slice(4 * c * LANES, 4 * (c + 1) * LANES)
        near_x[:, wide] = out[0:n] + out[n : 2 * n]
        near_r[:, wide] = out[2 * n : 3 * n] + out[3 * n : 4 * n]
        for copy in stores(c):
            copy.start()
    for c in range(half // LANES):
        for copy in stores(c):
            copy.wait()


def params(mebibytes=24):
    return pltpu.CompilerParams(vmem_limit_bytes=mebibytes * 1024 * 1024)


def cost(units):
    return pl.CostEstimate(flops=int(units * 10**9), bytes_accessed=int(units * 2**22), transcendentals=0)


def vmem(n):
    return [pl.BlockSpec(memory_space=pltpu.VMEM)] * n


def per_device(observed, frame_shift, kernel_ids, groups, kernels, gains):
    frames, count, wide = observed.shape
    half = wide // 2
    ext = half + LANES
    blocks = wide // LANES
    tiles, spread = lax.axis_size("tile"), lax.axis_size("frame")
    far = pl.BlockSpec(memory_space=pltpu.HBM)
    shape = jax.ShapeDtypeStruct
    inner = count - 4

    mine, theirs, own, send, weights = pl.pallas_call(
        outer_kernel,
        out_shape=(
            shape((blocks // 2 + 1, frames * count, LANES), F32),
            shape((blocks // 2 + 1, frames * count, LANES), F32),
            shape((88, ext), F32),
            shape((88, ext), F32),
            shape((128, 256), BF16),
        ),
        in_specs=[far] * 6,
        out_specs=tuple(vmem(5)),
        scratch_shapes=[
            pltpu.VMEM((192, wide), BF16),
            pltpu.VMEM((192, wide), BF16),
            pltpu.VMEM((192, wide), F32),
            pltpu.SemaphoreType.DMA((blocks + 2,)),
            pltpu.VMEM(frame_shift.shape, I32),
            pltpu.VMEM(kernel_ids.shape, I32),
            pltpu.VMEM(groups.shape, I32),
            pltpu.SMEM((5, kernels.shape[0], 5), F32),
            pltpu.SMEM(gains.shape, F32),
            pltpu.SemaphoreType.DMA((5,)),
        ],
        compiler_params=params(),
        name="outer",
    )(
        *(
            pltpu.with_memory_space_constraint(x, pltpu.HBM)
            for x in (frame_shift, kernel_ids, groups, kernels.transpose(1, 0, 2), gains, observed.reshape(-1, wide))
        )
    )
    other = lax.ppermute(send, "frame", [(0, 1), (1, 0)])

    ours = pl.pallas_call(
        early_kernel,
        out_shape=shape((inner * 32, ext), F32),
        in_specs=vmem(2),
        out_specs=vmem(1)[0],
        scratch_shapes=[pltpu.VMEM(((inner + 2) * 64, ext), BF16)],
        compiler_params=params(),
        cost_estimate=cost(1),
        name="early",
    )(mine, weights)
    halo = (5 * half // LANES + 1, 8, LANES)
    first, second, theirs = pl.pallas_call(
        border_kernel,
        out_shape=(shape(halo, F32), shape(halo, F32), shape(theirs.shape, F32)),
        in_specs=vmem(2) + [pl.BlockSpec(memory_space=pl.ANY)] * 2,
        out_specs=tuple(vmem(2)) + (pl.BlockSpec(memory_space=pl.ANY),),
        input_output_aliases={2: 2},
        compiler_params=params(),
        name="border",
    )(own, other, theirs, ours)
    theirs = lax.ppermute(theirs, "frame", [(0, 1), (1, 0)])
    pairs = [(i, i ^ 1) for i in range(tiles) if i ^ 1 < tiles]
    odd_pairs = [p for i in range(1, tiles - 1, 2) for p in ((i, i + 1), (i + 1, i))]
    second = lax.ppermute(second, "tile", odd_pairs)
    first = lax.ppermute(first, "tile", pairs)

    base, once, twice, stack1, stack2, tables, spreading, partial = pl.pallas_call(
        interior_kernel,
        out_shape=(
            shape(((inner + 2) * 16, ext), F32),
            shape((inner * 16, ext), F32),
            shape(((inner - 2) * 16, half), F32),
            shape(((inner + 2) * 64, ext), BF16),
            shape((inner * 64, ext), BF16),
            shape((5 * 128, 256), BF16),
            shape((4 * LANES, 4 * LANES), BF16),
            shape((32, LANES), F32),
        ),
        in_specs=vmem(4),
        out_specs=tuple(vmem(8)),
        scratch_shapes=[pltpu.VMEM(((inner + 2) * 64, ext), BF16), pltpu.VMEM((inner * 32, ext), F32)],
        compiler_params=params(),
        cost_estimate=cost(0.01),
        name="interior",
    )(own, other, ours, theirs)
    peers = tiles * spread
    base_rim, once_rim, twice_rim, sums = pl.pallas_call(
        rim_kernel,
        out_shape=(
            shape((32, half), F32),
            shape((64, half), F32),
            shape((96, half), F32),
            shape((peers, LANES), F32),
        ),
        in_specs=vmem(10),
        out_specs=tuple(vmem(4)),
        scratch_shapes=[pltpu.VMEM((320, ext), BF16)] * 4,
        compiler_params=params(),
        name="rim",
    )(own, other, first, second, base, once, stack1, stack2, tables, partial)
    sums = lax.all_to_all(sums, ("tile", "frame"), 0, 0)

    solution, residual = pl.pallas_call(
        update_kernel,
        out_shape=(shape((count * 4, 4 * half), F32),) * 2,
        in_specs=vmem(8),
        out_specs=(far,) * 2,
        scratch_shapes=[pltpu.VMEM((count * 4, 4 * half), F32)] * 2
        + [pltpu.SemaphoreType.DMA((2, half // LANES))],
        compiler_params=params(),
        name="update",
    )(base, once, twice, base_rim, once_rim, twice_rim, spreading, sums)
    return solution, residual


def solution(mesh):
    return jax.shard_map(
        per_device,
        mesh=mesh,
        in_specs=(
            P("frame", ("scene", "tile"), None),
            P("scene", "frame"),
            P("scene", "frame"),
            P("scene", "frame"),
            P(),
            P(),
        ),
        out_specs=(P(("scene", "tile"), "frame"), P(("scene", "tile"), "frame")),
        check_vma=False,
    )
```
